32 devices in a mesh: seq: 4 (over y, core), batch: 8 (over z, x).
Axes of the slice: x: 2, y: 2, z: 4, core: 2. Of those that a mesh axis runs over, the one named last changes fastest.
Arguments:
- block_input: bfloat16 [8, 1024, 1024], P('batch', 'seq'), may hold values from -6 to 6
- segment_ids: int32 [8, 1024], P('batch', 'seq'), may hold values from 0 to 2, never falling along the last dimension, each value on 1 to 512 neighbouring positions
- out_cotangent: bfloat16 [8, 1024, 1024], P('batch', 'seq'), may hold values from -6 to 6
- lower_bound: float32 [1024], replicated, as said below
- gain_first: bfloat16 [1024], P(('seq', 'batch')), may hold values from 0.099609375 to 1.8984375
- w_input: bfloat16 [1024, 2048], P('batch', 'seq'), may hold values from -0.1875 to 0.1875
- w_forget: bfloat16 [1024, 1024], P('batch', 'seq'), may hold values from -0.1875 to 0.1875
- w_outgate: bfloat16 [1024, 2048], P('batch', 'seq'), may hold values from -0.1875 to 0.1875
- phase_angle: bfloat16 [1024], P(('seq', 'batch')), may hold values from -3.140625 to 3.140625
- gain_mixer: bfloat16 [2048], P(('seq', 'batch')), may hold values from 0.099609375 to 1.8984375
- w_output: bfloat16 [2048, 1024], P('batch', 'seq'), may hold values from -0.125 to 0.125
- gain_second: bfloat16 [1024], P(('seq', 'batch')), may hold values from 0.099609375 to 1.8984375
- w_gate: bfloat16 [1024, 2816], P('batch', 'seq'), may hold values from -0.1875 to 0.1875
- w_up: bfloat16 [1024, 2816], P('batch', 'seq'), may hold values from -0.1875 to 0.1875
- w_down: bfloat16 [2816, 1024], P('seq', 'batch'), may hold values from -0.109375 to 0.109375
Outputs:
- block_output: bfloat16 [8, 1024, 1024], P('batch', 'seq')
- grad_input: bfloat16 [8, 1024, 1024], P('batch', 'seq')
- grad_gain_first: float32 [1024], P(('seq', 'batch'))
- grad_w_input: float32 [1024, 2048], P('batch', 'seq')
- grad_w_forget: float32 [1024, 1024], P('batch', 'seq')
- grad_w_outgate: float32 [1024, 2048], P('batch', 'seq')
- grad_phase_angle: float32 [1024], P(('seq', 'batch'))
- grad_gain_mixer: float32 [2048], P(('seq', 'batch'))
- grad_w_output: float32 [2048, 1024], P('batch', 'seq')
- grad_gain_second: float32 [1024], P(('seq', 'batch'))
- grad_w_gate: float32 [1024, 2816], P('batch', 'seq')
- grad_w_up: float32 [1024, 2816], P('batch', 'seq')
- grad_w_down: float32 [2816, 1024], P('seq', 'batch')
The draws below stay inside these ranges and needn't reach their ends.
Inputs may be any that keep to these rules, and one draw needn't show every extreme that they name: `segment_ids`: within a row the ids never fall; a token whose id differs from its predecessor's starts a new document and the recurrence restarts there. `lower_bound`: every entry lies in [0.85, 1).
All inputs are finite; a program needn't handle non-finite values.
Results may differ from the reference program's by a relative error of at most 0.014.
Values may be sent and summed in bfloat16 or wider, within the bound.
No kernel may reach another device: no remote copies, remote signals or barrier semaphores. Data moves between devices by JAX's collectives and lax.ppermute only.
A program may use at most 256 MiB of HBM per device.

```python
import math
import jax
import jax.numpy as jnp
import numpy as np
from jax import lax

D = 1024
FF = 2816
DOCS = 3
L = 1024
ROWS = 8


def draw_lower_bound(key, part):
    spread = jax.random.uniform(key, (D,), jnp.float32)
    bottom = math.log(0.5 / L)
    top = math.log(0.15)
    return 1.0 - jnp.exp(bottom + (top - bottom) * spread)


def levels(rng, shape, split, least, high):
    loudness = 1.0
    for position, parts in split:
        heights = jax.random.uniform(jax.random.fold_in(jax.random.fold_in(rng, 6), position), (parts,), jnp.float32, least / len(split), high / len(split))
        loudness = loudness * jnp.repeat(jnp.exp(heights), shape[position] // parts).reshape((-1,) + (1,) * (len(shape) - 1 - position))
    return loudness


def length_profile(number_of, total, most, lean):
    portions = [(1 << 20) // math.isqrt(rank ** lean) + 1 for rank in range(2, number_of + 1)]
    spare, holding = total - most - (number_of - 1), [1] * (number_of - 1)
    while spare > 0:
        free = [i for i in range(number_of - 1) if holding[i] < most]
        pool, left = sum([portions[i] for i in free]), spare
        for i in free:
            extra = min(most - holding[i], max(1, left * portions[i] // pool), spare)
            holding[i] = holding[i] + extra
            spare = spare - extra
    return np.array([most] + holding)


def ragged(stream_key, count, total, limit, skew):
    if count == 2:
        one = jax.random.randint(stream_key, (), max(1, total - limit), min(limit, total - 1) + 1)
        return jnp.stack([one, total - one])
    tallies = jnp.asarray(length_profile(count, total, limit, skew), jnp.int32)
    pairs = (count - 1) // 2
    giver, sink = tallies[1:1 + 2 * pairs:2], tallies[2:2 + 2 * pairs:2]
    slack = jnp.minimum(giver - 1, limit - sink)
    shifted = jax.random.randint(jax.random.fold_in(stream_key, 1), (pairs,), 0, 1 << 20) % (slack + 1)
    tallies = tallies.at[1:1 + 2 * pairs:2].set(giver - shifted).at[2:2 + 2 * pairs:2].set(sink + shifted)
    return tallies[jax.random.permutation(jax.random.fold_in(stream_key, 2), count)]


def bell_draw(rng, extent, scale, most, shards=(), kind=jnp.bfloat16):
    level = levels(rng, extent, shards, -0.22, 0.18) if shards else 1.0
    entries = jax.random.normal(rng, extent, jnp.float32) * scale * level
    return jnp.minimum(jnp.maximum(entries, -most), most).astype(kind)


def setup_inputs(seed: int = 0) -> dict:
    key_of = jax.random.split(jax.random.key(seed), 16)
    return {
        "block_input": bell_draw(key_of[0], (ROWS, L, D), 1.0, 6.0, ((0, 8), (1, 4))),
        "segment_ids": jax.vmap(lambda own: jnp.searchsorted(jnp.cumsum(ragged(own, DOCS, L, L // 2, 0)), jnp.arange(L), side="right"))(jax.random.split(key_of[1], ROWS)).reshape((ROWS, L)).astype(jnp.int32),
        "out_cotangent": bell_draw(key_of[2], (ROWS, L, D), 1.0, 6.0, ((0, 8), (1, 4))),
        "lower_bound": draw_lower_bound(jax.random.fold_in(key_of[15], 71), 0),
        "gain_first": jnp.clip(1.0 + 0.18 * jax.random.normal(key_of[4], (D,), jnp.float32), 0.099609375, 1.8984375).astype(jnp.bfloat16),
        "w_input": bell_draw(key_of[5], (D, 2 * D), D ** -0.5, 0.1875, ((0, 8), (1, 4))),
        "w_forget": bell_draw(key_of[6], (D, D), D ** -0.5, 0.1875, ((0, 8), (1, 4))),
        "w_outgate": bell_draw(key_of[7], (D, 2 * D), D ** -0.5, 0.1875, ((0, 8), (1, 4))),
        "phase_angle": jnp.clip(jax.random.uniform(key_of[8], (D,), jnp.float32, -3.140625, 3.140625), -3.140625, 3.140625).astype(jnp.bfloat16),
        "gain_mixer": jnp.clip(1.0 + 0.18 * jax.random.normal(key_of[9], (2 * D,), jnp.float32), 0.099609375, 1.8984375).astype(jnp.bfloat16),
        "w_output": bell_draw(key_of[10], (2 * D, D), (2 * D) ** -0.5, 0.125, ((0, 8), (1, 4))),
        "gain_second": jnp.clip(1.0 + 0.18 * jax.random.normal(key_of[11], (D,), jnp.float32), 0.099609375, 1.8984375).astype(jnp.bfloat16),
        "w_gate": bell_draw(key_of[12], (D, FF), D ** -0.5, 0.1875, ((0, 8), (1, 4))),
        "w_up": bell_draw(key_of[13], (D, FF), D ** -0.5, 0.1875, ((0, 8), (1, 4))),
        "w_down": bell_draw(key_of[14], (FF, D), FF ** -0.5, 0.109375, ((0, 4), (1, 8))),
    }


epsilon = 1e-06
highest = lax.Precision.HIGHEST

@jax.custom_vjp
def low(v):
    return lax.optimization_barrier(v.astype(jnp.bfloat16)).astype(jnp.float32)

@jax.custom_vjp
def low_back(v):
    return v

def low_keep(v):
    return (low(v), None)

def low_pass(kept, grad):
    return (grad,)

def back_keep(v):
    return (v, None)

def back_low(kept, grad):
    return (low(grad),)
low.defvjp(low_keep, low_pass)
low_back.defvjp(back_keep, back_low)

def complex_mul(left_re, left_im, right_re, right_im):
    return (left_re * right_re - left_im * right_im, left_re * right_im + left_im * right_re)

def linear_combine(earlier, latter):
    mult_re, mult_im = complex_mul(earlier[0], earlier[1], latter[0], latter[1])
    moved_re, moved_im = complex_mul(latter[0], latter[1], earlier[2], earlier[3])
    return (mult_re, mult_im, moved_re + latter[2], moved_im + latter[3])

def rms_scale(values):
    return lax.rsqrt(lax.optimization_barrier(jnp.mean(values * values, axis=-1, keepdims=True)) + epsilon)

def matmul(left_side, right_side):
    return jnp.dot(left_side, right_side, precision=highest, preferred_element_type=jnp.float32)

def row_forward(tokens, keep_mask, lower_bound, params):
    gain_first, w_input, w_forget, w_outgate, phase_angle, gain_mixer, w_output, gain_second, w_gate, w_up, w_down = params
    model_width = tokens.shape[1]
    first_norm = tokens * rms_scale(tokens)
    normed_in = low(first_norm * gain_first)
    input_pre = low_back(matmul(normed_in, w_input))
    forget_pre = low_back(matmul(normed_in, w_forget))
    gate_pre = low_back(matmul(normed_in, w_outgate))
    decay_rate = lower_bound + (1.0 - lower_bound) * jax.nn.sigmoid(forget_pre)
    source_re = jax.nn.silu(input_pre[:, :model_width]) * (1.0 - decay_rate)
    source_im = jax.nn.silu(input_pre[:, model_width:]) * (1.0 - decay_rate)
    mult_re = keep_mask * decay_rate * jnp.cos(phase_angle)
    mult_im = keep_mask * decay_rate * jnp.sin(phase_angle)
    states = lax.associative_scan(linear_combine, (mult_re, mult_im, source_re, source_im), axis=0)
    hidden_state = jnp.concatenate([states[2], states[3]], axis=1)
    gated_state = hidden_state * jax.nn.sigmoid(gate_pre)
    mixed_norm = gated_state * rms_scale(gated_state)
    mixer_act = low(mixed_norm * gain_mixer)
    resid_sum = tokens + low_back(matmul(mixer_act, w_output))
    second_norm = resid_sum * rms_scale(resid_sum)
    ffn_in = low(second_norm * gain_second)
    gate_act = low_back(matmul(ffn_in, w_gate))
    up_act = low_back(matmul(ffn_in, w_up))
    hidden = low(jax.nn.silu(gate_act) * up_act)
    return resid_sum + matmul(hidden, w_down)

def reference(block_input, segment_ids, out_cotangent, lower_bound, gain_first, w_input, w_forget, w_outgate, phase_angle, gain_mixer, w_output, gain_second, w_gate, w_up, w_down):
    params = tuple((weight.astype(jnp.float32) for weight in (gain_first, w_input, w_forget, w_outgate, phase_angle, gain_mixer, w_output, gain_second, w_gate, w_up, w_down)))
    bound_full = lower_bound.astype(jnp.float32)

    def one_row(totals, row_data):
        tokens, doc_ids, out_grad = row_data
        same_doc = (doc_ids[1:] == doc_ids[:-1]).astype(jnp.float32)
        keep_mask = jnp.concatenate([jnp.zeros((1,), jnp.float32), same_doc])[:, None]

        def forward_only(token_values, param_values):
            return row_forward(token_values, keep_mask, bound_full, param_values)
        output, pullback = jax.vjp(forward_only, tokens.astype(jnp.float32), params)
        grad_tokens, grad_params = pullback(out_grad.astype(jnp.float32))
        totals = tuple((running + update for running, update in zip(totals, grad_params)))
        return (totals, (output.astype(jnp.bfloat16), grad_tokens.astype(jnp.bfloat16)))
    zero_grads = tuple((jnp.zeros_like(weight) for weight in params))
    totals, (outputs, input_grads) = lax.scan(one_row, zero_grads, (block_input, segment_ids, out_cotangent))
    return (outputs, input_grads, totals[0], totals[1], totals[2], totals[3], totals[4], totals[5], totals[6], totals[7], totals[8], totals[9], totals[10])
```

```python
import functools
import jax
import jax.numpy as jnp
from jax import lax
from jax.experimental import pallas as pl
from jax.experimental.pallas import tpu as pltpu
from jax.sharding import PartitionSpec as P

EPS = 1e-6
F32 = jnp.float32
BF = jnp.bfloat16
MB = 1024 * 1024

CORE = [(s, s ^ 1) for s in range(4)]
YSWAP = [(s, s ^ 2) for s in range(4)]
XSWAP = [(b, b ^ 1) for b in range(8)]


def zshift(k):
    return [(2 * z + x, 2 * ((z + k) % 4) + x) for z in range(4) for x in range(2)]


def out_block_perm():
    pairs = []
    for s in range(4):
        for b in range(8):
            y, c, part = b & 1, (b >> 1) & 1, b >> 2
            ys, cs = s >> 1, s & 1
            pairs.append((s * 8 + b, (2 * y + c) * 8 + 2 * (2 * part + cs) + ys))
    return pairs


OUT_PERM = out_block_perm()
OUT_BACK = [(d, s) for s, d in OUT_PERM]
FORGET_PERM = [(2 * (d & 1) + (d >> 1), d) for d in range(4)]


def sigm(v):
    return 1.0 / (1.0 + jnp.exp(-v))


def mm(a, b):
    return jnp.dot(a, b, preferred_element_type=F32)


def mm_bt(a, b):
    return lax.dot_general(a, b, (((1,), (1,)), ((), ())), preferred_element_type=F32)


def mm_at(a, b):
    return lax.dot_general(a, b, (((0,), (0,)), ((), ())), preferred_element_type=F32)


def call(body, outs, args, scratch=(), smem=0, vmem=48, flops=0, name=None):
    specs = [pl.BlockSpec(memory_space=pltpu.SMEM)] * smem
    specs += [pl.BlockSpec(memory_space=pltpu.VMEM)] * (len(args) - smem)
    nbytes = sum(a.size * a.dtype.itemsize for a in args)
    nbytes += sum(o.size * o.dtype.itemsize for o in outs)
    return pl.pallas_call(
        body,
        out_shape=outs,
        in_specs=specs,
        out_specs=[pl.BlockSpec(memory_space=pltpu.VMEM)] * len(outs),
        scratch_shapes=list(scratch),
        compiler_params=pltpu.CompilerParams(vmem_limit_bytes=vmem * MB),
        cost_estimate=pl.CostEstimate(flops=flops, bytes_accessed=nbytes, transcendentals=0),
        name=name,
    )(*args)


def sds(shape, dtype):
    return jax.ShapeDtypeStruct(shape, dtype)


def hilo(col):
    rows = col.shape[0]
    hi = col.astype(BF)
    lo = (col - hi.astype(F32)).astype(BF)
    lane = lax.broadcasted_iota(jnp.int32, (rows, 128), 1)
    hi_b = jnp.broadcast_to(hi.astype(F32), (rows, 128))
    lo_b = jnp.broadcast_to(lo.astype(F32), (rows, 128))
    return jnp.where(lane == 0, hi_b, jnp.where(lane == 1, lo_b, 0.0)).astype(BF)


def lanesum(tile):
    return jnp.sum(tile.astype(F32), axis=1, keepdims=True)


def norm1_body(x_ref, g_ref, o_ref):
    x = x_ref[...].astype(F32)
    sc = lax.rsqrt(jnp.mean(x * x, axis=1, keepdims=True) + EPS)
    o_ref[...] = (x * sc * g_ref[...]).astype(BF)


def get_wide(ref, first, count, rows):
    return jnp.concatenate([ref[first + j, rows, :] for j in range(count)], axis=1)


def put_wide(ref, first, rows, value):
    for j in range(value.shape[1] // 128):
        ref[first + j, rows, :] = value[:, j * 128 : (j + 1) * 128]


def rot_power(cos, sin, steps):
    n = 1
    while n < steps:
        cos, sin = cos * cos - sin * sin, 2.0 * cos * sin
        n *= 2
    return cos, sin


def mixer_fwd_body(
    idx_ref, x_ref, w_ref, wo_ref, keep_ref, lb_ref, cos_ref, sin_ref, gm_ref,
    pre_ref, dk_ref, h_ref, kr_ref, u_ref, kout_ref, sout_ref,
    src_ref, gs_ref, init_ref, *, seg,
):
    s = idx_ref[0]
    tok = x_ref.shape[0]
    blk = tok // 4
    ch = lb_ref.shape[1]
    lb = lb_ref[...]
    n = tok // seg
    t = ch // 128

    def pre_step(k, carry):
        rel = pl.ds(pl.multiple_of(k * blk, blk), blk)
        ab = pl.ds(pl.multiple_of((s ^ k) * blk, blk), blk)
        p = mm(x_ref[rel, :], w_ref[...])
        pre_ref[ab, :] = p.astype(BF)
        sig = sigm(p[:, 2 * ch : 3 * ch])
        om = (1.0 - lb) * (1.0 - sig)
        put_wide(dk_ref, 0, ab, keep_ref[ab, :] * (lb + (1.0 - lb) * sig))
        a = p[:, 0:ch]
        b = p[:, ch : 2 * ch]
        put_wide(src_ref, 0, ab, a * sigm(a) * om)
        put_wide(src_ref, t, ab, b * sigm(b) * om)
        gs_ref[ab, :] = sigm(p[:, 3 * ch : 5 * ch])
        return carry

    lax.fori_loop(0, 4, pre_step, 0)

    cos = jnp.broadcast_to(cos_ref[...], (seg, ch))
    sin = jnp.broadcast_to(sin_ref[...], (seg, ch))
    zero = jnp.zeros((seg, ch), F32)

    def load(i):
        rows = pl.ds(i, seg, stride=n)
        return get_wide(dk_ref, 0, t, rows), get_wide(src_ref, 0, t, rows), get_wide(src_ref, t, t, rows)

    def first(i, st):
        ha, hb, prod = st
        d, sa, sb = load(i)
        ra = cos * ha - sin * hb
        rb = cos * hb + sin * ha
        return d * ra + sa, d * rb + sb, prod * d

    ha, hb, prod = lax.fori_loop(0, n, first, (zero, zero, zero + 1.0), unroll=8)
    cn, sn = rot_power(cos_ref[...], sin_ref[...], n)
    ca = jnp.zeros((1, ch), F32)
    cb = jnp.zeros((1, ch), F32)
    for j in range(seg):
        init_ref[j : j + 1, 0:ch] = ca
        init_ref[j : j + 1, ch : 2 * ch] = cb
        pj = prod[j : j + 1, :]
        ta = pj * (cn * ca - sn * cb) + ha[j : j + 1, :]
        cb = pj * (cn * cb + sn * ca) + hb[j : j + 1, :]
        ca = ta

    def second(i, st):
        ha, hb = st
        d, sa, sb = load(i)
        rows = pl.ds(i, seg, stride=n)
        ra = cos * ha - sin * hb
        rb = cos * hb + sin * ha
        ha = d * ra + sa
        hb = d * rb + sb
        live = d > 0.0
        put_wide(h_ref, 0, rows, ha)
        put_wide(h_ref, t, rows, hb)
        put_wide(kr_ref, 0, rows, jnp.where(live, ra, 0.0))
        put_wide(kr_ref, t, rows, jnp.where(live, rb, 0.0))
        return ha, hb

    lax.fori_loop(0, n, second, (init_ref[:, 0:ch], init_ref[:, ch : 2 * ch]), unroll=8)

    gm = gm_ref[...]
    width = wo_ref.shape[1]

    def emit(k, out_ref, i):
        rel = pl.ds(pl.multiple_of(k * blk, blk), blk)
        ab = pl.ds(pl.multiple_of((s ^ k) * blk, blk), blk)
        gated = get_wide(h_ref, 0, 2 * t, ab) * gs_ref[ab, :]
        ss = jnp.sum(gated * gated, axis=1, keepdims=True)
        u = (gated * gm).astype(BF)
        u_ref[rel, :] = u
        out_ref[i, :, 0:width] = mm(u, wo_ref[...]).astype(out_ref.dtype)
        out_ref[i, :, width:] = hilo(ss).astype(out_ref.dtype)

    def emit_send(i, carry):
        emit(2 * i + 1, sout_ref, i)
        return carry

    def emit_keep(i, carry):
        emit(2 * i, kout_ref, i)
        return carry

    lax.fori_loop(0, 2, emit_send, 0)
    lax.fori_loop(0, 2, emit_keep, 0)


def resid_body(x_ref, own_ref, r0_ref, ry_ref, g2_ref, resid_ref, fin_ref, sc_ref, *, chans):
    width = x_ref.shape[1]
    tot = own_ref[...].astype(F32) + r0_ref[...].astype(F32) + ry_ref[...].astype(F32)
    ss = jnp.sum(tot[:, width:], axis=1, keepdims=True)
    sc = lax.rsqrt(ss / chans + EPS)
    resid = x_ref[...].astype(F32) + sc * tot[:, 0:width]
    resid_ref[...] = resid
    sc2 = lax.rsqrt(jnp.mean(resid * resid, axis=1, keepdims=True) + EPS)
    fin_ref[...] = (resid * sc2 * g2_ref[...]).astype(BF)
    sc_ref[...] = jnp.broadcast_to(sc, sc_ref.shape)


def ffn1_body(x_ref, w_ref, hid_ref, p_ref, q_ref):
    tok = x_ref.shape[0]
    blk = tok // 4
    hu = hid_ref.shape[1]

    def step(k, carry):
        rel = pl.ds(pl.multiple_of(k * blk, blk), blk)
        gu = mm(x_ref[rel, :], w_ref[...])
        g = gu[:, 0:hu]
        u = gu[:, hu : 2 * hu]
        sg = sigm(g)
        q = g * sg
        hid_ref[rel, :] = (q * u).astype(BF)
        p_ref[rel, :] = (u * sg * (1.0 + g * (1.0 - sg))).astype(BF)
        q_ref[rel, :] = q.astype(BF)
        return carry

    lax.fori_loop(0, 4, step, 0)


def ffn2_body(c_ref, p_ref, q_ref, wd_ref, w_ref, ggu_ref, kout_ref, sout_ref):
    tok = c_ref.shape[0]
    blk = tok // 4
    hu = p_ref.shape[1]

    def emit(k, out_ref, i):
        rel = pl.ds(pl.multiple_of(k * blk, blk), blk)
        gh = mm_bt(c_ref[rel, :], wd_ref[...])
        gg = gh * p_ref[rel, :].astype(F32)
        gu = gh * q_ref[rel, :].astype(F32)
        both = jnp.concatenate([gg, gu], axis=1).astype(BF)
        ggu_ref[rel, :] = both
        out_ref[i] = mm_bt(both, w_ref[...]).astype(out_ref.dtype)

    def emit_send(i, carry):
        emit(2 * i + 1, sout_ref, i)
        return carry

    def emit_keep(i, carry):
        emit(2 * i, kout_ref, i)
        return carry

    lax.fori_loop(0, 2, emit_send, 0)
    lax.fori_loop(0, 2, emit_keep, 0)


def down_body(h_ref, w_ref, kout_ref, sout_ref):
    blk = h_ref.shape[0] // 4

    def emit(k, out_ref, i):
        rel = pl.ds(pl.multiple_of(k * blk, blk), blk)
        out_ref[i] = mm(h_ref[rel, :], w_ref[...]).astype(out_ref.dtype)

    def emit_send(i, carry):
        emit(2 * i + 1, sout_ref, i)
        return carry

    def emit_keep(i, carry):
        emit(2 * i, kout_ref, i)
        return carry

    lax.fori_loop(0, 2, emit_send, 0)
    lax.fori_loop(0, 2, emit_keep, 0)


def rowgrad_body(idx_ref, x_ref, g_ref, keep_ref, send_ref):
    xi = idx_ref[1]
    half = keep_ref.shape[1]
    for zz in range(4):
        v = mm_at(x_ref[:, zz * 2 * half : (zz + 1) * 2 * half], g_ref[...])
        lo = v[0:half, :]
        hi = v[half : 2 * half, :]
        first = xi == 0
        keep_ref[zz] = jnp.where(first, lo, hi).astype(keep_ref.dtype)
        send_ref[zz] = jnp.where(first, hi, lo).astype(send_ref.dtype)


def colgrad_body(idx_ref, h_ref, c_ref, keep_ref, send_ref):
    xi = idx_ref[1]
    half = keep_ref.shape[2]
    for zz in range(4):
        v = mm_at(h_ref[...], c_ref[:, zz * 2 * half : (zz + 1) * 2 * half])
        lo = v[:, 0:half]
        hi = v[:, half : 2 * half]
        first = xi == 0
        keep_ref[zz] = jnp.where(first, lo, hi).astype(keep_ref.dtype)
        send_ref[zz] = jnp.where(first, hi, lo).astype(send_ref.dtype)


def outgrad_body(idx_ref, u_ref, p_ref, keep_ref, send_ref):
    xi = idx_ref[1]
    y = idx_ref[2]
    for part in range(2):
        rowp = part ^ y
        for cs in range(2):
            u = u_ref[:, part * 256 : (part + 1) * 256]
            lo = mm_at(u, p_ref[:, cs * 256 : (cs + 1) * 256])
            hi = mm_at(u, p_ref[:, (2 + cs) * 256 : (3 + cs) * 256])
            first = xi == 0
            keep_ref[2 * rowp + cs] = jnp.where(first, lo, hi).astype(keep_ref.dtype)
            send_ref[2 * rowp + cs] = jnp.where(first, hi, lo).astype(send_ref.dtype)


def gresid_body(
    own_ref, r0_ref, ry_ref, c_ref, resid_ref, x_ref, sc_ref, g2_ref,
    gres_ref, pay_ref, gg2_ref, *, chans,
):
    width = x_ref.shape[1]
    gfi = own_ref[...].astype(F32) + r0_ref[...].astype(F32) + ry_ref[...].astype(F32)
    resid = resid_ref[...]
    sc2 = lax.rsqrt(jnp.mean(resid * resid, axis=1, keepdims=True) + EPS)
    second = resid * sc2
    gg2_ref[...] = jnp.sum(gfi * second, axis=0, keepdims=True)
    g = gfi * g2_ref[...]
    gres = c_ref[...].astype(F32) + sc2 * (
        g - second * jnp.mean(g * second, axis=1, keepdims=True)
    )
    gres_ref[...] = gres
    sc = sc_ref[:, 0:1]
    branch = resid - x_ref[...].astype(F32)
    kappa = sc * sc * (jnp.sum(gres * branch, axis=1, keepdims=True) / chans)
    pay_ref[:, 0:width] = (gres * sc).astype(BF)
    pay_ref[:, width:] = hilo(kappa)


def mixer_bwd_body(
    idx_ref, p_ref, wo_ref, h_ref, kr_ref, dk_ref, pre_ref, lb_ref, cos_ref, sin_ref, gm_ref,
    g_ref, ggm_ref, gph_ref,
    dir_ref, init_ref, *, seg,
):
    s = idx_ref[0]
    tok = p_ref.shape[0]
    blk = tok // 4
    ch = lb_ref.shape[1]
    n = tok // seg
    t = ch // 128
    width = wo_ref.shape[1]
    gm = gm_ref[...]
    ggm_ref[...] = jnp.zeros_like(ggm_ref)
    gph_ref[...] = jnp.zeros_like(gph_ref)

    def direct(k, carry):
        rel = pl.ds(pl.multiple_of(k * blk, blk), blk)
        ab = pl.ds(pl.multiple_of((s ^ k) * blk, blk), blk)
        back = mm_bt(p_ref[rel, 0:width], wo_ref[...])
        kappa = lanesum(p_ref[rel, width:])
        gs = sigm(pre_ref[ab, 3 * ch : 5 * ch].astype(F32))
        h = get_wide(h_ref, 0, 2 * t, ab)
        gated = h * gs
        ggm_ref[...] += jnp.sum(back * gated, axis=0, keepdims=True)
        gg = back * gm - gated * kappa
        d = gg * gs
        put_wide(dir_ref, 0, ab, d)
        g_ref[rel, 3 * ch : 5 * ch] = (d * h * (1.0 - gs)).astype(BF)
        return carry

    lax.fori_loop(0, 4, direct, 0)

    cos = jnp.broadcast_to(cos_ref[...], (seg, ch))
    sin = jnp.broadcast_to(sin_ref[...], (seg, ch))
    zero = jnp.zeros((seg, ch), F32)

    def load(i):
        rows = pl.ds(i, seg, stride=n)
        return get_wide(dk_ref, 0, t, rows), get_wide(dir_ref, 0, t, rows), get_wide(dir_ref, t, t, rows)

    def first(j, st):
        fa, fb, prod = st
        d, da, db = load(n - 1 - j)
        ga = da + fa
        gb = db + fb
        return d * (cos * ga + sin * gb), d * (cos * gb - sin * ga), prod * d

    fa, fb, prod = lax.fori_loop(0, n, first, (zero, zero, zero + 1.0), unroll=8)
    cn, sn = rot_power(cos_ref[...], sin_ref[...], n)
    ca = jnp.zeros((1, ch), F32)
    cb = jnp.zeros((1, ch), F32)
    for j in reversed(range(seg)):
        init_ref[j : j + 1, 0:ch] = ca
        init_ref[j : j + 1, ch : 2 * ch] = cb
        pj = prod[j : j + 1, :]
        ta = pj * (cn * ca + sn * cb) + fa[j : j + 1, :]
        cb = pj * (cn * cb - sn * ca) + fb[j : j + 1, :]
        ca = ta

    def second(j, st):
        fa, fb = st
        i = n - 1 - j
        d, da, db = load(i)
        rows = pl.ds(i, seg, stride=n)
        ga = da + fa
        gb = db + fb
        put_wide(dir_ref, 0, rows, ga)
        put_wide(dir_ref, t, rows, gb)
        return d * (cos * ga + sin * gb), d * (cos * gb - sin * ga)

    lax.fori_loop(0, n, second, (init_ref[:, 0:ch], init_ref[:, ch : 2 * ch]), unroll=8)

    lb = lb_ref[...]

    def grads(k, carry):
        rel = pl.ds(pl.multiple_of(k * blk, blk), blk)
        ab = pl.ds(pl.multiple_of((s ^ k) * blk, blk), blk)
        ga = get_wide(dir_ref, 0, t, ab)
        gb = get_wide(dir_ref, t, t, ab)
        ra = get_wide(kr_ref, 0, t, ab)
        rb = get_wide(kr_ref, t, t, ab)
        a = pre_ref[ab, 0:ch].astype(F32)
        b = pre_ref[ab, ch : 2 * ch].astype(F32)
        sf = sigm(pre_ref[ab, 2 * ch : 3 * ch].astype(F32))
        sa = sigm(a)
        sb = sigm(b)
        om = (1.0 - lb) * (1.0 - sf)
        gdec = ga * ra + gb * rb - (ga * a * sa + gb * b * sb)
        gph_ref[...] += jnp.sum(get_wide(dk_ref, 0, t, ab) * (gb * ra - ga * rb), axis=0, keepdims=True)
        g_ref[rel, 0:ch] = (ga * (sa * (1.0 + a * (1.0 - sa))) * om).astype(BF)
        g_ref[rel, ch : 2 * ch] = (gb * (sb * (1.0 + b * (1.0 - sb))) * om).astype(BF)
        g_ref[rel, 2 * ch : 3 * ch] = (gdec * om * sf).astype(BF)
        return carry

    lax.fori_loop(0, 4, grads, 0)


def gnormed_body(g_ref, w_ref, kout_ref, sout_ref):
    blk = g_ref.shape[0] // 4

    def emit(k, out_ref, i):
        rel = pl.ds(pl.multiple_of(k * blk, blk), blk)
        out_ref[i] = mm_bt(g_ref[rel, :], w_ref[...]).astype(out_ref.dtype)

    def emit_send(i, carry):
        emit(2 * i + 1, sout_ref, i)
        return carry

    def emit_keep(i, carry):
        emit(2 * i, kout_ref, i)
        return carry

    lax.fori_loop(0, 2, emit_send, 0)
    lax.fori_loop(0, 2, emit_keep, 0)


def gin_body(own_ref, r0_ref, ry_ref, x_ref, gres_ref, g1_ref, out_ref, gg1_ref):
    gn = own_ref[...].astype(F32) + r0_ref[...].astype(F32) + ry_ref[...].astype(F32)
    x = x_ref[...].astype(F32)
    sc = lax.rsqrt(jnp.mean(x * x, axis=1, keepdims=True) + EPS)
    first = x * sc
    gg1_ref[...] = jnp.sum(gn * first, axis=0, keepdims=True)
    nn = gn * g1_ref[...]
    out_ref[...] = (
        gres_ref[...] + sc * (nn - first * jnp.mean(nn * first, axis=1, keepdims=True))
    ).astype(BF)


def seq_gather(v):
    yv = lax.ppermute(v, "seq", YSWAP)
    cv = lax.ppermute(v, "seq", CORE)
    ycv = lax.ppermute(yv, "seq", CORE)
    return jnp.concatenate([v, cv, yv, ycv], axis=0)


def seq_scatter(keep, send):
    got = lax.ppermute(send, "seq", CORE)
    far = (keep[1].astype(F32) + got[1].astype(F32)).astype(BF)
    near = lax.ppermute(far, "seq", YSWAP)
    return keep[0], got[0], near


def batch_gather(pack):
    b = lax.axis_index("batch")
    z, x = b // 2, b % 2
    pieces = [(b, pack), (2 * z + 1 - x, lax.ppermute(pack, "batch", XSWAP))]
    for k in (1, 2, 3):
        got = lax.ppermute(pack, "batch", zshift(k))
        src = (z + 4 - k) % 4
        pieces.append((2 * src + x, got))
        pieces.append((2 * src + 1 - x, lax.ppermute(got, "batch", XSWAP)))
    return pieces


def batch_scatter(keep, send):
    z = lax.axis_index("batch") // 2
    got = lax.ppermute(send, "batch", XSWAP)
    total = lax.dynamic_index_in_dim(keep, z, 0, False).astype(
        F32
    ) + lax.dynamic_index_in_dim(got, z, 0, False).astype(F32)
    for k in (1, 2, 3):
        dst = (z + k) % 4
        part = lax.dynamic_index_in_dim(keep, dst, 0, False).astype(
            F32
        ) + lax.dynamic_index_in_dim(got, dst, 0, False).astype(F32)
        total = total + lax.ppermute(part.astype(BF), "batch", zshift(k)).astype(F32)
    return total


def place_rows(pieces, rows, cols):
    out = jnp.zeros((8 * rows, cols), BF)
    for at, piece in pieces:
        out = lax.dynamic_update_slice(out, piece, (at * rows, 0))
    return out


def per_device(
    block_input, segment_ids, out_cotangent, lower_bound, gain_first, w_input, w_forget,
    w_outgate, phase_angle, gain_mixer, w_output, gain_second, w_gate, w_up, w_down,
):
    s = lax.axis_index("seq")
    b = lax.axis_index("batch")
    y, c = s // 2, s % 2
    z, x = b // 2, b % 2
    nb = lax.axis_size("batch")
    blk, width = block_input.shape[1:]
    tok = 4 * blk
    ch = width // 4
    hu = w_gate.shape[1]
    start = 2 * ch * c + ch * y
    own_x = block_input[0]
    own_c = out_cotangent[0]
    idx = jnp.stack([s, x, y]).astype(jnp.int32)
    wide = nb == 8

    g1n, phn, gmn = gain_first.shape[0], phase_angle.shape[0], gain_mixer.shape[0]
    small = jnp.concatenate(
        [gain_first, gain_second, phase_angle, gain_mixer, segment_ids[0].astype(BF)]
    )
    allsmall = lax.all_gather(small, ("seq", "batch"), axis=0)
    gain1 = allsmall[:, 0:g1n].reshape(1, width).astype(F32)
    gain2 = allsmall[:, g1n : 2 * g1n].reshape(1, width).astype(F32)
    phase = allsmall[:, 2 * g1n : 3 * g1n].reshape(1, width).astype(F32)
    gainm = allsmall[:, 3 * g1n : 3 * g1n + gmn].reshape(2, width).astype(F32)
    ids = allsmall[:, 3 * g1n + gmn :].reshape(4, nb, blk)
    ids = lax.dynamic_index_in_dim(ids, b, 1, False).reshape(tok)
    keep = jnp.concatenate([jnp.zeros((1,), F32), (ids[1:] == ids[:-1]).astype(F32)])[:, None]
    phase = lax.dynamic_slice(phase, (0, start), (1, ch))
    sign = jnp.where(y == 0, 1.0, -1.0).astype(F32)
    cos = jnp.cos(phase)
    sin = jnp.sin(phase) * sign
    lb = lax.dynamic_slice(lower_bound[None, :], (0, start), (1, ch))
    gm_nat = lax.dynamic_slice(gainm, (y, start), (1, ch))
    gm_for = lax.dynamic_slice(gainm, (1 - y, start), (1, ch))
    gm = jnp.concatenate([gm_nat, gm_for], axis=1)

    def halves(w):
        nat = lax.dynamic_slice(w, (0, y * ch), (w.shape[0], ch))
        far = lax.dynamic_slice(w, (0, (1 - y) * ch), (w.shape[0], ch))
        return nat, far

    in_nat, in_far = halves(w_input)
    og_nat, og_far = halves(w_outgate)
    far = lax.ppermute(jnp.concatenate([in_far, og_far], axis=1), "seq", YSWAP)
    fg = lax.ppermute(w_forget, "seq", FORGET_PERM)
    pack_a = jnp.concatenate([in_nat, far[:, 0:ch], fg, og_nat, far[:, ch:]], axis=1)
    pack_c = jnp.concatenate([w_gate, w_up], axis=1)
    if wide:
        w_a = place_rows(batch_gather(pack_a), pack_a.shape[0], 5 * ch)
        moved = lax.ppermute(w_output, ("seq", "batch"), OUT_PERM)
        w_o = jnp.zeros((2 * ch, width), BF)
        for at, piece in batch_gather(moved):
            zz, xx = at // 2, at % 2
            w_o = lax.dynamic_update_slice(
                w_o, piece, (((zz // 2) ^ y) * ch, (2 * xx + zz % 2) * ch)
            )
        w_c = place_rows(batch_gather(pack_c), pack_c.shape[0], 2 * hu)
        w_d = jnp.zeros((hu, width), BF)
        for at, piece in batch_gather(w_down):
            w_d = lax.dynamic_update_slice(w_d, piece, (0, at * piece.shape[1]))
    else:
        w_a = lax.all_gather(pack_a, "batch", axis=0, tiled=True)
        w_c = lax.all_gather(pack_c, "batch", axis=0, tiled=True)
        w_d = lax.all_gather(w_down, "batch", axis=1, tiled=True)
        full = lax.all_gather(w_output, "batch", axis=0, tiled=True)
        full = lax.all_gather(full, "seq", axis=1, tiled=True)
        w_o = jnp.concatenate(
            [
                lax.dynamic_slice(full, (y * width + start, 0), (ch, width)),
                lax.dynamic_slice(full, ((1 - y) * width + start, 0), (ch, width)),
            ],
            axis=0,
        )

    x_own = call(norm1_body, [sds((blk, width), BF)], [own_x, gain1], name="norm1")[0]
    xn = seq_gather(x_own)
    cot = seq_gather(own_c)
    seg = 8
    tiles = ch // 128
    pre, dk, h, kr, u, kout, sout = call(
        functools.partial(mixer_fwd_body, seg=seg),
        [
            sds((tok, 5 * ch), BF), sds((tiles, tok, 128), F32), sds((2 * tiles, tok, 128), F32),
            sds((2 * tiles, tok, 128), F32), sds((tok, 2 * ch), BF),
            sds((2, blk, width + 128), F32), sds((2, blk, width + 128), BF),
        ],
        [idx, xn, w_a, w_o, keep, lb, cos, sin, gm],
        scratch=[
            pltpu.VMEM((2 * tiles, tok, 128), F32), pltpu.VMEM((tok, 2 * ch), F32),
            pltpu.VMEM((seg, 2 * ch), F32),
        ],
        smem=1, flops=2 * tok * width * 7 * ch, name="mixer_fwd",
    )
    own, r0, ry = seq_scatter(kout, sout)
    resid, fin, sc = call(
        functools.partial(resid_body, chans=2.0 * width),
        [sds((blk, width), F32), sds((blk, width), BF), sds((blk, 128), F32)],
        [own_x, own, r0, ry, gain2], name="resid",
    )
    ffn_in = seq_gather(fin)
    hid, p, q = call(
        ffn1_body, [sds((tok, hu), BF)] * 3, [ffn_in, w_c],
        flops=4 * tok * width * hu, name="ffn1",
    )
    ggu, kout2, sout2 = call(
        ffn2_body,
        [sds((tok, 2 * hu), BF), sds((2, blk, width), F32), sds((2, blk, width), BF)],
        [cot, p, q, w_d, w_c], flops=6 * tok * width * hu, name="ffn2",
    )
    own2, r02, ry2 = seq_scatter(kout2, sout2)
    kd, sd = call(
        colgrad_body, [sds((4, hu, width // 8), F32), sds((4, hu, width // 8), BF)],
        [idx, hid, cot], smem=1, flops=2 * tok * width * hu, name="down_grad",
    )
    kc, scd = call(
        rowgrad_body, [sds((4, width // 8, 2 * hu), F32), sds((4, width // 8, 2 * hu), BF)],
        [idx, ffn_in, ggu], smem=1, flops=4 * tok * width * hu, name="gu_grad",
    )
    kout3, sout3 = call(
        down_body, [sds((2, blk, width), F32), sds((2, blk, width), BF)],
        [hid, w_d], flops=2 * tok * width * hu, name="down",
    )
    own3, r03, ry3 = seq_scatter(kout3, sout3)
    block_output = (
        resid + own3 + r03.astype(F32) + ry3.astype(F32)
    ).astype(BF)[None]

    gres, pay, gg2 = call(
        functools.partial(gresid_body, chans=2.0 * width),
        [sds((blk, width), F32), sds((blk, width + 128), BF), sds((1, width), F32)],
        [own2, r02, ry2, own_c, resid, own_x, sc, gain2], name="gresid",
    )
    pays = seq_gather(pay)
    gall, ggm, gph = call(
        functools.partial(mixer_bwd_body, seg=seg),
        [sds((tok, 5 * ch), BF), sds((1, 2 * ch), F32), sds((1, ch), F32)],
        [idx, pays, w_o, h, kr, dk, pre, lb, cos, sin, gm],
        scratch=[pltpu.VMEM((2 * tiles, tok, 128), F32), pltpu.VMEM((seg, 2 * ch), F32)],
        smem=1, flops=2 * tok * width * 2 * ch, name="mixer_bwd",
    )
    ko, so = call(
        outgrad_body, [sds((4, ch, ch), F32), sds((4, ch, ch), BF)],
        [idx, u, pays], smem=1, flops=2 * tok * width * 2 * ch, name="out_grad",
    )
    ka, sa = call(
        rowgrad_body, [sds((4, width // 8, 5 * ch), F32), sds((4, width // 8, 5 * ch), BF)],
        [idx, xn, gall], smem=1, flops=2 * tok * width * 5 * ch, name="in_grad",
    )
    kout4, sout4 = call(
        gnormed_body, [sds((2, blk, width), F32), sds((2, blk, width), BF)],
        [gall, w_a], flops=2 * tok * width * 5 * ch, name="gnormed",
    )
    own4, r04, ry4 = seq_scatter(kout4, sout4)
    grad_input, gg1 = call(
        gin_body, [sds((blk, width), BF), sds((1, width), F32)],
        [own4, r04, ry4, own_x, gres, gain1], name="gin",
    )

    if wide:
        g_d = batch_scatter(kd, sd)
        g_c = batch_scatter(kc, scd)
        g_o = lax.ppermute(batch_scatter(ko, so), ("seq", "batch"), OUT_BACK)
        g_a = batch_scatter(ka, sa)
    else:
        def whole(keep_part, send_part, axis):
            first = jnp.where(x == 0, keep_part, send_part.astype(F32))
            second = jnp.where(x == 0, send_part.astype(F32), keep_part)
            both = jnp.stack([first, second], axis=1)
            return both.reshape((8,) + keep_part.shape[1:])

        d8 = whole(kd, sd, 1)
        d_full = jnp.swapaxes(d8, 0, 1).reshape(hu, width)
        g_d = lax.psum_scatter(d_full, "batch", scatter_dimension=1, tiled=True)
        g_c = lax.psum_scatter(
            whole(kc, scd, 0).reshape(width, 2 * hu), "batch", scatter_dimension=0, tiled=True
        )
        g_a = lax.psum_scatter(
            whole(ka, sa, 0).reshape(width, 5 * ch), "batch", scatter_dimension=0, tiled=True
        )
        o8 = whole(ko, so, 0).reshape(2, 2, 2, ch, ch)
        o_full = jnp.transpose(o8, (0, 3, 2, 1, 4)).reshape(2, ch, width)
        spread = jnp.zeros((2, width, width), F32)
        spread = lax.dynamic_update_slice(spread, o_full, (0, start, 0)).reshape(
            2 * width, width
        )
        g_o = lax.psum_scatter(spread, "batch", scatter_dimension=0, tiled=True)
        g_o = lax.psum_scatter(g_o, "seq", scatter_dimension=1, tiled=True)

    far_back = lax.ppermute(
        jnp.concatenate([g_a[:, ch : 2 * ch], g_a[:, 4 * ch :]], axis=1), "seq", YSWAP
    )
    g_f = lax.ppermute(g_a[:, 2 * ch : 3 * ch], "seq", [(d, q2) for q2, d in FORGET_PERM])

    def rejoin(nat, farp):
        return jnp.where(
            y == 0,
            jnp.concatenate([nat, farp], axis=1),
            jnp.concatenate([farp, nat], axis=1),
        )

    g_in = rejoin(g_a[:, 0:ch], far_back[:, 0:ch])
    g_og = rejoin(g_a[:, 3 * ch : 4 * ch], far_back[:, ch:])

    ggm2 = jnp.where(
        y == 0,
        ggm.reshape(2, ch),
        jnp.concatenate([ggm[:, ch:], ggm[:, 0:ch]], axis=0),
    )
    spread_gm = lax.dynamic_update_slice(jnp.zeros((2, width), F32), ggm2, (0, start))
    spread_ph = lax.dynamic_update_slice(jnp.zeros((1, width), F32), gph * sign, (0, start))
    nd = 4 * nb
    vec = jnp.concatenate(
        [
            gg1.reshape(nd, -1), gg2.reshape(nd, -1), spread_ph.reshape(nd, -1),
            spread_gm.reshape(nd, -1),
        ],
        axis=1,
    )
    mine = lax.psum(vec, ("seq", "batch"))
    mine = lax.dynamic_index_in_dim(mine, s * nb + b, 0, False)
    gg1o = mine[0:g1n]
    gg2o = mine[g1n : 2 * g1n]
    gpho = mine[2 * g1n : 3 * g1n]
    ggmo = mine[3 * g1n :]
    return (
        block_output, grad_input[None], gg1o, g_in, g_f, g_og, gpho, ggmo, g_o, gg2o,
        g_c[:, 0:hu], g_c[:, hu:], g_d,
    )


def solution(mesh):
    both = P(("seq", "batch"))
    mat = P("batch", "seq")
    in_specs = (
        P("batch", "seq", None), P("batch", "seq"), P("batch", "seq", None), P(), both, mat,
        mat, mat, both, both, mat, both, mat, mat, P("seq", "batch"),
    )
    out_specs = (
        P("batch", "seq", None), P("batch", "seq", None), both, mat, mat, mat, both, both, mat,
        both, mat, mat, P("seq", "batch"),
    )
    return jax.shard_map(
        per_device, mesh=mesh, in_specs=in_specs, out_specs=out_specs, check_vma=False
    )
```

```python
import functools
import math

import jax
import jax.numpy as jnp
from jax import lax
from jax.experimental import pallas as pl
from jax.experimental.pallas import tpu as pltpu
from jax.sharding import PartitionSpec as P

EPS = 1e-6
F32 = jnp.float32
BF = jnp.bfloat16
MB = 1024 * 1024

CORE = [(s, s ^ 1) for s in range(4)]
YSWAP = [(s, s ^ 2) for s in range(4)]
XSWAP = [(b, b ^ 1) for b in range(8)]


def zshift(k):
    return [(2 * z + x, 2 * ((z + k) % 4) + x) for z in range(4) for x in range(2)]


def out_block_perm():
    pairs = []
    for s in range(4):
        for b in range(8):
            y, c, part = b & 1, (b >> 1) & 1, b >> 2
            ys, cs = s >> 1, s & 1
            pairs.append((s * 8 + b, (2 * y + c) * 8 + 2 * (2 * part + cs) + ys))
    return pairs


OUT_PERM = out_block_perm()
OUT_BACK = [(d, s) for s, d in OUT_PERM]
FORGET_PERM = [(2 * (d & 1) + (d >> 1), d) for d in range(4)]


def sigm(v):
    return 0.5 * jnp.tanh(0.5 * v) + 0.5


def mm(a, b):
    return jnp.dot(a, b, preferred_element_type=F32)


def mm_bt(a, b):
    return lax.dot_general(a, b, (((1,), (1,)), ((), ())), preferred_element_type=F32)


def mm_at(a, b):
    return lax.dot_general(a, b, (((0,), (0,)), ((), ())), preferred_element_type=F32)


def sds(shape, dtype):
    return jax.ShapeDtypeStruct(shape, dtype)


HBM, SMEM, VMEM = "hbm", "smem", "vmem"


def tiled_bytes(a):
    shape = (1, 1) + tuple(a.shape)
    lanes, rows = -(-shape[-1] // 128) * 128, -(-shape[-2] // 16) * 16
    return math.prod(shape[:-2]) * rows * lanes * jnp.dtype(a.dtype).itemsize


def call(body, outs, args, kinds=None, okinds=None, scratch=(), room=8, flops=0, name=None):
    kinds = kinds or [VMEM] * len(args)
    okinds = okinds or [VMEM] * len(outs)
    held = sum(tiled_bytes(a) for a, k in zip(args, kinds) if k == VMEM)
    held += sum(tiled_bytes(o) for o, k in zip(outs, okinds) if k == VMEM)
    held += sum(tiled_bytes(m) for m in scratch if m.memory_space == pltpu.VMEM)
    vmem = 63 if room is None else -(-held // MB) + room
    space = {HBM: pl.ANY, SMEM: pltpu.SMEM, VMEM: pltpu.VMEM}
    nbytes = sum(a.size * a.dtype.itemsize for a in args)
    nbytes += sum(o.size * o.dtype.itemsize for o in outs)
    return pl.pallas_call(
        body,
        out_shape=outs,
        in_specs=[pl.BlockSpec(memory_space=space[k]) for k in kinds],
        out_specs=[pl.BlockSpec(memory_space=space[k]) for k in okinds],
        scratch_shapes=list(scratch),
        compiler_params=pltpu.CompilerParams(vmem_limit_bytes=vmem * MB),
        cost_estimate=pl.CostEstimate(
            flops=10 * (flops + 3 * 10**8), bytes_accessed=nbytes, transcendentals=0
        ),
        name=name,
    )(*args)


def hilo(col):
    rows = col.shape[0]
    hi = col.astype(BF)
    lo = (col - hi.astype(F32)).astype(BF)
    lane = lax.broadcasted_iota(jnp.int32, (rows, 128), 1)
    hi_b = jnp.broadcast_to(hi.astype(F32), (rows, 128))
    lo_b = jnp.broadcast_to(lo.astype(F32), (rows, 128))
    return jnp.where(lane == 0, hi_b, jnp.where(lane == 1, lo_b, 0.0)).astype(BF)


def lanesum(tile):
    return jnp.sum(tile.astype(F32), axis=1, keepdims=True)


def interleave(blk, back):
    row = lax.broadcasted_iota(jnp.int32, (blk, blk), 0)
    col = lax.broadcasted_iota(jnp.int32, (blk, blk), 1)
    if back:
        row, col = col, row
    hit = col == (row % 8) * (blk // 8) + row // 8
    return jnp.where(hit, 1.0, 0.0).astype(BF)


class Copies:
    def __init__(self, sems):
        self.sems, self.used = sems, 0

    def start(self, pairs):
        made = []
        for src, dst in pairs:
            made.append(pltpu.make_async_copy(src, dst, self.sems.at[self.used]))
            made[-1].start()
            self.used += 1
        return made


def wait_all(made):
    for m in made:
        m.wait()


def rows_of(i, n):
    return pl.ds(pl.multiple_of(i * n, n), n)


def norm1_body(x_ref, c_ref, o_ref, xp_ref, cp_ref):
    perm = interleave(x_ref.shape[0], False)
    x = mm(perm, x_ref[...])
    xp_ref[...] = x.astype(BF)
    cp_ref[...] = mm(perm, c_ref[...]).astype(BF)
    sc = lax.rsqrt(jnp.mean(x * x, axis=1, keepdims=True) + EPS)
    o_ref[...] = (x * sc).astype(BF)


def line_body(g1_ref, g2_ref, ph_ref, gm_ref, id_ref, o_ref):
    line = jnp.concatenate([g1_ref[...], g2_ref[...], ph_ref[...], gm_ref[...]])[None, :]
    line = jnp.concatenate([line.astype(F32), jnp.zeros((1, 256 - line.shape[1]), F32)], axis=1)
    both = jnp.concatenate([id_ref[...].astype(F32), line], axis=1)
    o_ref[...] = jnp.broadcast_to(both, o_ref.shape).astype(BF)


def pack_body(idx_ref, in_ref, og_ref, far_ref, fg_ref, out_ref, l_ref, lx_ref, o_ref, both_ref):
    rows, ch = fg_ref.shape
    nat = rows_of(idx_ref[2], ch)
    o_ref[0:rows, 0:ch] = in_ref[:, nat]
    o_ref[0:rows, ch : 2 * ch] = far_ref[:, 0:ch]
    o_ref[0:rows, 2 * ch : 3 * ch] = fg_ref[...]
    o_ref[0:rows, 3 * ch : 4 * ch] = og_ref[:, nat]
    o_ref[0:rows, 4 * ch : 5 * ch] = far_ref[:, ch:]
    o_ref[0:rows, 5 * ch : 6 * ch] = out_ref[0:rows, :]
    o_ref[0:rows, 6 * ch : 7 * ch] = out_ref[rows:, :]
    top = lax.broadcasted_iota(jnp.int32, l_ref.shape, 0) < 8
    both_ref[...] = jnp.where(top, l_ref[...].astype(F32), lx_ref[...].astype(F32)).astype(BF)


def smalls_body(
    idx_ref, v0, v1, v2, v3, lb_in,
    g1_ref, g2_ref, cos_ref, sin_ref, gm_ref, lb_ref, keep_ref,
    line_ref, ph_ref, gmix_ref,
):
    s, x, y, z = (idx_ref[i] for i in range(4))
    width = g1_ref.shape[1]
    ch = cos_ref.shape[1]
    blk = keep_ref.shape[1]
    vs = [
        jnp.concatenate([v[8 * j : 8 * j + 1, :] for j in range(8)], axis=0)
        for v in (v0, v1, v2, v3)
    ]
    rows = jnp.concatenate([v[:, blk:].astype(F32) for v in vs], axis=0)
    r = lax.broadcasted_iota(jnp.int32, (32, width), 0)
    lane = lax.broadcasted_iota(jnp.int32, (32, width), 1)
    i = r & 7
    piece = 2 * ((z - (i >> 1)) & 3) + jnp.where((i & 1) == 0, x, 1 - x)
    device = ((r >> 3) ^ s) * 8 + piece

    def spread(first, size):
        place = lax.broadcasted_iota(jnp.int32, (256, width), 0) - first
        to = lax.broadcasted_iota(jnp.int32, (256, width), 1) & (size - 1)
        one = jnp.where(place == to, 1.0, 0.0).astype(BF)
        wide = mm(rows.astype(BF), one)
        out = []
        for part in range(32 * size // width):
            mine = (lane + part * width) // size == device
            out.append(jnp.sum(jnp.where(mine, wide, 0.0), axis=0, keepdims=True))
        return out

    g1_ref[...] = spread(0, 32)[0]
    g2_ref[...] = spread(32, 32)[0]
    ph_ref[...] = spread(64, 32)[0]
    both = spread(96, 64)
    gmix_ref[0] = both[0]
    gmix_ref[1] = both[1]
    here = rows_of(2 * (s & 1) + (s >> 1), ch)
    phase = ph_ref[:, here]
    cos_ref[...] = jnp.cos(phase)
    sin_ref[...] = jnp.where(y == 0, 1.0, -1.0) * jnp.sin(phase)
    line_ref[...] = lb_in[...]
    lb_ref[...] = line_ref[:, here]
    gm_ref[:, 0:ch] = gmix_ref[y, :, here]
    gm_ref[:, ch:] = gmix_ref[1 - y, :, here]

    ids = [v[0:1, 0:blk].astype(F32) for v in vs]
    perm = interleave(blk, False)
    first = lax.broadcasted_iota(jnp.int32, (16, blk), 1) == 0
    for k in range(4):
        at = k ^ s
        last = jnp.full((1, 1), -1.0, F32)
        for q in range(4):
            last = jnp.where((q ^ s) == at - 1, ids[q][:, blk - 1 : blk], last)
        mine = jnp.broadcast_to(ids[k], (16, blk))
        before = jnp.where(first, jnp.broadcast_to(last, (16, blk)), pltpu.roll(mine, 1, 1))
        same = jnp.where(mine == before, 1.0, 0.0).astype(BF)
        keep_ref[k] = mm_bt(perm, same)[:, 0:1]


def rot_power(cos, sin, steps):
    n = 1
    while n < steps:
        cos, sin = cos * cos - sin * sin, 2.0 * cos * sin
        n *= 2
    return cos, sin


def combine_segments(s, order, end_ref, prod_ref, init_ref, ch, cn, sn):
    ca = jnp.zeros((1, ch), F32)
    cb = jnp.zeros((1, ch), F32)
    for at in order:
        k = at ^ s
        for j in range(8) if order[0] == 0 else reversed(range(8)):
            init_ref[k, j : j + 1, 0:ch] = ca
            init_ref[k, j : j + 1, ch : 2 * ch] = cb
            pj = prod_ref[k, j : j + 1, :]
            ta = pj * (cn * ca - sn * cb) + end_ref[k, j : j + 1, 0:ch]
            cb = pj * (cn * cb + sn * ca) + end_ref[k, j : j + 1, ch : 2 * ch]
            ca = ta


def blocks_in(refs, dst, blk):
    return [(r, dst.at[rows_of(k, blk)]) for k, r in enumerate(refs)]


def mix_in_copies(idx_ref, pieces, dst):
    cols = dst.shape[1]
    if len(pieces) == 1:
        return [(pieces[0].at[:, pl.ds(0, cols)], dst)]
    rows = dst.shape[0] // 8
    return [
        (p.at[pl.ds(0, rows), pl.ds(0, cols)], dst.at[rows_of(idx_ref[4 + i], rows)])
        for i, p in enumerate(pieces)
    ]


def mix_out_copies(idx_ref, pieces, dst):
    ch = dst.shape[0] // 2
    if len(pieces) == 1:
        return [(pieces[0], dst)]
    half = ch // 2
    out = []
    for i, p in enumerate(pieces):
        for j in range(2):
            rows = pl.ds(pl.multiple_of(idx_ref[12 + i] * ch + j * half, half), half)
            src = p.at[pl.ds(0, half), pl.ds((5 + j) * ch, ch)]
            out.append((src, dst.at[rows, rows_of(idx_ref[20 + i], ch)]))
    return out


def mixer_fwd_body(*refs, pieces):
    idx_ref, *refs = refs
    xs, refs = refs[:4], refs[4:]
    ps, refs = refs[:pieces], refs[pieces:]
    os, refs = (refs[:1], refs[1:]) if pieces == 1 else (ps, refs)
    (
        g1_ref, keep_ref, lb_ref, cos_ref, sin_ref, gm_ref,
        pre_out, dk_out, h_out, kr_out, k0_out, k1_out, s_out,
        x_ref, w_ref, wo_ref, pre_ref, dk_ref, h_ref, kr_ref, k0_ref, k1_ref, sout_ref,
        src_ref, gs_ref, end_ref, prod_ref, init_ref, sems,
    ) = refs
    s = idx_ref[0]
    ch = lb_ref.shape[1]
    blk = dk_ref.shape[1]
    width = wo_ref.shape[1]
    n = blk // 8
    dma = Copies(sems)
    need = dma.start(blocks_in(xs, x_ref, blk) + mix_in_copies(idx_ref, ps, w_ref))
    need_out = dma.start(mix_out_copies(idx_ref, os, wo_ref))
    wait_all(need)

    lb = lb_ref[...]
    g1 = g1_ref[...]
    saved = []
    for k in range(4):
        xg = (x_ref[rows_of(k, blk), :].astype(F32) * g1).astype(BF)
        p = mm(xg, w_ref[...])
        pre_ref[k] = p.astype(BF)
        sig = sigm(p[:, 2 * ch : 3 * ch])
        om = (1.0 - lb) * (1.0 - sig)
        dk_ref[k] = keep_ref[k] * (lb + (1.0 - lb) * sig)
        a = p[:, 0:ch]
        b = p[:, ch : 2 * ch]
        src_ref[k, :, 0:ch] = a * sigm(a) * om
        src_ref[k, :, ch : 2 * ch] = b * sigm(b) * om
        gs_ref[k] = sigm(p[:, 3 * ch : 5 * ch])
        saved += dma.start([(pre_ref.at[k], pre_out.at[k]), (dk_ref.at[k], dk_out.at[k])])

    cos = cos_ref[...][None]
    sin = sin_ref[...][None]
    zero = jnp.zeros((4, 8, ch), F32)

    def load(i):
        rows = rows_of(i, 8)
        return dk_ref[:, rows, :], src_ref[:, rows, 0:ch], src_ref[:, rows, ch : 2 * ch]

    def first_pass(i, st):
        ha, hb, prod = st
        d, sa, sb = load(i)
        ra = cos * ha - sin * hb
        rb = cos * hb + sin * ha
        return d * ra + sa, d * rb + sb, prod * d

    ha, hb, prod = lax.fori_loop(0, n, first_pass, (zero, zero, zero + 1.0), unroll=4)
    end_ref[:, :, 0:ch] = ha
    end_ref[:, :, ch : 2 * ch] = hb
    prod_ref[...] = prod
    cn, sn = rot_power(cos_ref[...], sin_ref[...], n)
    combine_segments(s, (0, 1, 2, 3), end_ref, prod_ref, init_ref, ch, cn, sn)

    def second_pass(i, st):
        ha, hb = st
        d, sa, sb = load(i)
        rows = rows_of(i, 8)
        ra = cos * ha - sin * hb
        rb = cos * hb + sin * ha
        ha = d * ra + sa
        hb = d * rb + sb
        live = d > 0.0
        h_ref[:, rows, 0:ch] = ha
        h_ref[:, rows, ch : 2 * ch] = hb
        kr_ref[:, rows, 0:ch] = jnp.where(live, ra, 0.0)
        kr_ref[:, rows, ch : 2 * ch] = jnp.where(live, rb, 0.0)
        return ha, hb

    lax.fori_loop(
        0, n, second_pass, (init_ref[:, :, 0:ch], init_ref[:, :, ch : 2 * ch]), unroll=4
    )
    saved += dma.start([(h_ref, h_out), (kr_ref, kr_out)])
    wait_all(need_out)
    gm = gm_ref[...]

    def emit(k):
        gated = h_ref[k] * gs_ref[k]
        ss = jnp.sum(gated * gated, axis=1, keepdims=True)
        return mm((gated * gm).astype(BF), wo_ref[...]), hilo(ss)

    for i in range(2):
        v, tail = emit(2 * i + 1)
        sout_ref[i, :, 0:width] = v.astype(BF)
        sout_ref[i, :, width:] = tail
        saved += dma.start([(sout_ref.at[i], s_out.at[i])])
    for k, ref, out in ((2, k1_ref, k1_out), (0, k0_ref, k0_out)):
        v, tail = emit(k)
        ref[:, 0:width] = v.astype(BF)
        ref[:, width:] = tail
        saved += dma.start([(ref, out)])
    wait_all(saved)


def resid_body(x_ref, own_ref, got_ref, ry_ref, g2_ref, resid_ref, fin_ref, sc_ref, *, chans):
    width = x_ref.shape[1]
    tot = own_ref[...].astype(F32) + got_ref[0].astype(F32) + ry_ref[...].astype(F32)
    ss = jnp.sum(tot[:, width:], axis=1, keepdims=True)
    sc = lax.rsqrt(ss / chans + EPS)
    resid = x_ref[...].astype(F32) + sc * tot[:, 0:width]
    resid_ref[...] = resid
    sc2 = lax.rsqrt(jnp.mean(resid * resid, axis=1, keepdims=True) + EPS)
    fin_ref[...] = (resid * sc2 * g2_ref[...]).astype(BF)
    sc_ref[...] = jnp.broadcast_to(sc, sc_ref.shape)


def col_copies(idx_ref, pieces, dst):
    if len(pieces) == 1:
        return [(pieces[0], dst)]
    out = []
    for i, p in enumerate(pieces):
        rows, cols = p.shape
        place = i if i < 8 else 2 if i == 8 else 6
        at = pl.ds(0 if i < 8 else rows, rows)
        out.append((p, dst.at[at, rows_of(idx_ref[4 + place], cols)]))
    return out


def ffn_body(*refs, pieces):
    idx_ref, *refs = refs
    xs, cots, refs = refs[:4], refs[4:8], refs[8:]
    ps, refs = refs[:pieces], refs[pieces:]
    (
        hid_out, ggu_out, k0_out, k1_out, s_out, kept2_out, s2_out,
        x_ref, c_ref, w_ref, hid_ref, ggu_ref, k0_ref, k1_ref, sout_ref, kept2_ref, s2_ref, sems,
    ) = refs
    blk = k0_ref.shape[0]
    hu = hid_ref.shape[1]
    dma = Copies(sems)
    need = dma.start(blocks_in(xs, x_ref, blk) + col_copies(idx_ref, ps, w_ref))
    later = dma.start(blocks_in(cots, c_ref, blk))
    wait_all(need)
    saved = []
    for k in (1, 3, 2, 0):
        rel = pl.ds(k * blk, blk)
        gu = mm_bt(x_ref[rel, :], w_ref[0 : 2 * hu, :])
        wait_all(later)
        later = []
        gh = mm_bt(c_ref[rel, :], w_ref[2 * hu :, :])
        g = gu[:, 0:hu]
        u = gu[:, hu : 2 * hu]
        sg = sigm(g)
        q = g * sg
        hid_ref[rel, :] = (q * u).astype(BF)
        dg = gh * (u * (sg + q * (1.0 - sg)))
        both = jnp.concatenate([dg, gh * q], axis=1).astype(BF)
        ggu_ref[rel, :] = both
        saved += dma.start(
            [(hid_ref.at[rel], hid_out.at[rel]), (ggu_ref.at[rel], ggu_out.at[rel])]
        )
        back = mm(both, w_ref[0 : 2 * hu, :])
        if k in (1, 3):
            sout_ref[k // 2] = back.astype(BF)
            saved += dma.start([(sout_ref.at[k // 2], s_out.at[k // 2])])
        else:
            ref, out = (k1_ref, k1_out) if k == 2 else (k0_ref, k0_out)
            ref[...] = back.astype(BF)
            saved += dma.start([(ref, out)])
    ffn_grad_part(idx_ref, 2, ggu_ref, hid_ref, x_ref, c_ref, kept2_ref, s2_ref)
    wait_all(saved + dma.start([(kept2_ref, kept2_out), (s2_ref, s2_out)]))


def down_body(*refs, pieces):
    idx_ref, h_ref, *refs = refs
    ps, refs = refs[:pieces], refs[pieces:]
    k0_ref, k1_ref, sout_ref, wd_ref, sems = refs
    blk = k0_ref.shape[0]
    hu = h_ref.shape[1]
    if pieces > 1:
        last = {2: ps[8], 6: ps[9]}
        ps = [last.get(i, p) for i, p in enumerate(ps[:8])]
    ps = [p.at[pl.ds(p.shape[0] - hu, hu)] for p in ps]
    wait_all(Copies(sems).start(col_copies(idx_ref, ps, wd_ref)))

    def emit(k):
        return mm(h_ref[rows_of(k, blk), :], wd_ref[...])

    sout_ref[0] = emit(1).astype(BF)
    sout_ref[1] = emit(3).astype(BF)
    k1_ref[...] = emit(2).astype(BF)
    k0_ref[...] = emit(0).astype(BF)


def put_parts(kk, keep, send, outs, where):
    kept_ref, send_ref = outs[kk]
    kept_ref[where] = keep.astype(kept_ref.dtype)
    send_ref[where] = send.astype(BF)


def ffn_grad_part(idx_ref, kk, g_ref, h_ref, x_ref, c_ref, keep_ref, send_ref):
    first = idx_ref[1] == 0
    hu = h_ref.shape[1]
    cols = rows_of((idx_ref[3] + kk) & 3, 256)
    for src, left, at, size in ((x_ref, g_ref, 0, 2 * hu), (c_ref, h_ref, 2 * hu, hu)):
        v = mm_at(left[...], src[:, cols])
        lo, hi = v[:, 0:128], v[:, 128:256]
        where = pl.ds(at, size)
        keep_ref[where, :] = jnp.where(first, lo, hi).astype(keep_ref.dtype)
        send_ref[where, :] = jnp.where(first, hi, lo).astype(send_ref.dtype)


def ffn_grad_body(
    idx_ref, h_ref, g_ref, x0, x1, x2, x3, c0, c1, c2, c3,
    own_ref, k1_ref, k3_ref, s1_ref, s3_ref, s0_ref, x_ref, c_ref, sems,
):
    blk = x_ref.shape[0] // 4
    dma = Copies(sems)
    need = dma.start(blocks_in((x0, x1, x2, x3), x_ref, blk))
    need += dma.start(blocks_in((c0, c1, c2, c3), c_ref, blk))
    wait_all(need)
    for kk, keep, send in (
        (1, k1_ref, s1_ref), (3, k3_ref, s3_ref), (0, own_ref, s0_ref),
    ):
        ffn_grad_part(idx_ref, kk, g_ref, h_ref, x_ref, c_ref, keep, send)


def gresid_body(
    own_ref, got_ref, ry_ref, c_ref, resid_ref, x_ref, sc_ref, g2_ref,
    gres_ref, pay_ref, gg2_ref, *, chans,
):
    width = x_ref.shape[1]
    gfi = own_ref[...].astype(F32) + got_ref[0].astype(F32) + ry_ref[...].astype(F32)
    resid = resid_ref[...]
    sc2 = lax.rsqrt(jnp.mean(resid * resid, axis=1, keepdims=True) + EPS)
    second = resid * sc2
    gg2_ref[...] = jnp.sum(gfi * second, axis=0, keepdims=True)
    g = gfi * g2_ref[...]
    gres = c_ref[...].astype(F32) + sc2 * (
        g - second * jnp.mean(g * second, axis=1, keepdims=True)
    )
    gres_ref[...] = gres
    sc = sc_ref[:, 0:1]
    branch = resid - x_ref[...].astype(F32)
    kappa = sc * sc * (jnp.sum(gres * branch, axis=1, keepdims=True) / chans)
    pay_ref[:, 0:width] = (gres * sc).astype(BF)
    pay_ref[:, width:] = hilo(kappa)


def bwd_body(*refs, pieces):
    idx_ref, *refs = refs
    pays, xs, refs = refs[:4], refs[4:8], refs[8:]
    ps, refs = refs[:pieces], refs[pieces:]
    os, refs = (refs[:1], refs[1:]) if pieces == 1 else (ps, refs)
    (
        pre_in, dk_in, h_in, kr_in, lb_ref, cos_ref, sin_ref, g1_ref, gm_ref,
        ggm_ref, gph_ref, own_out, e1_out, e3_out, e2_out, s2_out, s1_out, s3_out, s0_out,
        k0_out, k1_out, s_out,
        own_ref, e1_ref, e3_ref, e2_ref, s2_ref, s1_ref, s3_ref, s0_ref,
        k0_ref, k1_ref, sout_ref,
        p_ref, x_ref, w_ref, wo_ref, pre_ref, dk_ref, h_ref, kr_ref, u_ref, g_ref, dir_ref,
        end_ref, prod_ref, init_ref, sems,
    ) = refs
    s = idx_ref[0]
    ch = lb_ref.shape[1]
    blk = dk_ref.shape[1]
    n = blk // 8
    width = wo_ref.shape[1]
    dma = Copies(sems)
    need = dma.start(blocks_in(pays, p_ref, blk) + mix_out_copies(idx_ref, os, wo_ref))
    by_block = [
        dma.start([(pre_in.at[k], pre_ref.at[k]), (h_in.at[k], h_ref.at[k])]) for k in range(4)
    ]
    need2 = dma.start([(dk_in, dk_ref), (kr_in, kr_ref)])
    need3 = dma.start(blocks_in(xs, x_ref, blk) + mix_in_copies(idx_ref, ps, w_ref))
    wait_all(need)
    gm = gm_ref[...]
    ggm_ref[...] = jnp.zeros_like(ggm_ref)

    for k in range(4):
        rel = pl.ds(k * blk, blk)
        back = mm_bt(p_ref[rel, 0:width], wo_ref[...])
        wait_all(by_block[k])
        kappa = lanesum(p_ref[rel, width:])
        gs = sigm(pre_ref[k, :, 3 * ch : 5 * ch].astype(F32))
        h = h_ref[k]
        gated = h * gs
        u_ref[rel, :] = (gated * gm).astype(BF)
        ggm_ref[...] += jnp.sum(back * gated, axis=0, keepdims=True)
        d = (back * gm - gated * kappa) * gs
        dir_ref[k] = d
        g_ref[rel, 3 * ch : 5 * ch] = (d * h * (1.0 - gs)).astype(BF)

    wait_all(need2)
    gph_ref[...] = jnp.zeros_like(gph_ref)
    cos = cos_ref[...][None]
    sin = sin_ref[...][None]
    zero = jnp.zeros((4, 8, ch), F32)

    def load(i):
        rows = rows_of(i, 8)
        return dk_ref[:, rows, :], dir_ref[:, rows, 0:ch], dir_ref[:, rows, ch : 2 * ch]

    def first_pass(j, st):
        fa, fb, prod = st
        d, da, db = load(n - 1 - j)
        ga = da + fa
        gb = db + fb
        return d * (cos * ga + sin * gb), d * (cos * gb - sin * ga), prod * d

    fa, fb, prod = lax.fori_loop(0, n, first_pass, (zero, zero, zero + 1.0), unroll=4)
    end_ref[:, :, 0:ch] = fa
    end_ref[:, :, ch : 2 * ch] = fb
    prod_ref[...] = prod
    cn, sn = rot_power(cos_ref[...], sin_ref[...], n)
    combine_segments(s, (3, 2, 1, 0), end_ref, prod_ref, init_ref, ch, cn, -sn)

    def second_pass(j, st):
        fa, fb = st
        i = n - 1 - j
        d, da, db = load(i)
        rows = rows_of(i, 8)
        ga = da + fa
        gb = db + fb
        dir_ref[:, rows, 0:ch] = ga
        dir_ref[:, rows, ch : 2 * ch] = gb
        return d * (cos * ga + sin * gb), d * (cos * gb - sin * ga)

    lax.fori_loop(
        0, n, second_pass, (init_ref[:, :, 0:ch], init_ref[:, :, ch : 2 * ch]), unroll=4
    )
    lb = lb_ref[...]

    def grads(k, carry):
        rel = rows_of(k, blk)
        ga = dir_ref[k, :, 0:ch]
        gb = dir_ref[k, :, ch : 2 * ch]
        ra = kr_ref[k, :, 0:ch]
        rb = kr_ref[k, :, ch : 2 * ch]
        a = pre_ref[k, :, 0:ch].astype(F32)
        b = pre_ref[k, :, ch : 2 * ch].astype(F32)
        sf = sigm(pre_ref[k, :, 2 * ch : 3 * ch].astype(F32))
        sa = sigm(a)
        sb = sigm(b)
        om = (1.0 - lb) * (1.0 - sf)
        gdec = ga * ra + gb * rb - (ga * a * sa + gb * b * sb)
        gph_ref[...] += jnp.sum(dk_ref[k] * (gb * ra - ga * rb), axis=0, keepdims=True)
        g_ref[rel, 0:ch] = (ga * (sa * (1.0 + a * (1.0 - sa))) * om).astype(BF)
        g_ref[rel, ch : 2 * ch] = (gb * (sb * (1.0 + b * (1.0 - sb))) * om).astype(BF)
        g_ref[rel, 2 * ch : 3 * ch] = (gdec * om * sf).astype(BF)
        return carry

    lax.fori_loop(0, 4, grads, 0)
    wait_all(need3)

    def emit(k):
        return mm_bt(g_ref[rows_of(k, blk), :], w_ref[...])

    sout_ref[0] = emit(1).astype(BF)
    sout_ref[1] = emit(3).astype(BF)
    saved = dma.start([(sout_ref, s_out)])
    k1_ref[...] = emit(2).astype(BF)
    k0_ref[...] = emit(0).astype(BF)
    saved += dma.start([(k1_ref, k1_out), (k0_ref, k0_out)])

    g1 = g1_ref[...]

    def gain(k, carry):
        rel = rows_of(k, blk)
        x_ref[rel, :] = (x_ref[rel, :].astype(F32) * g1).astype(BF)
        return carry

    lax.fori_loop(0, 4, gain, 0)
    first = idx_ref[1] == 0
    outs = ((own_ref, s0_ref), (e1_ref, s1_ref), (e2_ref, s2_ref), (e3_ref, s3_ref))
    targets = ((own_out, s0_out), (e1_out, s1_out), (e2_out, s2_out), (e3_out, s3_out))
    half = own_ref.shape[0]
    for kk in (2, 1, 3, 0):
        zz = (idx_ref[3] + kk) & 3
        v = mm_at(x_ref[:, rows_of(zz, 2 * half)], g_ref[...])
        lo, hi = v[0:half, :], v[half:, :]
        put_parts(
            kk, jnp.where(first, lo, hi), jnp.where(first, hi, lo), outs,
            (slice(None), pl.ds(0, 5 * ch)),
        )
        u = u_ref[:, rows_of((zz >> 1) ^ idx_ref[2], ch)]
        lo = mm_at(u, p_ref[:, rows_of(zz & 1, ch)])
        hi = mm_at(u, p_ref[:, rows_of(2 + (zz & 1), ch)])
        keep, send = jnp.where(first, lo, hi), jnp.where(first, hi, lo)
        for j in range(2):
            rows = slice(j * half, (j + 1) * half)
            put_parts(
                kk, keep[rows], send[rows], outs, (slice(None), pl.ds((5 + j) * ch, ch)),
            )
        saved += dma.start(list(zip(outs[kk], targets[kk])))
    wait_all(saved)


def gin_body(own_ref, got_ref, ry_ref, x_ref, gres_ref, g1_ref, out_ref, gg1_ref):
    gn = own_ref[...].astype(F32) + got_ref[0].astype(F32) + ry_ref[...].astype(F32)
    x = x_ref[...].astype(F32)
    sc = lax.rsqrt(jnp.mean(x * x, axis=1, keepdims=True) + EPS)
    first = x * sc
    gg1_ref[...] = jnp.sum(gn * first, axis=0, keepdims=True)
    nn = gn * g1_ref[...]
    res = gres_ref[...] + sc * (nn - first * jnp.mean(nn * first, axis=1, keepdims=True))
    out_ref[...] = mm(interleave(x.shape[0], True), res.astype(BF)).astype(BF)


def finish_body(idx_ref, m_ref, far_ref, o_in, f_in, gi_ref, go_ref, o_ref, f_ref):
    rows = m_ref.shape[0]
    ch = far_ref.shape[1] // 2
    nat, far = rows_of(idx_ref[2], ch), rows_of(1 - idx_ref[2], ch)
    gi_ref[:, nat] = m_ref[:, 0:ch]
    gi_ref[:, far] = far_ref[:, 0:ch].astype(F32)
    go_ref[:, nat] = m_ref[:, 3 * ch : 4 * ch]
    go_ref[:, far] = far_ref[:, ch:].astype(F32)
    o_ref[0:rows, :] = o_in[:, 0:ch].astype(F32)
    o_ref[rows:, :] = o_in[:, ch:].astype(F32)
    f_ref[...] = f_in[...].astype(F32)


def blockout_body(resid_ref, own_ref, got_ref, ry_ref, out_ref):
    res = resid_ref[...] + own_ref[...].astype(F32) + got_ref[0].astype(F32) + ry_ref[...].astype(F32)
    out_ref[...] = mm(interleave(res.shape[0], True), res.astype(BF)).astype(BF)


def after(value, *deps):
    return lax.optimization_barrier((value, deps))[0]


def seq_gather(v):
    yv = lax.ppermute(v, "seq", YSWAP)
    cv = lax.ppermute(v, "seq", CORE)
    ycv = lax.ppermute(yv, "seq", CORE)
    return [v, cv, yv, ycv]


def seq_scatter(k1, got):
    far = plus(k1, got[1])
    return got, lax.ppermute(far, "seq", YSWAP)


def batch_pieces():
    b = lax.axis_index("batch")
    z, x = b // 2, b % 2
    at = [2 * ((z + 4 - k) % 4) + x for k in range(4)]
    return at + [a ^ 1 for a in at]


def xsend(pack):
    return lax.ppermute(pack, "batch", XSWAP)


def plus(a, b):
    return (a.astype(F32) + b.astype(F32)).astype(BF)


class Scatter:
    def __init__(self, own, kept1, kept3, kept2, s2, s1, s3, s0):
        self.kept = [own, kept1, kept2, kept3]
        self.send = [s0, s1, s2, s3]
        self.got, self.part, self.z = {}, {}, {}

    def along_x(self, kk, *deps):
        self.got[kk] = xsend(after(self.send[kk], *deps) if deps else self.send[kk])

    def add(self, kk, *deps):
        kept = after(self.kept[kk], *deps) if deps else self.kept[kk]
        self.part[kk] = plus(kept, self.got[kk])

    def along_z(self, kk):
        self.z[kk] = lax.ppermute(self.part[kk], "batch", zshift(kk))

    def total(self, *deps):
        out = after(self.kept[0], *deps) + self.got[0].astype(F32)
        for v in self.z.values():
            out = out + v.astype(F32)
        return out


def small_sum(v, *deps):
    v = v + lax.ppermute(v, "seq", CORE)
    v = v + lax.ppermute(v, "seq", YSWAP)
    v = v + lax.ppermute(v, "batch", XSWAP)
    v = after(v, *deps)
    return v + sum(lax.ppermute(v, "batch", zshift(k)) for k in (1, 2, 3))


def per_device(
    block_input, segment_ids, out_cotangent, lower_bound, gain_first, w_input, w_forget,
    w_outgate, phase_angle, gain_mixer, w_output, gain_second, w_gate, w_up, w_down,
):
    s = lax.axis_index("seq")
    b = lax.axis_index("batch")
    y, c = s // 2, s % 2
    z, x = b // 2, b % 2
    nb = lax.axis_size("batch")
    blk, width = block_input.shape[1:]
    tok = 4 * blk
    ch = width // 4
    hu = w_gate.shape[1]
    start = 2 * ch * c + ch * y
    wide = nb == 8
    dma = pltpu.SemaphoreType.DMA
    tail = width + 128
    row8 = width // 8

    far_cols = (1 - y) * ch
    far_src = jnp.concatenate(
        [
            lax.dynamic_slice(w_input, (0, far_cols), (w_input.shape[0], ch)),
            lax.dynamic_slice(w_outgate, (0, far_cols), (w_input.shape[0], ch)),
        ],
        axis=1,
    )
    far = lax.ppermute(far_src, "seq", YSWAP)
    fg = lax.ppermute(w_forget, "seq", FORGET_PERM)
    x_own, xp, cp = call(
        norm1_body, [sds((blk, width), BF)] * 3, [block_input[0], out_cotangent[0]],
        name="norm1",
    )
    pack_f = jnp.concatenate([w_gate.T, w_up.T, w_down], axis=0)
    zero = jnp.zeros((), jnp.int32)
    smem1 = [SMEM] + [VMEM] * 11
    if wide:
        at = batch_pieces()
        brow = [(a // 4) ^ y for a in at]
        bcol = [2 * (a % 2) + (a // 2) % 2 for a in at]
        idx = jnp.stack([s, x, y, z] + at + brow + bcol).astype(jnp.int32)
        moved = lax.ppermute(w_output, ("seq", "batch"), OUT_PERM)
        line = call(
            line_body, [sds((16, 512), BF)],
            [gain_first, gain_second, phase_angle, gain_mixer, segment_ids], room=None,
            name="line",
        )[0]
        line_x = xsend(line)
        pack_m, both = call(
            pack_body, [sds((row8, 7 * ch), BF), sds((16, 512), BF)],
            [idx, w_input, w_outgate, far, fg, moved, line, line_x],
            smem1[:8], room=None, name="pack",
        )
        mz1 = lax.ppermute(pack_m, "batch", zshift(1))
        mx0 = xsend(pack_m)
        mz3 = lax.ppermute(after(pack_m, mz1), "batch", zshift(3))
        mx1 = xsend(after(mz1, mx0))
        mz2 = lax.ppermute(after(pack_m, mz3, mx1), "batch", zshift(2))
        mx3 = xsend(after(mz3, mx1))
        xs = seq_gather(after(x_own, far))
        xs[3] = lax.ppermute(after(xs[2], mx3), "seq", CORE)
        mx2 = xsend(after(mz2, mx1, mx3))
        fz1 = lax.ppermute(after(pack_f, mz2), "batch", zshift(1))
        fz3 = lax.ppermute(after(pack_f, fz1), "batch", zshift(3))
        fx0 = xsend(after(pack_f, mx2))
        half = 3 * hu // 2
        fz2a = lax.ppermute(after(pack_f[0:half], fz3), "batch", zshift(2))
        fz2b = lax.ppermute(after(pack_f[half:], fz2a), "batch", zshift(2))
        fx1 = xsend(after(fz1, fx0))
        fx3 = xsend(after(fz3, fx1))
        fx2a = xsend(after(fz2a, fx3))
        fx2b = xsend(after(fz2b, fx3))
        mixes = [pack_m, mz1, mz2, mz3, mx0, mx1, mx2, mx3]
        ffns = [pack_f, fz1, fz2a, fz3, fx0, fx1, fx2a, fx3, fz2b, fx2b]
        lines = jnp.concatenate(
            [both] + [lax.ppermute(after(both, xs[2]), "batch", zshift(k)) for k in (1, 2, 3)], axis=0
        )
        lines = seq_gather(after(lines, mx3))
        cots = seq_gather(after(cp, lines[2]))
        gain1, gain2, cos, sin, gm, lb, keep = call(
            smalls_body,
            [sds((1, width), F32)] * 2 + [sds((1, ch), F32)] * 2
            + [sds((1, 2 * ch), F32), sds((1, ch), F32), sds((4, blk, 1), F32)],
            [idx, *lines, lower_bound[None]], smem1[:6],
            scratch=[
                pltpu.VMEM((1, width), F32), pltpu.VMEM((1, width), F32),
                pltpu.VMEM((2, 1, width), F32),
            ],
            room=None, name="smalls",
        )
        outs_w = []
    else:
        idx = jnp.stack([s, zero, y, zero] + [zero] * 24).astype(jnp.int32)
        xs = seq_gather(x_own)
        cots = seq_gather(cp)
        nat = lambda w: lax.dynamic_slice(w, (0, y * ch), (w.shape[0], ch))
        mix = [nat(w_input), far[:, 0:ch], fg, nat(w_outgate), far[:, ch:]]
        mixes = [lax.all_gather(jnp.concatenate(mix, axis=1), "batch", axis=0, tiled=True)]
        ffns = [lax.all_gather(pack_f, "batch", axis=1, tiled=True)]
        full = lax.all_gather(w_output, "batch", axis=0, tiled=True)
        full = lax.all_gather(full, "seq", axis=1, tiled=True)
        outs_w = [
            jnp.concatenate(
                [
                    lax.dynamic_slice(full, (y * width + start, 0), (ch, width)),
                    lax.dynamic_slice(full, ((1 - y) * width + start, 0), (ch, width)),
                ],
                axis=0,
            )
        ]
        small = jnp.concatenate(
            [gain_first, gain_second, phase_angle, gain_mixer, segment_ids[0].astype(BF)]
        )
        g1n, gmn = gain_first.shape[0], gain_mixer.shape[0]
        every = lax.all_gather(small, ("seq", "batch"), axis=0).reshape(4, nb, -1)
        gain1 = every[:, :, 0:g1n].reshape(1, width).astype(F32)
        gain2 = every[:, :, g1n : 2 * g1n].reshape(1, width).astype(F32)
        phase = every[:, :, 2 * g1n : 3 * g1n].reshape(1, width).astype(F32)
        gainm = every[:, :, 3 * g1n : 3 * g1n + gmn].reshape(2, width).astype(F32)
        ids = lax.dynamic_index_in_dim(every[:, :, 3 * g1n + gmn :], b, 1, False).reshape(tok)
        keep = jnp.concatenate([jnp.zeros((1,), F32), (ids[1:] == ids[:-1]).astype(F32)])
        keep = jnp.swapaxes(keep.reshape(4, 8, blk // 8), 1, 2).reshape(4, blk)
        keep = jnp.where(c == 1, keep[jnp.array([1, 0, 3, 2])], keep)
        keep = jnp.where(y == 1, keep[jnp.array([2, 3, 0, 1])], keep)[:, :, None]
        phase = lax.dynamic_slice(phase, (0, start), (1, ch))
        cos = jnp.cos(phase)
        sin = jnp.sin(phase) * jnp.where(y == 0, 1.0, -1.0).astype(F32)
        lb = lax.dynamic_slice(lower_bound[None, :], (0, start), (1, ch))
        gm = jnp.concatenate(
            [
                lax.dynamic_slice(gainm, (y, start), (1, ch)),
                lax.dynamic_slice(gainm, (1 - y, start), (1, ch)),
            ],
            axis=1,
        )
    early = [fz1] if wide else []
    pieces = len(mixes)
    fpieces = len(ffns)
    sign = jnp.where(y == 0, 1.0, -1.0).astype(F32)

    scan_scratch = [
        pltpu.VMEM((4, 8, 2 * ch), F32), pltpu.VMEM((4, 8, ch), F32),
        pltpu.VMEM((4, 8, 2 * ch), F32),
    ]
    full_tok = pltpu.VMEM((tok, width), BF)
    big = pltpu.VMEM((4, blk, 2 * ch), F32)
    mix_all = mixes + outs_w
    pre, dk, h, kr, k0, k1, sout = call(
        functools.partial(mixer_fwd_body, pieces=pieces),
        [
            sds((4, blk, 5 * ch), BF), sds((4, blk, ch), F32), sds((4, blk, 2 * ch), F32),
            sds((4, blk, 2 * ch), F32), sds((blk, tail), BF), sds((blk, tail), BF),
            sds((2, blk, tail), BF),
        ],
        [idx, *xs, *mix_all, after(gain1, *early), keep, lb, cos, sin, gm],
        [SMEM] + [HBM] * (4 + len(mix_all)) + [VMEM] * 6,
        [HBM] * 7,
        scratch=[
            full_tok, pltpu.VMEM((width, 5 * ch), BF), pltpu.VMEM((2 * ch, width), BF),
            pltpu.VMEM((4, blk, 5 * ch), BF), pltpu.VMEM((4, blk, ch), F32), big, big,
            pltpu.VMEM((blk, tail), BF), pltpu.VMEM((blk, tail), BF),
            pltpu.VMEM((2, blk, tail), BF), big, big, *scan_scratch, dma((48,)),
        ],
        room=None, flops=2 * tok * width * 7 * ch, name="mixer_fwd",
    )
    if wide:
        sout = after(sout, fz3, fx0, *cots[1:3])
    got, near = seq_scatter(k1, lax.ppermute(sout, "seq", CORE))
    if wide:
        near = after(near, fz2a, fx1, cots[3])
    resid, fin, sc = call(
        functools.partial(resid_body, chans=2.0 * width),
        [sds((blk, width), F32), sds((blk, width), BF), sds((blk, 128), F32)],
        [xp, k0, got, near, gain2], name="resid",
    )
    fins = seq_gather(fin)
    if wide:
        fins[3] = lax.ppermute(after(fins[2], fx2a, fz2b), "seq", CORE)
    scat = [sds((blk, width), BF), sds((blk, width), BF), sds((2, blk, width), BF)]
    scat_v = [pltpu.VMEM(v.shape, v.dtype) for v in scat]
    part_f = sds((3 * hu, row8), BF)
    hid, ggu, k02, k12, sout2, kept2, s2 = call(
        functools.partial(ffn_body, pieces=fpieces),
        [sds((tok, hu), BF), sds((tok, 2 * hu), BF)] + scat + [part_f, part_f],
        [idx, *fins, *cots, *ffns], [SMEM] + [HBM] * (8 + fpieces),
        [HBM] * 7,
        scratch=[
            full_tok, full_tok, pltpu.VMEM((3 * hu, width), BF),
            pltpu.VMEM((tok, hu), BF), pltpu.VMEM((tok, 2 * hu), BF), *scat_v,
            pltpu.VMEM(part_f.shape, BF), pltpu.VMEM(part_f.shape, BF), dma((40,)),
        ],
        room=None, flops=10 * tok * width * hu, name="ffn",
    )

    got2 = lax.ppermute(sout2, "seq", CORE)
    far2 = plus(k12, got2[1])
    near2 = lax.ppermute(far2, "seq", YSWAP)
    own_f, kept1, kept3, s1, s3, s0 = call(
        ffn_grad_body,
        [sds((3 * hu, row8), F32)] + [part_f] * 5,
        [idx, after(hid, far2), ggu, *fins, *cots],
        [SMEM, VMEM, VMEM] + [HBM] * 8, scratch=[full_tok, full_tok, dma((8,))],
        room=None, flops=6 * tok * width * hu, name="ffn_grad",
    )
    fsc = Scatter(own_f, kept1, kept3, kept2, s2, s1, s3, s0)
    first_sum = [s1]
    if wide:
        fsc.along_x(2)
        fsc.add(2, s1)
        fsc.along_z(2)
        fsc.along_x(1, fsc.got[2])
        fsc.along_x(3, fsc.got[1])
        first_sum.append(fsc.part[2])
    gres, pay, gg2 = call(
        functools.partial(gresid_body, chans=2.0 * width),
        [sds((blk, width), F32), sds((blk, tail), BF), sds((1, width), F32)],
        [k02, got2, near2, after(cp, *first_sum), resid, xp, sc, gain2], room=None, name="gresid",
    )
    pays = seq_gather(pay)
    if wide:
        fsc.add(1, pay)
        fsc.along_z(1)
        pays[2] = after(pays[2], fsc.part[1])
        pays[3] = lax.ppermute(pays[2], "seq", CORE)
        fsc.add(3, pays[2])
        fsc.along_z(3)
        fsc.along_x(0, fsc.got[3])
        pays[1] = after(pays[1], fsc.part[3])
    part_m = [sds((row8, 7 * ch), F32)] + [sds((row8, 7 * ch), BF)] * 7
    ggm, gph, *msc, k04, k14, sout4 = call(
        functools.partial(bwd_body, pieces=pieces),
        [sds((1, 2 * ch), F32), sds((1, ch), F32)] + part_m + scat,
        [idx, *pays, *xs, *mix_all, pre, dk, h, kr, lb, cos, sin, gain1, gm],
        [SMEM] + [HBM] * (12 + len(mix_all)) + [VMEM] * 5, [VMEM] * 2 + [HBM] * 11,
        scratch=[
            *[pltpu.VMEM(v.shape, v.dtype) for v in part_m + scat],
            pltpu.VMEM((tok, tail), BF), full_tok, pltpu.VMEM((width, 5 * ch), BF),
            pltpu.VMEM((2 * ch, width), BF), pltpu.VMEM((4, blk, 5 * ch), BF),
            pltpu.VMEM((4, blk, ch), F32), big, big, pltpu.VMEM((tok, 2 * ch), BF),
            pltpu.VMEM((tok, 5 * ch), BF), big, *scan_scratch, dma((64,)),
        ],
        room=None, flops=6 * tok * width * 5 * ch, name="bwd",
    )
    msc = Scatter(*msc)
    if wide:
        msc.along_x(2)
        sout4 = after(sout4, *fsc.z.values(), fsc.got[0])
    got4, near4 = seq_scatter(k14, lax.ppermute(sout4, "seq", CORE))
    if wide:
        msc.add(2)
        msc.along_z(2)
        msc.along_x(1, msc.part[2])
        k04 = after(k04, msc.part[2])
    grad_input, gg1 = call(
        gin_body, [sds((blk, width), BF), sds((1, width), F32)],
        [k04, got4, near4, xp, gres, gain1], room=None, name="gin",
    )
    k03, k13, sout3 = call(
        functools.partial(down_body, pieces=fpieces), scat,
        [idx, after(hid, gg1), *ffns], [SMEM, VMEM] + [HBM] * fpieces,
        scratch=[pltpu.VMEM((hu, width), BF), dma((8,))],
        room=None, flops=2 * tok * width * hu, name="down",
    )
    got3, near3 = seq_scatter(k13, lax.ppermute(sout3, "seq", CORE))
    if wide:
        msc.add(1, gg1)
        msc.along_z(1)
        msc.along_x(3, msc.part[1])
        msc.add(3, sout3, msc.z[2])
        msc.along_z(3)
        msc.along_x(0, msc.part[3])
    block_output = call(
        blockout_body, [sds((blk, width), BF)], [resid, k03, got3, near3], name="blockout",
    )[0]

    if wide:
        g_f3 = fsc.total(msc.part[3])
        g_m = msc.total(near3)
        o_back = lax.ppermute(g_m[:, 5 * ch :].astype(BF), ("seq", "batch"), OUT_BACK)
    else:
        def whole(parts):
            lo = jnp.stack([v.astype(F32) for v in parts.kept])
            hi = jnp.stack([v.astype(F32) for v in parts.send])
            return jnp.stack([lo, hi], axis=1).reshape((8,) + parts.send[0].shape)

        f8 = whole(fsc)
        g_f3 = lax.psum_scatter(
            jnp.swapaxes(f8, 0, 1).reshape(3 * hu, width), "batch", scatter_dimension=1,
            tiled=True,
        )
        m8 = whole(msc)
        g_m = lax.psum_scatter(
            m8[:, :, 0 : 5 * ch].reshape(width, 5 * ch), "batch", scatter_dimension=0, tiled=True
        )
        o8 = m8[:, :, 5 * ch :].reshape(2, 2, 2, row8, 2, ch)
        o_full = jnp.transpose(o8, (0, 4, 3, 2, 1, 5)).reshape(2, ch, width)
        spread = jnp.zeros((2, width, width), F32)
        spread = lax.dynamic_update_slice(spread, o_full, (0, start, 0)).reshape(
            2 * width, width
        )
        g_o = lax.psum_scatter(spread, "batch", scatter_dimension=0, tiled=True)
        g_o = lax.psum_scatter(g_o, "seq", scatter_dimension=1, tiled=True)

    far_back = lax.ppermute(
        jnp.concatenate([g_m[:, ch : 2 * ch], g_m[:, 4 * ch : 5 * ch]], axis=1).astype(BF),
        "seq", YSWAP,
    )
    g_f = lax.ppermute(
        g_m[:, 2 * ch : 3 * ch].astype(BF), "seq", [(d, q2) for q2, d in FORGET_PERM]
    )

    if wide:
        g_in, g_og, g_o, g_f = call(
            finish_body,
            [
                sds((row8, 2 * ch), F32), sds((row8, 2 * ch), F32), sds((2 * row8, ch), F32),
                sds((row8, ch), F32),
            ],
            [idx, g_m, far_back, o_back, g_f], [SMEM] + [VMEM] * 4, name="finish",
        )
    else:
        g_f = g_f.astype(F32)
        far_back = far_back.astype(F32)

        def rejoin(nat, farp):
            return jnp.where(
                y == 0,
                jnp.concatenate([nat, farp], axis=1),
                jnp.concatenate([farp, nat], axis=1),
            )

        g_in = rejoin(g_m[:, 0:ch], far_back[:, 0:ch])
        g_og = rejoin(g_m[:, 3 * ch : 4 * ch], far_back[:, ch:])

    ggm2 = jnp.where(
        y == 0,
        ggm.reshape(2, ch),
        jnp.concatenate([ggm[:, ch:], ggm[:, 0:ch]], axis=0),
    )
    spread_gm = lax.dynamic_update_slice(jnp.zeros((2, width), F32), ggm2, (0, start))
    spread_ph = lax.dynamic_update_slice(jnp.zeros((1, width), F32), gph * sign, (0, start))
    nd = 4 * nb
    vec = jnp.concatenate(
        [
            gg1.reshape(nd, -1), gg2.reshape(nd, -1), spread_ph.reshape(nd, -1),
            spread_gm.reshape(nd, -1),
        ],
        axis=1,
    )
    mine = small_sum(after(vec, sout3), msc.got[0], near3) if wide else lax.psum(vec, ("seq", "batch"))
    mine = lax.dynamic_index_in_dim(mine, s * nb + b, 0, False)
    g1n = gain_first.shape[0]
    gg1o = mine[0:g1n]
    gg2o = mine[g1n : 2 * g1n]
    gpho = mine[2 * g1n : 3 * g1n]
    ggmo = mine[3 * g1n :]
    return (
        block_output[None], grad_input[None], gg1o, g_in, g_f, g_og, gpho, ggmo, g_o, gg2o,
        g_f3[0:hu].T, g_f3[hu : 2 * hu].T, g_f3[2 * hu :],
    )


def solution(mesh):
    both = P(("seq", "batch"))
    mat = P("batch", "seq")
    in_specs = (
        P("batch", "seq", None), P("batch", "seq"), P("batch", "seq", None), P(), both, mat,
        mat, mat, both, both, mat, both, mat, mat, P("seq", "batch"),
    )
    out_specs = (
        P("batch", "seq", None), P("batch", "seq", None), both, mat, mat, mat, both, both, mat,
        both, mat, mat, P("seq", "batch"),
    )
    return jax.shard_map(
        per_device, mesh=mesh, in_specs=in_specs, out_specs=out_specs, check_vma=False
    )
```

```python
import functools
import math

import jax
import jax.numpy as jnp
from jax import lax
from jax.experimental import pallas as pl
from jax.experimental.pallas import tpu as pltpu
from jax.sharding import PartitionSpec as P

EPS = 1e-6
F32 = jnp.float32
BF = jnp.bfloat16
MB = 1024 * 1024

CORE = [(s, s ^ 1) for s in range(4)]
YSWAP = [(s, s ^ 2) for s in range(4)]
XSWAP = [(b, b ^ 1) for b in range(8)]


def zshift(k):
    return [(2 * z + x, 2 * ((z + k) % 4) + x) for z in range(4) for x in range(2)]


def out_block_perm():
    pairs = []
    for s in range(4):
        for b in range(8):
            y, c, part = b & 1, (b >> 1) & 1, b >> 2
            ys, cs = s >> 1, s & 1
            pairs.append((s * 8 + b, (2 * y + c) * 8 + 2 * (2 * part + cs) + ys))
    return pairs


OUT_PERM = out_block_perm()
OUT_BACK = [(d, s) for s, d in OUT_PERM]
FORGET_PERM = [(2 * (d & 1) + (d >> 1), d) for d in range(4)]


def sigm(v):
    return 0.5 * jnp.tanh(0.5 * v) + 0.5


def mm(a, b):
    return jnp.dot(a, b, preferred_element_type=F32)


def mm_bt(a, b):
    return lax.dot_general(a, b, (((1,), (1,)), ((), ())), preferred_element_type=F32)


def mm_at(a, b):
    return lax.dot_general(a, b, (((0,), (0,)), ((), ())), preferred_element_type=F32)


def sds(shape, dtype):
    return jax.ShapeDtypeStruct(shape, dtype)


HBM, SMEM, VMEM = "hbm", "smem", "vmem"


def tiled_bytes(a):
    shape = (1, 1) + tuple(a.shape)
    lanes, rows = -(-shape[-1] // 128) * 128, -(-shape[-2] // 16) * 16
    return math.prod(shape[:-2]) * rows * lanes * jnp.dtype(a.dtype).itemsize


def call(body, outs, args, kinds=None, okinds=None, scratch=(), room=8, flops=0, name=None):
    kinds = kinds or [VMEM] * len(args)
    okinds = okinds or [VMEM] * len(outs)
    held = sum(tiled_bytes(a) for a, k in zip(args, kinds) if k == VMEM)
    held += sum(tiled_bytes(o) for o, k in zip(outs, okinds) if k == VMEM)
    held += sum(tiled_bytes(m) for m in scratch if m.memory_space == pltpu.VMEM)
    vmem = 63 if room is None else -(-held // MB) + room
    space = {HBM: pl.ANY, SMEM: pltpu.SMEM, VMEM: pltpu.VMEM}
    nbytes = sum(a.size * a.dtype.itemsize for a in args)
    nbytes += sum(o.size * o.dtype.itemsize for o in outs)
    return pl.pallas_call(
        body,
        out_shape=outs,
        in_specs=[pl.BlockSpec(memory_space=space[k]) for k in kinds],
        out_specs=[pl.BlockSpec(memory_space=space[k]) for k in okinds],
        scratch_shapes=list(scratch),
        compiler_params=pltpu.CompilerParams(vmem_limit_bytes=vmem * MB),
        cost_estimate=pl.CostEstimate(
            flops=10 * (flops + 3 * 10**8), bytes_accessed=nbytes, transcendentals=0
        ),
        name=name,
    )(*args)


def hilo(col):
    rows = col.shape[0]
    hi = col.astype(BF)
    lo = (col - hi.astype(F32)).astype(BF)
    lane = lax.broadcasted_iota(jnp.int32, (rows, 128), 1)
    hi_b = jnp.broadcast_to(hi.astype(F32), (rows, 128))
    lo_b = jnp.broadcast_to(lo.astype(F32), (rows, 128))
    return jnp.where(lane == 0, hi_b, jnp.where(lane == 1, lo_b, 0.0)).astype(BF)


def lanesum(tile):
    return jnp.sum(tile.astype(F32), axis=1, keepdims=True)


def interleave(blk, back):
    row = lax.broadcasted_iota(jnp.int32, (blk, blk), 0)
    col = lax.broadcasted_iota(jnp.int32, (blk, blk), 1)
    if back:
        row, col = col, row
    hit = col == (row % 8) * (blk // 8) + row // 8
    return jnp.where(hit, 1.0, 0.0).astype(BF)


class Copies:
    def __init__(self, sems):
        self.sems, self.used = sems, 0

    def start(self, pairs):
        made = []
        for src, dst in pairs:
            made.append(pltpu.make_async_copy(src, dst, self.sems.at[self.used]))
            made[-1].start()
            self.used += 1
        return made


def wait_all(made):
    for m in made:
        m.wait()


def rows_of(i, n):
    return pl.ds(pl.multiple_of(i * n, n), n)


def norm1_body(x_ref, c_ref, o_ref, xp_ref, cp_ref):
    perm = interleave(x_ref.shape[0], False)
    x = mm(perm, x_ref[...])
    xp_ref[...] = x.astype(BF)
    cp_ref[...] = mm(perm, c_ref[...]).astype(BF)
    sc = lax.rsqrt(jnp.mean(x * x, axis=1, keepdims=True) + EPS)
    o_ref[...] = (x * sc).astype(BF)


def line_body(g1_ref, g2_ref, ph_ref, gm_ref, id_ref, o_ref):
    line = jnp.concatenate([g1_ref[...], g2_ref[...], ph_ref[...], gm_ref[...]])[None, :]
    line = jnp.concatenate([line.astype(F32), jnp.zeros((1, 256 - line.shape[1]), F32)], axis=1)
    both = jnp.concatenate([id_ref[...].astype(F32), line], axis=1)
    o_ref[...] = jnp.broadcast_to(both, o_ref.shape).astype(BF)


def pack_body(idx_ref, in_ref, og_ref, far_ref, fg_ref, out_ref, l_ref, lx_ref, o_ref, both_ref):
    rows, ch = fg_ref.shape
    nat = rows_of(idx_ref[2], ch)
    o_ref[0:rows, 0:ch] = in_ref[:, nat]
    o_ref[0:rows, ch : 2 * ch] = far_ref[:, 0:ch]
    o_ref[0:rows, 2 * ch : 3 * ch] = fg_ref[...]
    o_ref[0:rows, 3 * ch : 4 * ch] = og_ref[:, nat]
    o_ref[0:rows, 4 * ch : 5 * ch] = far_ref[:, ch:]
    o_ref[0:rows, 5 * ch : 6 * ch] = out_ref[0:rows, :]
    o_ref[0:rows, 6 * ch : 7 * ch] = out_ref[rows:, :]
    top = lax.broadcasted_iota(jnp.int32, l_ref.shape, 0) < 8
    both_ref[...] = jnp.where(top, l_ref[...].astype(F32), lx_ref[...].astype(F32)).astype(BF)


def smalls_body(
    idx_ref, v0, v1, v2, v3, lb_in,
    g1_ref, g2_ref, cos_ref, sin_ref, gm_ref, lb_ref, keep_ref,
    line_ref, ph_ref, gmix_ref,
):
    s, x, y, z = (idx_ref[i] for i in range(4))
    width = g1_ref.shape[1]
    ch = cos_ref.shape[1]
    blk = keep_ref.shape[1]
    vs = [
        jnp.concatenate([v[8 * j : 8 * j + 1, :] for j in range(8)], axis=0)
        for v in (v0, v1, v2, v3)
    ]
    rows = jnp.concatenate([v[:, blk:].astype(F32) for v in vs], axis=0)
    r = lax.broadcasted_iota(jnp.int32, (32, width), 0)
    lane = lax.broadcasted_iota(jnp.int32, (32, width), 1)
    i = r & 7
    piece = 2 * ((z - (i >> 1)) & 3) + jnp.where((i & 1) == 0, x, 1 - x)
    device = ((r >> 3) ^ s) * 8 + piece

    def spread(first, size):
        place = lax.broadcasted_iota(jnp.int32, (256, width), 0) - first
        to = lax.broadcasted_iota(jnp.int32, (256, width), 1) & (size - 1)
        one = jnp.where(place == to, 1.0, 0.0).astype(BF)
        wide = mm(rows.astype(BF), one)
        out = []
        for part in range(32 * size // width):
            mine = (lane + part * width) // size == device
            out.append(jnp.sum(jnp.where(mine, wide, 0.0), axis=0, keepdims=True))
        return out

    g1_ref[...] = spread(0, 32)[0]
    g2_ref[...] = spread(32, 32)[0]
    ph_ref[...] = spread(64, 32)[0]
    both = spread(96, 64)
    gmix_ref[0] = both[0]
    gmix_ref[1] = both[1]
    here = rows_of(2 * (s & 1) + (s >> 1), ch)
    phase = ph_ref[:, here]
    cos_ref[...] = jnp.cos(phase)
    sin_ref[...] = jnp.where(y == 0, 1.0, -1.0) * jnp.sin(phase)
    line_ref[...] = lb_in[...]
    lb_ref[...] = line_ref[:, here]
    gm_ref[:, 0:ch] = gmix_ref[y, :, here]
    gm_ref[:, ch:] = gmix_ref[1 - y, :, here]

    ids = [v[0:1, 0:blk].astype(F32) for v in vs]
    perm = interleave(blk, False)
    first = lax.broadcasted_iota(jnp.int32, (16, blk), 1) == 0
    for k in range(4):
        at = k ^ s
        last = jnp.full((1, 1), -1.0, F32)
        for q in range(4):
            last = jnp.where((q ^ s) == at - 1, ids[q][:, blk - 1 : blk], last)
        mine = jnp.broadcast_to(ids[k], (16, blk))
        before = jnp.where(first, jnp.broadcast_to(last, (16, blk)), pltpu.roll(mine, 1, 1))
        same = jnp.where(mine == before, 1.0, 0.0).astype(BF)
        keep_ref[k] = mm_bt(perm, same)[:, 0:1]


def rot_power(cos, sin, steps):
    n = 1
    while n < steps:
        cos, sin = cos * cos - sin * sin, 2.0 * cos * sin
        n *= 2
    return cos, sin


def combine_segments(s, order, end_ref, prod_ref, init_ref, ch, cn, sn):
    ca = jnp.zeros((1, ch), F32)
    cb = jnp.zeros((1, ch), F32)
    for at in order:
        k = at ^ s
        for j in range(8) if order[0] == 0 else reversed(range(8)):
            init_ref[k, j : j + 1, 0:ch] = ca
            init_ref[k, j : j + 1, ch : 2 * ch] = cb
            pj = prod_ref[k, j : j + 1, :]
            ta = pj * (cn * ca - sn * cb) + end_ref[k, j : j + 1, 0:ch]
            cb = pj * (cn * cb + sn * ca) + end_ref[k, j : j + 1, ch : 2 * ch]
            ca = ta


def blocks_in(refs, dst, blk):
    return [(r, dst.at[rows_of(k, blk)]) for k, r in enumerate(refs)]


def mix_in_copies(idx_ref, pieces, dst):
    cols = dst.shape[1]
    if len(pieces) == 1:
        return [(pieces[0].at[:, pl.ds(0, cols)], dst)]
    rows = dst.shape[0] // 8
    return [
        (p.at[pl.ds(0, rows), pl.ds(0, cols)], dst.at[rows_of(idx_ref[4 + i], rows)])
        for i, p in enumerate(pieces)
    ]


def mix_out_copies(idx_ref, pieces, dst):
    ch = dst.shape[0] // 2
    if len(pieces) == 1:
        return [(pieces[0], dst)]
    half = ch // 2
    out = []
    for i, p in enumerate(pieces):
        for j in range(2):
            rows = pl.ds(pl.multiple_of(idx_ref[12 + i] * ch + j * half, half), half)
            src = p.at[pl.ds(0, half), pl.ds((5 + j) * ch, ch)]
            out.append((src, dst.at[rows, rows_of(idx_ref[20 + i], ch)]))
    return out


def mixer_fwd_body(*refs, pieces):
    idx_ref, *refs = refs
    xs, refs = refs[:4], refs[4:]
    ps, refs = refs[:pieces], refs[pieces:]
    os, refs = (refs[:1], refs[1:]) if pieces == 1 else (ps, refs)
    (
        g1_ref, keep_ref, lb_ref, cos_ref, sin_ref, gm_ref,
        pre_out, dk_out, h_out, kr_out, k0_out, k1_out, s_out,
        x_ref, w_ref, wo_ref, pre_ref, dk_ref, h_ref, kr_ref, k0_ref, k1_ref, sout_ref,
        src_ref, gs_ref, end_ref, prod_ref, init_ref, sems,
    ) = refs
    s = idx_ref[0]
    ch = lb_ref.shape[1]
    blk = dk_ref.shape[1]
    width = wo_ref.shape[1]
    n = blk // 8
    dma = Copies(sems)
    need = dma.start(blocks_in(xs, x_ref, blk) + mix_in_copies(idx_ref, ps, w_ref))
    need_out = dma.start(mix_out_copies(idx_ref, os, wo_ref))
    wait_all(need)

    lb = lb_ref[...]
    g1 = g1_ref[...]
    saved = []
    for k in range(4):
        xg = (x_ref[rows_of(k, blk), :].astype(F32) * g1).astype(BF)
        p = mm(xg, w_ref[...])
        pre_ref[k] = p.astype(BF)
        sig = sigm(p[:, 2 * ch : 3 * ch])
        om = (1.0 - lb) * (1.0 - sig)
        dk_ref[k] = keep_ref[k] * (lb + (1.0 - lb) * sig)
        a = p[:, 0:ch]
        b = p[:, ch : 2 * ch]
        src_ref[k, :, 0:ch] = a * sigm(a) * om
        src_ref[k, :, ch : 2 * ch] = b * sigm(b) * om
        gs_ref[k] = sigm(p[:, 3 * ch : 5 * ch])
        saved += dma.start([(pre_ref.at[k], pre_out.at[k]), (dk_ref.at[k], dk_out.at[k])])

    cos = cos_ref[...][None]
    sin = sin_ref[...][None]
    zero = jnp.zeros((4, 8, ch), F32)

    def load(i):
        rows = rows_of(i, 8)
        return dk_ref[:, rows, :], src_ref[:, rows, 0:ch], src_ref[:, rows, ch : 2 * ch]

    def first_pass(i, st):
        ha, hb, prod = st
        d, sa, sb = load(i)
        ra = cos * ha - sin * hb
        rb = cos * hb + sin * ha
        return d * ra + sa, d * rb + sb, prod * d

    ha, hb, prod = lax.fori_loop(0, n, first_pass, (zero, zero, zero + 1.0), unroll=4)
    end_ref[:, :, 0:ch] = ha
    end_ref[:, :, ch : 2 * ch] = hb
    prod_ref[...] = prod
    cn, sn = rot_power(cos_ref[...], sin_ref[...], n)
    combine_segments(s, (0, 1, 2, 3), end_ref, prod_ref, init_ref, ch, cn, sn)

    def second_pass(i, st):
        ha, hb = st
        d, sa, sb = load(i)
        rows = rows_of(i, 8)
        ra = cos * ha - sin * hb
        rb = cos * hb + sin * ha
        ha = d * ra + sa
        hb = d * rb + sb
        live = d > 0.0
        h_ref[:, rows, 0:ch] = ha
        h_ref[:, rows, ch : 2 * ch] = hb
        kr_ref[:, rows, 0:ch] = jnp.where(live, ra, 0.0)
        kr_ref[:, rows, ch : 2 * ch] = jnp.where(live, rb, 0.0)
        return ha, hb

    lax.fori_loop(
        0, n, second_pass, (init_ref[:, :, 0:ch], init_ref[:, :, ch : 2 * ch]), unroll=4
    )
    saved += dma.start([(h_ref, h_out), (kr_ref, kr_out)])
    wait_all(need_out)
    gm = gm_ref[...]

    def emit(k):
        gated = h_ref[k] * gs_ref[k]
        ss = jnp.sum(gated * gated, axis=1, keepdims=True)
        return mm((gated * gm).astype(BF), wo_ref[...]), hilo(ss)

    for i in range(2):
        v, tail = emit(2 * i + 1)
        sout_ref[i, :, 0:width] = v.astype(BF)
        sout_ref[i, :, width:] = tail
        saved += dma.start([(sout_ref.at[i], s_out.at[i])])
    for k, ref, out in ((2, k1_ref, k1_out), (0, k0_ref, k0_out)):
        v, tail = emit(k)
        ref[:, 0:width] = v.astype(BF)
        ref[:, width:] = tail
        saved += dma.start([(ref, out)])
    wait_all(saved)


def resid_body(x_ref, own_ref, got_ref, ry_ref, g2_ref, resid_ref, fin_ref, sc_ref, *, chans):
    width = x_ref.shape[1]
    tot = own_ref[...].astype(F32) + got_ref[0].astype(F32) + ry_ref[...].astype(F32)
    ss = jnp.sum(tot[:, width:], axis=1, keepdims=True)
    sc = lax.rsqrt(ss / chans + EPS)
    resid = x_ref[...].astype(F32) + sc * tot[:, 0:width]
    resid_ref[...] = resid
    sc2 = lax.rsqrt(jnp.mean(resid * resid, axis=1, keepdims=True) + EPS)
    fin_ref[...] = (resid * sc2 * g2_ref[...]).astype(BF)
    sc_ref[...] = jnp.broadcast_to(sc, sc_ref.shape)


def col_copies(idx_ref, pieces, dst):
    if len(pieces) == 1:
        return [(pieces[0], dst)]
    out = []
    for i, p in enumerate(pieces):
        rows, cols = p.shape
        place = i if i < 8 else 2 if i == 8 else 6
        at = pl.ds(0 if i < 8 else rows, rows)
        out.append((p, dst.at[at, rows_of(idx_ref[4 + place], cols)]))
    return out


def ffn_body(*refs, pieces):
    idx_ref, *refs = refs
    xs, cots, refs = refs[:4], refs[4:8], refs[8:]
    ps, refs = refs[:pieces], refs[pieces:]
    (
        hid_out, ggu_out, k0_out, k1_out, s_out, kept2_out, s2_out,
        x_ref, c_ref, w_ref, hid_ref, ggu_ref, k0_ref, k1_ref, sout_ref, kept2_ref, s2_ref, sems,
    ) = refs
    blk = k0_ref.shape[0]
    hu = hid_ref.shape[1]
    dma = Copies(sems)
    need = dma.start(blocks_in(xs, x_ref, blk) + col_copies(idx_ref, ps, w_ref))
    later = dma.start(blocks_in(cots, c_ref, blk))
    wait_all(need)
    saved = []
    for k in (1, 3, 2, 0):
        rel = pl.ds(k * blk, blk)
        gu = mm_bt(x_ref[rel, :], w_ref[0 : 2 * hu, :])
        wait_all(later)
        later = []
        gh = mm_bt(c_ref[rel, :], w_ref[2 * hu :, :])
        g = gu[:, 0:hu]
        u = gu[:, hu : 2 * hu]
        sg = sigm(g)
        q = g * sg
        hid_ref[rel, :] = (q * u).astype(BF)
        dg = gh * (u * (sg + q * (1.0 - sg)))
        both = jnp.concatenate([dg, gh * q], axis=1).astype(BF)
        ggu_ref[rel, :] = both
        saved += dma.start(
            [(hid_ref.at[rel], hid_out.at[rel]), (ggu_ref.at[rel], ggu_out.at[rel])]
        )
        back = mm(both, w_ref[0 : 2 * hu, :])
        if k in (1, 3):
            sout_ref[k // 2] = back.astype(BF)
            saved += dma.start([(sout_ref.at[k // 2], s_out.at[k // 2])])
        else:
            ref, out = (k1_ref, k1_out) if k == 2 else (k0_ref, k0_out)
            ref[...] = back.astype(BF)
            saved += dma.start([(ref, out)])
    ffn_grad_part(idx_ref, 2, ggu_ref, hid_ref, x_ref, c_ref, kept2_ref, s2_ref)
    wait_all(saved + dma.start([(kept2_ref, kept2_out), (s2_ref, s2_out)]))


def down_body(*refs, pieces):
    idx_ref, h_ref, *refs = refs
    ps, refs = refs[:pieces], refs[pieces:]
    k0_ref, k1_ref, sout_ref, wd_ref, sems = refs
    blk = k0_ref.shape[0]
    hu = h_ref.shape[1]
    if pieces > 1:
        last = {2: ps[8], 6: ps[9]}
        ps = [last.get(i, p) for i, p in enumerate(ps[:8])]
    ps = [p.at[pl.ds(p.shape[0] - hu, hu)] for p in ps]
    wait_all(Copies(sems).start(col_copies(idx_ref, ps, wd_ref)))

    def emit(k):
        return mm(h_ref[rows_of(k, blk), :], wd_ref[...])

    sout_ref[0] = emit(1).astype(BF)
    sout_ref[1] = emit(3).astype(BF)
    k1_ref[...] = emit(2).astype(BF)
    k0_ref[...] = emit(0).astype(BF)


def put_parts(kk, keep, send, outs, where):
    kept_ref, send_ref = outs[kk]
    kept_ref[where] = keep.astype(kept_ref.dtype)
    send_ref[where] = send.astype(BF)


def ffn_grad_part(idx_ref, kk, g_ref, h_ref, x_ref, c_ref, keep_ref, send_ref):
    first = idx_ref[1] == 0
    hu = h_ref.shape[1]
    cols = rows_of((idx_ref[3] + kk) & 3, 256)
    for src, left, at, size in ((x_ref, g_ref, 0, 2 * hu), (c_ref, h_ref, 2 * hu, hu)):
        v = mm_at(left[...], src[:, cols])
        lo, hi = v[:, 0:128], v[:, 128:256]
        where = pl.ds(at, size)
        keep_ref[where, :] = jnp.where(first, lo, hi).astype(keep_ref.dtype)
        send_ref[where, :] = jnp.where(first, hi, lo).astype(send_ref.dtype)


def ffn_grad_body(
    idx_ref, h_ref, g_ref, x0, x1, x2, x3, c0, c1, c2, c3,
    own_ref, k1_ref, k3_ref, s1_ref, s3_ref, s0_ref, x_ref, c_ref, sems,
):
    blk = x_ref.shape[0] // 4
    dma = Copies(sems)
    need = dma.start(blocks_in((x0, x1, x2, x3), x_ref, blk))
    need += dma.start(blocks_in((c0, c1, c2, c3), c_ref, blk))
    wait_all(need)
    for kk, keep, send in (
        (1, k1_ref, s1_ref), (3, k3_ref, s3_ref), (0, own_ref, s0_ref),
    ):
        ffn_grad_part(idx_ref, kk, g_ref, h_ref, x_ref, c_ref, keep, send)


def gresid_body(
    own_ref, got_ref, ry_ref, c_ref, resid_ref, x_ref, sc_ref, g2_ref,
    gres_ref, pay_ref, gg2_ref, *, chans,
):
    width = x_ref.shape[1]
    gfi = own_ref[...].astype(F32) + got_ref[0].astype(F32) + ry_ref[...].astype(F32)
    resid = resid_ref[...]
    sc2 = lax.rsqrt(jnp.mean(resid * resid, axis=1, keepdims=True) + EPS)
    second = resid * sc2
    @pl.when(pl.program_id(0) == 0)
    def _():
        gg2_ref[...] = jnp.zeros_like(gg2_ref)

    gg2_ref[...] += jnp.sum(gfi * second, axis=0, keepdims=True)
    g = gfi * g2_ref[...]
    gres = c_ref[...].astype(F32) + sc2 * (
        g - second * jnp.mean(g * second, axis=1, keepdims=True)
    )
    gres_ref[...] = gres
    sc = sc_ref[:, 0:1]
    branch = resid - x_ref[...].astype(F32)
    kappa = sc * sc * (jnp.sum(gres * branch, axis=1, keepdims=True) / chans)
    pay_ref[:, 0:width] = (gres * sc).astype(BF)
    pay_ref[:, width:] = hilo(kappa)


def bwd_body(*refs, pieces):
    idx_ref, *refs = refs
    pays, xs, refs = refs[:4], refs[4:8], refs[8:]
    ps, refs = refs[:pieces], refs[pieces:]
    os, refs = (refs[:1], refs[1:]) if pieces == 1 else (ps, refs)
    (
        pre_in, dk_in, h_in, kr_in, lb_ref, cos_ref, sin_ref, g1_ref, gm_ref,
        ggm_ref, gph_ref, own_out, e1_out, e3_out, e2_out, s2_out, s1_out, s3_out, s0_out,
        k0_out, k1_out, s_out,
        own_ref, e1_ref, e3_ref, e2_ref, s2_ref, s1_ref, s3_ref, s0_ref,
        k0_ref, k1_ref, sout_ref,
        p_ref, x_ref, w_ref, wo_ref, pre_ref, dk_ref, h_ref, kr_ref, u_ref, g_ref, dir_ref,
        end_ref, prod_ref, init_ref, sems,
    ) = refs
    s = idx_ref[0]
    ch = lb_ref.shape[1]
    blk = dk_ref.shape[1]
    n = blk // 8
    width = wo_ref.shape[1]
    dma = Copies(sems)
    need = dma.start(blocks_in(pays, p_ref, blk) + mix_out_copies(idx_ref, os, wo_ref))
    by_block = [
        dma.start([(pre_in.at[k], pre_ref.at[k]), (h_in.at[k], h_ref.at[k])]) for k in range(4)
    ]
    need2 = dma.start([(dk_in, dk_ref), (kr_in, kr_ref)])
    need3 = dma.start(blocks_in(xs, x_ref, blk) + mix_in_copies(idx_ref, ps, w_ref))
    wait_all(need)
    gm = gm_ref[...]
    ggm_ref[...] = jnp.zeros_like(ggm_ref)

    for k in range(4):
        rel = pl.ds(k * blk, blk)
        back = mm_bt(p_ref[rel, 0:width], wo_ref[...])
        wait_all(by_block[k])
        kappa = lanesum(p_ref[rel, width:])
        gs = sigm(pre_ref[k, :, 3 * ch : 5 * ch].astype(F32))
        h = h_ref[k]
        gated = h * gs
        u_ref[rel, :] = (gated * gm).astype(BF)
        ggm_ref[...] += jnp.sum(back * gated, axis=0, keepdims=True)
        d = (back * gm - gated * kappa) * gs
        dir_ref[k] = d
        g_ref[rel, 3 * ch : 5 * ch] = (d * h * (1.0 - gs)).astype(BF)

    wait_all(need2)
    gph_ref[...] = jnp.zeros_like(gph_ref)
    cos = cos_ref[...][None]
    sin = sin_ref[...][None]
    zero = jnp.zeros((4, 8, ch), F32)

    def load(i):
        rows = rows_of(i, 8)
        return dk_ref[:, rows, :], dir_ref[:, rows, 0:ch], dir_ref[:, rows, ch : 2 * ch]

    def first_pass(j, st):
        fa, fb, prod = st
        d, da, db = load(n - 1 - j)
        ga = da + fa
        gb = db + fb
        return d * (cos * ga + sin * gb), d * (cos * gb - sin * ga), prod * d

    fa, fb, prod = lax.fori_loop(0, n, first_pass, (zero, zero, zero + 1.0), unroll=4)
    end_ref[:, :, 0:ch] = fa
    end_ref[:, :, ch : 2 * ch] = fb
    prod_ref[...] = prod
    cn, sn = rot_power(cos_ref[...], sin_ref[...], n)
    combine_segments(s, (3, 2, 1, 0), end_ref, prod_ref, init_ref, ch, cn, -sn)

    def second_pass(j, st):
        fa, fb = st
        i = n - 1 - j
        d, da, db = load(i)
        rows = rows_of(i, 8)
        ga = da + fa
        gb = db + fb
        dir_ref[:, rows, 0:ch] = ga
        dir_ref[:, rows, ch : 2 * ch] = gb
        return d * (cos * ga + sin * gb), d * (cos * gb - sin * ga)

    lax.fori_loop(
        0, n, second_pass, (init_ref[:, :, 0:ch], init_ref[:, :, ch : 2 * ch]), unroll=4
    )
    lb = lb_ref[...]

    def grads(k, carry):
        rel = rows_of(k, blk)
        ga = dir_ref[k, :, 0:ch]
        gb = dir_ref[k, :, ch : 2 * ch]
        ra = kr_ref[k, :, 0:ch]
        rb = kr_ref[k, :, ch : 2 * ch]
        a = pre_ref[k, :, 0:ch].astype(F32)
        b = pre_ref[k, :, ch : 2 * ch].astype(F32)
        sf = sigm(pre_ref[k, :, 2 * ch : 3 * ch].astype(F32))
        sa = sigm(a)
        sb = sigm(b)
        om = (1.0 - lb) * (1.0 - sf)
        gdec = ga * ra + gb * rb - (ga * a * sa + gb * b * sb)
        gph_ref[...] += jnp.sum(dk_ref[k] * (gb * ra - ga * rb), axis=0, keepdims=True)
        g_ref[rel, 0:ch] = (ga * (sa * (1.0 + a * (1.0 - sa))) * om).astype(BF)
        g_ref[rel, ch : 2 * ch] = (gb * (sb * (1.0 + b * (1.0 - sb))) * om).astype(BF)
        g_ref[rel, 2 * ch : 3 * ch] = (gdec * om * sf).astype(BF)
        return carry

    lax.fori_loop(0, 4, grads, 0)
    wait_all(need3)

    def emit(k):
        return mm_bt(g_ref[rows_of(k, blk), :], w_ref[...])

    sout_ref[0] = emit(1).astype(BF)
    sout_ref[1] = emit(3).astype(BF)
    saved = dma.start([(sout_ref, s_out)])
    k1_ref[...] = emit(2).astype(BF)
    k0_ref[...] = emit(0).astype(BF)
    saved += dma.start([(k1_ref, k1_out), (k0_ref, k0_out)])

    g1 = g1_ref[...]

    def gain(k, carry):
        rel = rows_of(k, blk)
        x_ref[rel, :] = (x_ref[rel, :].astype(F32) * g1).astype(BF)
        return carry

    lax.fori_loop(0, 4, gain, 0)
    first = idx_ref[1] == 0
    outs = ((own_ref, s0_ref), (e1_ref, s1_ref), (e2_ref, s2_ref), (e3_ref, s3_ref))
    targets = ((own_out, s0_out), (e1_out, s1_out), (e2_out, s2_out), (e3_out, s3_out))
    half = own_ref.shape[0]
    for kk in (2, 1, 3, 0):
        zz = (idx_ref[3] + kk) & 3
        v = mm_at(x_ref[:, rows_of(zz, 2 * half)], g_ref[...])
        lo, hi = v[0:half, :], v[half:, :]
        put_parts(
            kk, jnp.where(first, lo, hi), jnp.where(first, hi, lo), outs,
            (slice(None), pl.ds(0, 5 * ch)),
        )
        u = u_ref[:, rows_of((zz >> 1) ^ idx_ref[2], ch)]
        lo = mm_at(u, p_ref[:, rows_of(zz & 1, ch)])
        hi = mm_at(u, p_ref[:, rows_of(2 + (zz & 1), ch)])
        keep, send = jnp.where(first, lo, hi), jnp.where(first, hi, lo)
        for j in range(2):
            rows = slice(j * half, (j + 1) * half)
            put_parts(
                kk, keep[rows], send[rows], outs, (slice(None), pl.ds((5 + j) * ch, ch)),
            )
        saved += dma.start(list(zip(outs[kk], targets[kk])))
    wait_all(saved)


def gin_body(own_ref, got_ref, ry_ref, x_ref, gres_ref, g1_ref, out_ref, gg1_ref):
    gn = own_ref[...].astype(F32) + got_ref[0].astype(F32) + ry_ref[...].astype(F32)
    x = x_ref[...].astype(F32)
    sc = lax.rsqrt(jnp.mean(x * x, axis=1, keepdims=True) + EPS)
    first = x * sc
    gg1_ref[...] = jnp.sum(gn * first, axis=0, keepdims=True)
    nn = gn * g1_ref[...]
    res = gres_ref[...] + sc * (nn - first * jnp.mean(nn * first, axis=1, keepdims=True))
    out_ref[...] = mm(interleave(x.shape[0], True), res.astype(BF)).astype(BF)


def finish_body(idx_ref, m_ref, far_ref, o_in, f_in, gi_ref, go_ref, o_ref, f_ref):
    rows = m_ref.shape[0]
    ch = far_ref.shape[1] // 2
    nat, far = rows_of(idx_ref[2], ch), rows_of(1 - idx_ref[2], ch)
    gi_ref[:, nat] = m_ref[:, 0:ch]
    gi_ref[:, far] = far_ref[:, 0:ch].astype(F32)
    go_ref[:, nat] = m_ref[:, 3 * ch : 4 * ch]
    go_ref[:, far] = far_ref[:, ch:].astype(F32)
    o_ref[0:rows, :] = o_in[:, 0:ch].astype(F32)
    o_ref[rows:, :] = o_in[:, ch:].astype(F32)
    f_ref[...] = f_in[...].astype(F32)


def blockout_body(resid_ref, own_ref, got_ref, ry_ref, out_ref):
    res = resid_ref[...] + own_ref[...].astype(F32) + got_ref[0].astype(F32) + ry_ref[...].astype(F32)
    out_ref[...] = mm(interleave(res.shape[0], True), res.astype(BF)).astype(BF)


def after(value, *deps):
    return lax.optimization_barrier((value, deps))[0]


def seq_gather(v):
    yv = lax.ppermute(v, "seq", YSWAP)
    cv = lax.ppermute(v, "seq", CORE)
    ycv = lax.ppermute(yv, "seq", CORE)
    return [v, cv, yv, ycv]


def seq_scatter(k1, got):
    far = plus(k1, got[1])
    return got, lax.ppermute(far, "seq", YSWAP)


def batch_pieces():
    b = lax.axis_index("batch")
    z, x = b // 2, b % 2
    at = [2 * ((z + 4 - k) % 4) + x for k in range(4)]
    return at + [a ^ 1 for a in at]


def xsend(pack):
    return lax.ppermute(pack, "batch", XSWAP)


def plus(a, b):
    return (a.astype(F32) + b.astype(F32)).astype(BF)


class Scatter:
    def __init__(self, own, kept1, kept3, kept2, s2, s1, s3, s0):
        self.kept = [own, kept1, kept2, kept3]
        self.send = [s0, s1, s2, s3]
        self.got, self.part, self.z = {}, {}, {}

    def along_x(self, kk, *deps):
        self.got[kk] = xsend(after(self.send[kk], *deps) if deps else self.send[kk])

    def add(self, kk, *deps):
        kept = after(self.kept[kk], *deps) if deps else self.kept[kk]
        self.part[kk] = plus(kept, self.got[kk])

    def along_z(self, kk, *deps):
        part = after(self.part[kk], *deps) if deps else self.part[kk]
        self.z[kk] = lax.ppermute(part, "batch", zshift(kk))

    def total(self, *deps):
        out = after(self.kept[0], *deps) + self.got[0].astype(F32)
        for v in self.z.values():
            out = out + v.astype(F32)
        return out


def small_sum(v, *deps):
    v = v + lax.ppermute(v, "seq", CORE)
    v = v + lax.ppermute(v, "seq", YSWAP)
    v = v + lax.ppermute(v, "batch", XSWAP)
    v = after(v, *deps)
    return v + sum(lax.ppermute(v, "batch", zshift(k)) for k in (1, 2, 3))


def per_device(
    block_input, segment_ids, out_cotangent, lower_bound, gain_first, w_input, w_forget,
    w_outgate, phase_angle, gain_mixer, w_output, gain_second, w_gate, w_up, w_down,
):
    s = lax.axis_index("seq")
    b = lax.axis_index("batch")
    y, c = s // 2, s % 2
    z, x = b // 2, b % 2
    nb = lax.axis_size("batch")
    blk, width = block_input.shape[1:]
    tok = 4 * blk
    ch = width // 4
    hu = w_gate.shape[1]
    start = 2 * ch * c + ch * y
    wide = nb == 8
    dma = pltpu.SemaphoreType.DMA
    tail = width + 128
    row8 = width // 8

    far_cols = (1 - y) * ch
    far_src = jnp.concatenate(
        [
            lax.dynamic_slice(w_input, (0, far_cols), (w_input.shape[0], ch)),
            lax.dynamic_slice(w_outgate, (0, far_cols), (w_input.shape[0], ch)),
        ],
        axis=1,
    )
    far = lax.ppermute(far_src, "seq", YSWAP)
    fg = lax.ppermute(w_forget, "seq", FORGET_PERM)
    x_own, xp, cp = call(
        norm1_body, [sds((blk, width), BF)] * 3, [block_input[0], out_cotangent[0]],
        name="norm1",
    )
    pack_f = jnp.concatenate([w_gate.T, w_up.T, w_down], axis=0)
    zero = jnp.zeros((), jnp.int32)
    smem1 = [SMEM] + [VMEM] * 11
    if wide:
        at = batch_pieces()
        brow = [(a // 4) ^ y for a in at]
        bcol = [2 * (a % 2) + (a // 2) % 2 for a in at]
        idx = jnp.stack([s, x, y, z] + at + brow + bcol).astype(jnp.int32)
        moved = lax.ppermute(w_output, ("seq", "batch"), OUT_PERM)
        line = call(
            line_body, [sds((16, 512), BF)],
            [gain_first, gain_second, phase_angle, gain_mixer, segment_ids], room=None,
            name="line",
        )[0]
        line_x = xsend(line)
        pack_m, both = call(
            pack_body, [sds((row8, 7 * ch), BF), sds((16, 512), BF)],
            [idx, w_input, w_outgate, far, fg, moved, line, line_x],
            smem1[:8], room=None, name="pack",
        )
        mz1 = lax.ppermute(pack_m, "batch", zshift(1))
        mx0 = xsend(pack_m)
        mz3 = lax.ppermute(after(pack_m, mz1), "batch", zshift(3))
        mx1 = xsend(after(mz1, mx0))
        mz2 = lax.ppermute(after(pack_m, mz3, mx1), "batch", zshift(2))
        mx3 = xsend(after(mz3, mx1))
        xs = seq_gather(after(x_own, far))
        xs[3] = lax.ppermute(after(xs[2], mx3), "seq", CORE)
        mx2 = xsend(after(mz2, mx1, mx3))
        fz1 = lax.ppermute(after(pack_f, mz2), "batch", zshift(1))
        fz3 = lax.ppermute(after(pack_f, fz1), "batch", zshift(3))
        fx0 = xsend(after(pack_f, mx2))
        half = 3 * hu // 2
        fz2a = lax.ppermute(after(pack_f[0:half], fz3), "batch", zshift(2))
        fz2b = lax.ppermute(after(pack_f[half:], fz2a), "batch", zshift(2))
        fx1 = xsend(after(fz1, fx0))
        fx3 = xsend(after(fz3, fx1))
        fx2a = xsend(after(fz2a, fx3))
        fx2b = xsend(after(fz2b, fx3))
        mixes = [pack_m, mz1, mz2, mz3, mx0, mx1, mx2, mx3]
        ffns = [pack_f, fz1, fz2a, fz3, fx0, fx1, fx2a, fx3, fz2b, fx2b]
        lines = jnp.concatenate(
            [both] + [lax.ppermute(after(both, xs[2]), "batch", zshift(k)) for k in (1, 2, 3)], axis=0
        )
        lines = seq_gather(after(lines, mx3))
        cots = seq_gather(after(cp, lines[2]))
        gain1, gain2, cos, sin, gm, lb, keep = call(
            smalls_body,
            [sds((1, width), F32)] * 2 + [sds((1, ch), F32)] * 2
            + [sds((1, 2 * ch), F32), sds((1, ch), F32), sds((4, blk, 1), F32)],
            [idx, *lines, lower_bound[None]], smem1[:6],
            scratch=[
                pltpu.VMEM((1, width), F32), pltpu.VMEM((1, width), F32),
                pltpu.VMEM((2, 1, width), F32),
            ],
            room=None, name="smalls",
        )
        outs_w = []
    else:
        idx = jnp.stack([s, zero, y, zero] + [zero] * 24).astype(jnp.int32)
        xs = seq_gather(x_own)
        cots = seq_gather(cp)
        nat = lambda w: lax.dynamic_slice(w, (0, y * ch), (w.shape[0], ch))
        mix = [nat(w_input), far[:, 0:ch], fg, nat(w_outgate), far[:, ch:]]
        mixes = [lax.all_gather(jnp.concatenate(mix, axis=1), "batch", axis=0, tiled=True)]
        ffns = [lax.all_gather(pack_f, "batch", axis=1, tiled=True)]
        full = lax.all_gather(w_output, "batch", axis=0, tiled=True)
        full = lax.all_gather(full, "seq", axis=1, tiled=True)
        outs_w = [
            jnp.concatenate(
                [
                    lax.dynamic_slice(full, (y * width + start, 0), (ch, width)),
                    lax.dynamic_slice(full, ((1 - y) * width + start, 0), (ch, width)),
                ],
                axis=0,
            )
        ]
        small = jnp.concatenate(
            [gain_first, gain_second, phase_angle, gain_mixer, segment_ids[0].astype(BF)]
        )
        g1n, gmn = gain_first.shape[0], gain_mixer.shape[0]
        every = lax.all_gather(small, ("seq", "batch"), axis=0).reshape(4, nb, -1)
        gain1 = every[:, :, 0:g1n].reshape(1, width).astype(F32)
        gain2 = every[:, :, g1n : 2 * g1n].reshape(1, width).astype(F32)
        phase = every[:, :, 2 * g1n : 3 * g1n].reshape(1, width).astype(F32)
        gainm = every[:, :, 3 * g1n : 3 * g1n + gmn].reshape(2, width).astype(F32)
        ids = lax.dynamic_index_in_dim(every[:, :, 3 * g1n + gmn :], b, 1, False).reshape(tok)
        keep = jnp.concatenate([jnp.zeros((1,), F32), (ids[1:] == ids[:-1]).astype(F32)])
        keep = jnp.swapaxes(keep.reshape(4, 8, blk // 8), 1, 2).reshape(4, blk)
        keep = jnp.where(c == 1, keep[jnp.array([1, 0, 3, 2])], keep)
        keep = jnp.where(y == 1, keep[jnp.array([2, 3, 0, 1])], keep)[:, :, None]
        phase = lax.dynamic_slice(phase, (0, start), (1, ch))
        cos = jnp.cos(phase)
        sin = jnp.sin(phase) * jnp.where(y == 0, 1.0, -1.0).astype(F32)
        lb = lax.dynamic_slice(lower_bound[None, :], (0, start), (1, ch))
        gm = jnp.concatenate(
            [
                lax.dynamic_slice(gainm, (y, start), (1, ch)),
                lax.dynamic_slice(gainm, (1 - y, start), (1, ch)),
            ],
            axis=1,
        )
    early = [fz1] if wide else []
    pieces = len(mixes)
    fpieces = len(ffns)
    sign = jnp.where(y == 0, 1.0, -1.0).astype(F32)

    scan_scratch = [
        pltpu.VMEM((4, 8, 2 * ch), F32), pltpu.VMEM((4, 8, ch), F32),
        pltpu.VMEM((4, 8, 2 * ch), F32),
    ]
    full_tok = pltpu.VMEM((tok, width), BF)
    big = pltpu.VMEM((4, blk, 2 * ch), F32)
    mix_all = mixes + outs_w
    pre, dk, h, kr, k0, k1, sout = call(
        functools.partial(mixer_fwd_body, pieces=pieces),
        [
            sds((4, blk, 5 * ch), BF), sds((4, blk, ch), F32), sds((4, blk, 2 * ch), F32),
            sds((4, blk, 2 * ch), F32), sds((blk, tail), BF), sds((blk, tail), BF),
            sds((2, blk, tail), BF),
        ],
        [idx, *xs, *mix_all, after(gain1, *early), keep, lb, cos, sin, gm],
        [SMEM] + [HBM] * (4 + len(mix_all)) + [VMEM] * 6,
        [HBM] * 7,
        scratch=[
            full_tok, pltpu.VMEM((width, 5 * ch), BF), pltpu.VMEM((2 * ch, width), BF),
            pltpu.VMEM((4, blk, 5 * ch), BF), pltpu.VMEM((4, blk, ch), F32), big, big,
            pltpu.VMEM((blk, tail), BF), pltpu.VMEM((blk, tail), BF),
            pltpu.VMEM((2, blk, tail), BF), big, big, *scan_scratch, dma((48,)),
        ],
        room=None, flops=2 * tok * width * 7 * ch, name="mixer_fwd",
    )
    if wide:
        sout = after(sout, fz3, fx0, *cots[1:3])
    got, near = seq_scatter(k1, lax.ppermute(sout, "seq", CORE))
    if wide:
        near = after(near, fz2a, fx1, cots[3])
    resid, fin, sc = call(
        functools.partial(resid_body, chans=2.0 * width),
        [sds((blk, width), F32), sds((blk, width), BF), sds((blk, 128), F32)],
        [xp, k0, got, near, gain2], name="resid",
    )
    fins = seq_gather(fin)
    if wide:
        fins[3] = lax.ppermute(after(fins[2], fx2a, fz2b), "seq", CORE)
    scat = [sds((blk, width), BF), sds((blk, width), BF), sds((2, blk, width), BF)]
    scat_v = [pltpu.VMEM(v.shape, v.dtype) for v in scat]
    part_f = sds((3 * hu, row8), BF)
    hid, ggu, k02, k12, sout2, kept2, s2 = call(
        functools.partial(ffn_body, pieces=fpieces),
        [sds((tok, hu), BF), sds((tok, 2 * hu), BF)] + scat + [part_f, part_f],
        [idx, *fins, *cots, *ffns], [SMEM] + [HBM] * (8 + fpieces),
        [HBM] * 7,
        scratch=[
            full_tok, full_tok, pltpu.VMEM((3 * hu, width), BF),
            pltpu.VMEM((tok, hu), BF), pltpu.VMEM((tok, 2 * hu), BF), *scat_v,
            pltpu.VMEM(part_f.shape, BF), pltpu.VMEM(part_f.shape, BF), dma((40,)),
        ],
        room=None, flops=10 * tok * width * hu, name="ffn",
    )

    got2 = lax.ppermute(sout2, "seq", CORE)
    far2 = plus(k12, got2[1])
    near2 = lax.ppermute(far2, "seq", YSWAP)
    own_f, kept1, kept3, s1, s3, s0 = call(
        ffn_grad_body,
        [sds((3 * hu, row8), F32)] + [part_f] * 5,
        [idx, after(hid, far2), ggu, *fins, *cots],
        [SMEM, VMEM, VMEM] + [HBM] * 8, scratch=[full_tok, full_tok, dma((8,))],
        room=None, flops=6 * tok * width * hu, name="ffn_grad",
    )
    fsc = Scatter(own_f, kept1, kept3, kept2, s2, s1, s3, s0)
    first_sum = [s1]
    if wide:
        fsc.along_x(2)
        fsc.add(2, s1)
        fsc.along_z(2)
        fsc.along_x(1, fsc.got[2])
        fsc.along_x(3, fsc.got[1])
        first_sum.append(fsc.part[2])
    rows4 = blk // 4
    row = lambda w: pl.BlockSpec((rows4, w), lambda i: (i, 0))
    one = pl.BlockSpec((1, width), lambda i: (0, 0))
    gres, pay, gg2 = pl.pallas_call(
        functools.partial(gresid_body, chans=2.0 * width),
        grid=(4,),
        out_shape=[sds((blk, width), F32), sds((blk, tail), BF), sds((1, width), F32)],
        in_specs=[
            row(width), pl.BlockSpec((1, rows4, width), lambda i: (0, i, 0)), row(width),
            row(width), row(width), row(width), row(128), one,
        ],
        out_specs=[row(width), row(tail), one],
        compiler_params=pltpu.CompilerParams(vmem_limit_bytes=63 * MB),
        cost_estimate=pl.CostEstimate(
            flops=3 * 10**9, bytes_accessed=6 * 10**6, transcendentals=0
        ),
        name="gresid",
    )(k02, got2, near2, after(cp, *first_sum), resid, xp, sc, gain2)
    pays = seq_gather(pay)
    if wide:
        fsc.add(1, pay)
        fsc.along_z(1)
        pays[2] = after(pays[2], fsc.part[1])
        pays[3] = lax.ppermute(pays[2], "seq", CORE)
        fsc.add(3, pays[2])
        fsc.along_x(0, fsc.got[3])
        pays[1] = after(pays[1], fsc.part[3])
    part_m = [sds((row8, 7 * ch), F32)] + [sds((row8, 7 * ch), BF)] * 7
    ggm, gph, *msc, k04, k14, sout4 = call(
        functools.partial(bwd_body, pieces=pieces),
        [sds((1, 2 * ch), F32), sds((1, ch), F32)] + part_m + scat,
        [idx, *pays, *xs, *mix_all, pre, dk, h, kr, lb, cos, sin, gain1, gm],
        [SMEM] + [HBM] * (12 + len(mix_all)) + [VMEM] * 5, [VMEM] * 2 + [HBM] * 11,
        scratch=[
            *[pltpu.VMEM(v.shape, v.dtype) for v in part_m + scat],
            pltpu.VMEM((tok, tail), BF), full_tok, pltpu.VMEM((width, 5 * ch), BF),
            pltpu.VMEM((2 * ch, width), BF), pltpu.VMEM((4, blk, 5 * ch), BF),
            pltpu.VMEM((4, blk, ch), F32), big, big, pltpu.VMEM((tok, 2 * ch), BF),
            pltpu.VMEM((tok, 5 * ch), BF), big, *scan_scratch, dma((64,)),
        ],
        room=None, flops=6 * tok * width * 5 * ch, name="bwd",
    )
    msc = Scatter(*msc)
    if wide:
        msc.along_x(2)
        fsc.along_z(3, ggm)
        sout4 = after(sout4, fsc.z[2], fsc.z[1], fsc.got[0])
    got4, near4 = seq_scatter(k14, lax.ppermute(sout4, "seq", CORE))
    if wide:
        msc.add(2)
        msc.along_z(2)
        msc.along_x(1, msc.part[2])
        k04 = after(k04, msc.part[2])
    grad_input, gg1 = call(
        gin_body, [sds((blk, width), BF), sds((1, width), F32)],
        [k04, got4, near4, xp, gres, gain1], room=None, name="gin",
    )
    k03, k13, sout3 = call(
        functools.partial(down_body, pieces=fpieces), scat,
        [idx, after(hid, gg1, *([fsc.z[3]] if wide else [])), *ffns], [SMEM, VMEM] + [HBM] * fpieces,
        scratch=[pltpu.VMEM((hu, width), BF), dma((8,))],
        room=None, flops=2 * tok * width * hu, name="down",
    )
    got3, near3 = seq_scatter(k13, lax.ppermute(sout3, "seq", CORE))
    if wide:
        msc.add(1, gg1)
        msc.along_z(1)
        msc.along_x(3, msc.part[1])
        msc.add(3, sout3, msc.z[2])
        msc.along_z(3)
        msc.along_x(0, msc.part[3])
    block_output = call(
        blockout_body, [sds((blk, width), BF)], [resid, k03, got3, near3], name="blockout",
    )[0]

    if wide:
        g_f3 = fsc.total(msc.part[3])
        g_m = msc.total(near3)
        o_back = lax.ppermute(g_m[:, 5 * ch :].astype(BF), ("seq", "batch"), OUT_BACK)
    else:
        def whole(parts):
            lo = jnp.stack([v.astype(F32) for v in parts.kept])
            hi = jnp.stack([v.astype(F32) for v in parts.send])
            return jnp.stack([lo, hi], axis=1).reshape((8,) + parts.send[0].shape)

        f8 = whole(fsc)
        g_f3 = lax.psum_scatter(
            jnp.swapaxes(f8, 0, 1).reshape(3 * hu, width), "batch", scatter_dimension=1,
            tiled=True,
        )
        m8 = whole(msc)
        g_m = lax.psum_scatter(
            m8[:, :, 0 : 5 * ch].reshape(width, 5 * ch), "batch", scatter_dimension=0, tiled=True
        )
        o8 = m8[:, :, 5 * ch :].reshape(2, 2, 2, row8, 2, ch)
        o_full = jnp.transpose(o8, (0, 4, 3, 2, 1, 5)).reshape(2, ch, width)
        spread = jnp.zeros((2, width, width), F32)
        spread = lax.dynamic_update_slice(spread, o_full, (0, start, 0)).reshape(
            2 * width, width
        )
        g_o = lax.psum_scatter(spread, "batch", scatter_dimension=0, tiled=True)
        g_o = lax.psum_scatter(g_o, "seq", scatter_dimension=1, tiled=True)

    far_back = lax.ppermute(
        jnp.concatenate([g_m[:, ch : 2 * ch], g_m[:, 4 * ch : 5 * ch]], axis=1).astype(BF),
        "seq", YSWAP,
    )
    g_f = lax.ppermute(
        g_m[:, 2 * ch : 3 * ch].astype(BF), "seq", [(d, q2) for q2, d in FORGET_PERM]
    )

    if wide:
        g_in, g_og, g_o, g_f = call(
            finish_body,
            [
                sds((row8, 2 * ch), F32), sds((row8, 2 * ch), F32), sds((2 * row8, ch), F32),
                sds((row8, ch), F32),
            ],
            [idx, g_m, far_back, o_back, g_f], [SMEM] + [VMEM] * 4, name="finish",
        )
    else:
        g_f = g_f.astype(F32)
        far_back = far_back.astype(F32)

        def rejoin(nat, farp):
            return jnp.where(
                y == 0,
                jnp.concatenate([nat, farp], axis=1),
                jnp.concatenate([farp, nat], axis=1),
            )

        g_in = rejoin(g_m[:, 0:ch], far_back[:, 0:ch])
        g_og = rejoin(g_m[:, 3 * ch : 4 * ch], far_back[:, ch:])

    ggm2 = jnp.where(
        y == 0,
        ggm.reshape(2, ch),
        jnp.concatenate([ggm[:, ch:], ggm[:, 0:ch]], axis=0),
    )
    spread_gm = lax.dynamic_update_slice(jnp.zeros((2, width), F32), ggm2, (0, start))
    spread_ph = lax.dynamic_update_slice(jnp.zeros((1, width), F32), gph * sign, (0, start))
    nd = 4 * nb
    vec = jnp.concatenate(
        [
            gg1.reshape(nd, -1), gg2.reshape(nd, -1), spread_ph.reshape(nd, -1),
            spread_gm.reshape(nd, -1),
        ],
        axis=1,
    )
    mine = small_sum(after(vec, sout3), msc.got[0], near3) if wide else lax.psum(vec, ("seq", "batch"))
    mine = lax.dynamic_index_in_dim(mine, s * nb + b, 0, False)
    g1n = gain_first.shape[0]
    gg1o = mine[0:g1n]
    gg2o = mine[g1n : 2 * g1n]
    gpho = mine[2 * g1n : 3 * g1n]
    ggmo = mine[3 * g1n :]
    return (
        block_output[None], grad_input[None], gg1o, g_in, g_f, g_og, gpho, ggmo, g_o, gg2o,
        g_f3[0:hu].T, g_f3[hu : 2 * hu].T, g_f3[2 * hu :],
    )


def solution(mesh):
    both = P(("seq", "batch"))
    mat = P("batch", "seq")
    in_specs = (
        P("batch", "seq", None), P("batch", "seq"), P("batch", "seq", None), P(), both, mat,
        mat, mat, both, both, mat, both, mat, mat, P("seq", "batch"),
    )
    out_specs = (
        P("batch", "seq", None), P("batch", "seq", None), both, mat, mat, mat, both, both, mat,
        both, mat, mat, P("seq", "batch"),
    )
    return jax.shard_map(
        per_device, mesh=mesh, in_specs=in_specs, out_specs=out_specs, check_vma=False
    )
```

```python
import functools
import math

import jax
import jax.numpy as jnp
from jax import lax
from jax.experimental import pallas as pl
from jax.experimental.pallas import tpu as pltpu
from jax.sharding import PartitionSpec as P

EPS = 1e-6
F32 = jnp.float32
BF = jnp.bfloat16
MB = 1024 * 1024

CORE = [(s, s ^ 1) for s in range(4)]
YSWAP = [(s, s ^ 2) for s in range(4)]
XSWAP = [(b, b ^ 1) for b in range(8)]


def zshift(k):
    return [(2 * z + x, 2 * ((z + k) % 4) + x) for z in range(4) for x in range(2)]


def out_block_perm():
    pairs = []
    for s in range(4):
        for b in range(8):
            y, c, part = b & 1, (b >> 1) & 1, b >> 2
            ys, cs = s >> 1, s & 1
            pairs.append((s * 8 + b, (2 * y + c) * 8 + 2 * (2 * part + cs) + ys))
    return pairs


OUT_PERM = out_block_perm()
OUT_BACK = [(d, s) for s, d in OUT_PERM]
FORGET_PERM = [(2 * (d & 1) + (d >> 1), d) for d in range(4)]


def sigm(v):
    return 0.5 * jnp.tanh(0.5 * v) + 0.5


def mm(a, b):
    return jnp.dot(a, b, preferred_element_type=F32)


def mm_bt(a, b):
    return lax.dot_general(a, b, (((1,), (1,)), ((), ())), preferred_element_type=F32)


def mm_at(a, b):
    return lax.dot_general(a, b, (((0,), (0,)), ((), ())), preferred_element_type=F32)


def sds(shape, dtype):
    return jax.ShapeDtypeStruct(shape, dtype)


HBM, SMEM, VMEM = "hbm", "smem", "vmem"


def tiled_bytes(a):
    shape = (1, 1) + tuple(a.shape)
    lanes, rows = -(-shape[-1] // 128) * 128, -(-shape[-2] // 16) * 16
    return math.prod(shape[:-2]) * rows * lanes * jnp.dtype(a.dtype).itemsize


def call(body, outs, args, kinds=None, okinds=None, scratch=(), room=8, flops=0, name=None):
    kinds = kinds or [VMEM] * len(args)
    okinds = okinds or [VMEM] * len(outs)
    held = sum(tiled_bytes(a) for a, k in zip(args, kinds) if k == VMEM)
    held += sum(tiled_bytes(o) for o, k in zip(outs, okinds) if k == VMEM)
    held += sum(tiled_bytes(m) for m in scratch if m.memory_space == pltpu.VMEM)
    vmem = 63 if room is None else -(-held // MB) + room
    space = {HBM: pl.ANY, SMEM: pltpu.SMEM, VMEM: pltpu.VMEM}
    nbytes = sum(a.size * a.dtype.itemsize for a in args)
    nbytes += sum(o.size * o.dtype.itemsize for o in outs)
    return pl.pallas_call(
        body,
        out_shape=outs,
        in_specs=[pl.BlockSpec(memory_space=space[k]) for k in kinds],
        out_specs=[pl.BlockSpec(memory_space=space[k]) for k in okinds],
        scratch_shapes=list(scratch),
        compiler_params=pltpu.CompilerParams(vmem_limit_bytes=vmem * MB),
        cost_estimate=pl.CostEstimate(
            flops=10 * (flops + 3 * 10**8), bytes_accessed=nbytes, transcendentals=0
        ),
        name=name,
    )(*args)


def hilo(col):
    rows = col.shape[0]
    hi = col.astype(BF)
    lo = (col - hi.astype(F32)).astype(BF)
    lane = lax.broadcasted_iota(jnp.int32, (rows, 128), 1)
    hi_b = jnp.broadcast_to(hi.astype(F32), (rows, 128))
    lo_b = jnp.broadcast_to(lo.astype(F32), (rows, 128))
    return jnp.where(lane == 0, hi_b, jnp.where(lane == 1, lo_b, 0.0)).astype(BF)


def lanesum(tile):
    return jnp.sum(tile.astype(F32), axis=1, keepdims=True)


def interleave(blk, back):
    row = lax.broadcasted_iota(jnp.int32, (blk, blk), 0)
    col = lax.broadcasted_iota(jnp.int32, (blk, blk), 1)
    if back:
        row, col = col, row
    hit = col == (row % 8) * (blk // 8) + row // 8
    return jnp.where(hit, 1.0, 0.0).astype(BF)


class Copies:
    def __init__(self, sems):
        self.sems, self.used = sems, 0

    def start(self, pairs):
        made = []
        for src, dst in pairs:
            made.append(pltpu.make_async_copy(src, dst, self.sems.at[self.used]))
            made[-1].start()
            self.used += 1
        return made


def wait_all(made):
    for m in made:
        m.wait()


def rows_of(i, n):
    return pl.ds(pl.multiple_of(i * n, n), n)


def norm1_body(x_ref, c_ref, o_ref, xp_ref, cp_ref):
    perm = interleave(x_ref.shape[0], False)
    x = mm(perm, x_ref[...])
    xp_ref[...] = x.astype(BF)
    cp_ref[...] = mm(perm, c_ref[...]).astype(BF)
    sc = lax.rsqrt(jnp.mean(x * x, axis=1, keepdims=True) + EPS)
    o_ref[...] = (x * sc).astype(BF)


def line_body(g1_ref, g2_ref, ph_ref, gm_ref, id_ref, o_ref):
    line = jnp.concatenate([g1_ref[...], g2_ref[...], ph_ref[...], gm_ref[...]])[None, :]
    line = jnp.concatenate([line.astype(F32), jnp.zeros((1, 256 - line.shape[1]), F32)], axis=1)
    both = jnp.concatenate([id_ref[...].astype(F32), line], axis=1)
    o_ref[...] = jnp.broadcast_to(both, o_ref.shape).astype(BF)


def pack_body(idx_ref, in_ref, og_ref, far_ref, fg_ref, out_ref, l_ref, lx_ref, o_ref, both_ref):
    rows, ch = fg_ref.shape
    nat = rows_of(idx_ref[2], ch)
    o_ref[0:rows, 0:ch] = in_ref[:, nat]
    o_ref[0:rows, ch : 2 * ch] = far_ref[:, 0:ch]
    o_ref[0:rows, 2 * ch : 3 * ch] = fg_ref[...]
    o_ref[0:rows, 3 * ch : 4 * ch] = og_ref[:, nat]
    o_ref[0:rows, 4 * ch : 5 * ch] = far_ref[:, ch:]
    o_ref[0:rows, 5 * ch : 6 * ch] = out_ref[0:rows, :]
    o_ref[0:rows, 6 * ch : 7 * ch] = out_ref[rows:, :]
    top = lax.broadcasted_iota(jnp.int32, l_ref.shape, 0) < 8
    both_ref[...] = jnp.where(top, l_ref[...].astype(F32), lx_ref[...].astype(F32)).astype(BF)


def smalls_body(
    idx_ref, v0, v1, v2, v3, lb_in,
    g1_ref, g2_ref, cos_ref, sin_ref, gm_ref, lb_ref, keep_ref,
    line_ref, ph_ref, gmix_ref,
):
    s, x, y, z = (idx_ref[i] for i in range(4))
    width = g1_ref.shape[1]
    ch = cos_ref.shape[1]
    blk = keep_ref.shape[1]
    vs = [
        jnp.concatenate([v[8 * j : 8 * j + 1, :] for j in range(8)], axis=0)
        for v in (v0, v1, v2, v3)
    ]
    rows = jnp.concatenate([v[:, blk:].astype(F32) for v in vs], axis=0)
    r = lax.broadcasted_iota(jnp.int32, (32, width), 0)
    lane = lax.broadcasted_iota(jnp.int32, (32, width), 1)
    i = r & 7
    piece = 2 * ((z - (i >> 1)) & 3) + jnp.where((i & 1) == 0, x, 1 - x)
    device = ((r >> 3) ^ s) * 8 + piece

    def spread(first, size):
        place = lax.broadcasted_iota(jnp.int32, (256, width), 0) - first
        to = lax.broadcasted_iota(jnp.int32, (256, width), 1) & (size - 1)
        one = jnp.where(place == to, 1.0, 0.0).astype(BF)
        wide = mm(rows.astype(BF), one)
        out = []
        for part in range(32 * size // width):
            mine = (lane + part * width) // size == device
            out.append(jnp.sum(jnp.where(mine, wide, 0.0), axis=0, keepdims=True))
        return out

    g1_ref[...] = spread(0, 32)[0]
    g2_ref[...] = spread(32, 32)[0]
    ph_ref[...] = spread(64, 32)[0]
    both = spread(96, 64)
    gmix_ref[0] = both[0]
    gmix_ref[1] = both[1]
    here = rows_of(2 * (s & 1) + (s >> 1), ch)
    phase = ph_ref[:, here]
    cos_ref[...] = jnp.cos(phase)
    sin_ref[...] = jnp.where(y == 0, 1.0, -1.0) * jnp.sin(phase)
    line_ref[...] = lb_in[...]
    lb_ref[...] = line_ref[:, here]
    gm_ref[:, 0:ch] = gmix_ref[y, :, here]
    gm_ref[:, ch:] = gmix_ref[1 - y, :, here]

    ids = [v[0:1, 0:blk].astype(F32) for v in vs]
    perm = interleave(blk, False)
    first = lax.broadcasted_iota(jnp.int32, (16, blk), 1) == 0
    for k in range(4):
        at = k ^ s
        last = jnp.full((1, 1), -1.0, F32)
        for q in range(4):
            last = jnp.where((q ^ s) == at - 1, ids[q][:, blk - 1 : blk], last)
        mine = jnp.broadcast_to(ids[k], (16, blk))
        before = jnp.where(first, jnp.broadcast_to(last, (16, blk)), pltpu.roll(mine, 1, 1))
        same = jnp.where(mine == before, 1.0, 0.0).astype(BF)
        keep_ref[k] = mm_bt(perm, same)[:, 0:1]


def rot_power(cos, sin, steps):
    n = 1
    while n < steps:
        cos, sin = cos * cos - sin * sin, 2.0 * cos * sin
        n *= 2
    return cos, sin


def combine_segments(s, order, end_ref, prod_ref, init_ref, ch, cn, sn):
    ca = jnp.zeros((1, ch), F32)
    cb = jnp.zeros((1, ch), F32)
    for at in order:
        k = at ^ s
        for j in range(8) if order[0] == 0 else reversed(range(8)):
            init_ref[k, j : j + 1, 0:ch] = ca
            init_ref[k, j : j + 1, ch : 2 * ch] = cb
            pj = prod_ref[k, j : j + 1, :]
            ta = pj * (cn * ca - sn * cb) + end_ref[k, j : j + 1, 0:ch]
            cb = pj * (cn * cb + sn * ca) + end_ref[k, j : j + 1, ch : 2 * ch]
            ca = ta


def blocks_in(refs, dst, blk):
    return [(r, dst.at[rows_of(k, blk)]) for k, r in enumerate(refs)]


def mix_in_copies(idx_ref, pieces, dst):
    cols = dst.shape[1]
    if len(pieces) == 1:
        return [(pieces[0].at[:, pl.ds(0, cols)], dst)]
    rows = dst.shape[0] // 8
    return [
        (p.at[pl.ds(0, rows), pl.ds(0, cols)], dst.at[rows_of(idx_ref[4 + i], rows)])
        for i, p in enumerate(pieces)
    ]


def mix_out_copies(idx_ref, pieces, dst):
    ch = dst.shape[0] // 2
    if len(pieces) == 1:
        return [(pieces[0], dst)]
    half = ch // 2
    out = []
    for i, p in enumerate(pieces):
        for j in range(2):
            rows = pl.ds(pl.multiple_of(idx_ref[12 + i] * ch + j * half, half), half)
            src = p.at[pl.ds(0, half), pl.ds((5 + j) * ch, ch)]
            out.append((src, dst.at[rows, rows_of(idx_ref[20 + i], ch)]))
    return out


def mixer_fwd_body(*refs, pieces):
    idx_ref, *refs = refs
    xs, refs = refs[:4], refs[4:]
    ps, refs = refs[:pieces], refs[pieces:]
    os, refs = (refs[:1], refs[1:]) if pieces == 1 else (ps, refs)
    (
        g1_ref, keep_ref, lb_ref, cos_ref, sin_ref, gm_ref,
        pre_out, dk_out, h_out, kr_out, k0_out, k1_out, s_out,
        x_ref, w_ref, wo_ref, pre_ref, dk_ref, h_ref, kr_ref, k0_ref, k1_ref, sout_ref,
        src_ref, gs_ref, end_ref, prod_ref, init_ref, sems,
    ) = refs
    s = idx_ref[0]
    ch = lb_ref.shape[1]
    blk = dk_ref.shape[1]
    width = wo_ref.shape[1]
    n = blk // 8
    dma = Copies(sems)
    need = dma.start(blocks_in(xs, x_ref, blk) + mix_in_copies(idx_ref, ps, w_ref))
    need_out = dma.start(mix_out_copies(idx_ref, os, wo_ref))
    wait_all(need)

    lb = lb_ref[...]
    g1 = g1_ref[...]
    saved = []
    for k in range(4):
        xg = (x_ref[rows_of(k, blk), :].astype(F32) * g1).astype(BF)
        p = mm(xg, w_ref[...])
        pre_ref[k] = p.astype(BF)
        sig = sigm(p[:, 2 * ch : 3 * ch])
        om = (1.0 - lb) * (1.0 - sig)
        dk_ref[k] = keep_ref[k] * (lb + (1.0 - lb) * sig)
        a = p[:, 0:ch]
        b = p[:, ch : 2 * ch]
        src_ref[k, :, 0:ch] = a * sigm(a) * om
        src_ref[k, :, ch : 2 * ch] = b * sigm(b) * om
        gs_ref[k] = sigm(p[:, 3 * ch : 5 * ch])
        saved += dma.start([(pre_ref.at[k], pre_out.at[k]), (dk_ref.at[k], dk_out.at[k])])

    cos = cos_ref[...][None]
    sin = sin_ref[...][None]
    zero = jnp.zeros((4, 8, ch), F32)

    def load(i):
        rows = rows_of(i, 8)
        return dk_ref[:, rows, :], src_ref[:, rows, 0:ch], src_ref[:, rows, ch : 2 * ch]

    def first_pass(i, st):
        ha, hb, prod = st
        d, sa, sb = load(i)
        ra = cos * ha - sin * hb
        rb = cos * hb + sin * ha
        return d * ra + sa, d * rb + sb, prod * d

    ha, hb, prod = lax.fori_loop(0, n, first_pass, (zero, zero, zero + 1.0), unroll=4)
    end_ref[:, :, 0:ch] = ha
    end_ref[:, :, ch : 2 * ch] = hb
    prod_ref[...] = prod
    cn, sn = rot_power(cos_ref[...], sin_ref[...], n)
    combine_segments(s, (0, 1, 2, 3), end_ref, prod_ref, init_ref, ch, cn, sn)

    def second_pass(i, st):
        ha, hb = st
        d, sa, sb = load(i)
        rows = rows_of(i, 8)
        ra = cos * ha - sin * hb
        rb = cos * hb + sin * ha
        ha = d * ra + sa
        hb = d * rb + sb
        live = d > 0.0
        h_ref[:, rows, 0:ch] = ha
        h_ref[:, rows, ch : 2 * ch] = hb
        kr_ref[:, rows, 0:ch] = jnp.where(live, ra, 0.0)
        kr_ref[:, rows, ch : 2 * ch] = jnp.where(live, rb, 0.0)
        return ha, hb

    lax.fori_loop(
        0, n, second_pass, (init_ref[:, :, 0:ch], init_ref[:, :, ch : 2 * ch]), unroll=4
    )
    saved += dma.start([(h_ref, h_out), (kr_ref, kr_out)])
    wait_all(need_out)
    gm = gm_ref[...]

    def emit(k):
        gated = h_ref[k] * gs_ref[k]
        ss = jnp.sum(gated * gated, axis=1, keepdims=True)
        return mm((gated * gm).astype(BF), wo_ref[...]), hilo(ss)

    for i in range(2):
        v, tail = emit(2 * i + 1)
        sout_ref[i, :, 0:width] = v.astype(BF)
        sout_ref[i, :, width:] = tail
        saved += dma.start([(sout_ref.at[i], s_out.at[i])])
    for k, ref, out in ((2, k1_ref, k1_out), (0, k0_ref, k0_out)):
        v, tail = emit(k)
        ref[:, 0:width] = v.astype(BF)
        ref[:, width:] = tail
        saved += dma.start([(ref, out)])
    wait_all(saved)


def resid_body(x_ref, own_ref, got_ref, ry_ref, g2_ref, resid_ref, fin_ref, sc_ref, *, chans):
    width = x_ref.shape[1]
    tot = own_ref[...].astype(F32) + got_ref[0].astype(F32) + ry_ref[...].astype(F32)
    ss = jnp.sum(tot[:, width:], axis=1, keepdims=True)
    sc = lax.rsqrt(ss / chans + EPS)
    resid = x_ref[...].astype(F32) + sc * tot[:, 0:width]
    resid_ref[...] = resid
    sc2 = lax.rsqrt(jnp.mean(resid * resid, axis=1, keepdims=True) + EPS)
    fin_ref[...] = (resid * sc2 * g2_ref[...]).astype(BF)
    sc_ref[...] = jnp.broadcast_to(sc, sc_ref.shape)


def col_copies(idx_ref, pieces, dst):
    if len(pieces) == 1:
        return [(pieces[0], dst)]
    out = []
    for i, p in enumerate(pieces):
        rows, cols = p.shape
        place = i if i < 8 else 2 if i == 8 else 6
        at = pl.ds(0 if i < 8 else rows, rows)
        out.append((p, dst.at[at, rows_of(idx_ref[4 + place], cols)]))
    return out


def ffn_body(*refs, pieces):
    idx_ref, *refs = refs
    xs, cots, refs = refs[:4], refs[4:8], refs[8:]
    ps, refs = refs[:pieces], refs[pieces:]
    (
        hid_out, ggu_out, k0_out, k1_out, s_out, kept2_out, s2_out,
        x_ref, c_ref, w_ref, hid_ref, ggu_ref, k0_ref, k1_ref, sout_ref, kept2_ref, s2_ref, sems,
    ) = refs
    blk = k0_ref.shape[0]
    hu = hid_ref.shape[1]
    dma = Copies(sems)
    need = dma.start(blocks_in(xs, x_ref, blk) + col_copies(idx_ref, ps, w_ref))
    later = dma.start(blocks_in(cots, c_ref, blk))
    wait_all(need)
    saved = []
    for k in (1, 3, 2, 0):
        rel = pl.ds(k * blk, blk)
        gu = mm_bt(x_ref[rel, :], w_ref[0 : 2 * hu, :])
        wait_all(later)
        later = []
        gh = mm_bt(c_ref[rel, :], w_ref[2 * hu :, :])
        g = gu[:, 0:hu]
        u = gu[:, hu : 2 * hu]
        sg = sigm(g)
        q = g * sg
        hid_ref[rel, :] = (q * u).astype(BF)
        dg = gh * (u * (sg + q * (1.0 - sg)))
        both = jnp.concatenate([dg, gh * q], axis=1).astype(BF)
        ggu_ref[rel, :] = both
        saved += dma.start(
            [(hid_ref.at[rel], hid_out.at[rel]), (ggu_ref.at[rel], ggu_out.at[rel])]
        )
        back = mm(both, w_ref[0 : 2 * hu, :])
        if k in (1, 3):
            sout_ref[k // 2] = back.astype(BF)
            saved += dma.start([(sout_ref.at[k // 2], s_out.at[k // 2])])
        else:
            ref, out = (k1_ref, k1_out) if k == 2 else (k0_ref, k0_out)
            ref[...] = back.astype(BF)
            saved += dma.start([(ref, out)])
    ffn_grad_part(idx_ref, 2, ggu_ref, hid_ref, x_ref, c_ref, kept2_ref, s2_ref)
    wait_all(saved + dma.start([(kept2_ref, kept2_out), (s2_ref, s2_out)]))


def down_body(*refs, pieces):
    idx_ref, h_ref, *refs = refs
    ps, refs = refs[:pieces], refs[pieces:]
    k0_ref, k1_ref, sout_ref, wd_ref, sems = refs
    blk = k0_ref.shape[0]
    hu = h_ref.shape[1]
    if pieces > 1:
        last = {2: ps[8], 6: ps[9]}
        ps = [last.get(i, p) for i, p in enumerate(ps[:8])]
    ps = [p.at[pl.ds(p.shape[0] - hu, hu)] for p in ps]
    wait_all(Copies(sems).start(col_copies(idx_ref, ps, wd_ref)))

    def emit(k):
        return mm(h_ref[rows_of(k, blk), :], wd_ref[...])

    sout_ref[0] = emit(1).astype(BF)
    sout_ref[1] = emit(3).astype(BF)
    k1_ref[...] = emit(2).astype(BF)
    k0_ref[...] = emit(0).astype(BF)


def put_parts(kk, keep, send, outs, where):
    kept_ref, send_ref = outs[kk]
    kept_ref[where] = keep.astype(kept_ref.dtype)
    send_ref[where] = send.astype(BF)


def ffn_grad_part(idx_ref, kk, g_ref, h_ref, x_ref, c_ref, keep_ref, send_ref):
    first = idx_ref[1] == 0
    hu = h_ref.shape[1]
    cols = rows_of((idx_ref[3] + kk) & 3, 256)
    for src, left, at, size in ((x_ref, g_ref, 0, 2 * hu), (c_ref, h_ref, 2 * hu, hu)):
        v = mm_at(left[...], src[:, cols])
        lo, hi = v[:, 0:128], v[:, 128:256]
        where = pl.ds(at, size)
        keep_ref[where, :] = jnp.where(first, lo, hi).astype(keep_ref.dtype)
        send_ref[where, :] = jnp.where(first, hi, lo).astype(send_ref.dtype)


def ffn_grad_body(
    idx_ref, h_ref, g_ref, x0, x1, x2, x3, c0, c1, c2, c3,
    own_ref, k1_ref, k3_ref, s1_ref, s3_ref, s0_ref, x_ref, c_ref, sems,
):
    blk = x_ref.shape[0] // 4
    dma = Copies(sems)
    need = dma.start(blocks_in((x0, x1, x2, x3), x_ref, blk))
    need += dma.start(blocks_in((c0, c1, c2, c3), c_ref, blk))
    wait_all(need)
    for kk, keep, send in (
        (1, k1_ref, s1_ref), (3, k3_ref, s3_ref), (0, own_ref, s0_ref),
    ):
        ffn_grad_part(idx_ref, kk, g_ref, h_ref, x_ref, c_ref, keep, send)


def gresid_body(
    own_ref, got_ref, ry_ref, c_ref, resid_ref, x_ref, sc_ref, g2_ref,
    gres_ref, pay_ref, gg2_ref, *, chans,
):
    width = x_ref.shape[1]
    gfi = own_ref[...].astype(F32) + got_ref[0].astype(F32) + ry_ref[...].astype(F32)
    resid = resid_ref[...]
    sc2 = lax.rsqrt(jnp.mean(resid * resid, axis=1, keepdims=True) + EPS)
    second = resid * sc2
    @pl.when(pl.program_id(0) == 0)
    def _():
        gg2_ref[...] = jnp.zeros_like(gg2_ref)

    gg2_ref[...] += jnp.sum(gfi * second, axis=0, keepdims=True)
    g = gfi * g2_ref[...]
    gres = c_ref[...].astype(F32) + sc2 * (
        g - second * jnp.mean(g * second, axis=1, keepdims=True)
    )
    gres_ref[...] = gres
    sc = sc_ref[:, 0:1]
    branch = resid - x_ref[...].astype(F32)
    kappa = sc * sc * (jnp.sum(gres * branch, axis=1, keepdims=True) / chans)
    pay_ref[:, 0:width] = (gres * sc).astype(BF)
    pay_ref[:, width:] = hilo(kappa)


def bwd_body(*refs, pieces):
    idx_ref, *refs = refs
    pays, xs, refs = refs[:4], refs[4:8], refs[8:]
    ps, refs = refs[:pieces], refs[pieces:]
    os, refs = (refs[:1], refs[1:]) if pieces == 1 else (ps, refs)
    (
        pre_in, dk_in, h_in, kr_in, lb_ref, cos_ref, sin_ref, g1_ref, gm_ref,
        ggm_ref, gph_ref, own_out, e1_out, e3_out, e2_out, s2_out, s1_out, s3_out, s0_out,
        k0_out, k1_out, s_out,
        own_ref, e1_ref, e3_ref, e2_ref, s2_ref, s1_ref, s3_ref, s0_ref,
        k0_ref, k1_ref, sout_ref,
        p_ref, x_ref, w_ref, wo_ref, pre_ref, dk_ref, h_ref, kr_ref, u_ref, g_ref, dir_ref,
        end_ref, prod_ref, init_ref, sems,
    ) = refs
    s = idx_ref[0]
    ch = lb_ref.shape[1]
    blk = dk_ref.shape[1]
    n = blk // 8
    width = wo_ref.shape[1]
    dma = Copies(sems)
    need = dma.start(blocks_in(pays, p_ref, blk) + mix_out_copies(idx_ref, os, wo_ref))
    by_block = [
        dma.start([(pre_in.at[k], pre_ref.at[k]), (h_in.at[k], h_ref.at[k])]) for k in range(4)
    ]
    need2 = dma.start([(dk_in, dk_ref), (kr_in, kr_ref)])
    need3 = dma.start(blocks_in(xs, x_ref, blk) + mix_in_copies(idx_ref, ps, w_ref))
    wait_all(need)
    gm = gm_ref[...]
    ggm_ref[...] = jnp.zeros_like(ggm_ref)

    for k in range(4):
        rel = pl.ds(k * blk, blk)
        back = mm_bt(p_ref[rel, 0:width], wo_ref[...])
        wait_all(by_block[k])
        kappa = lanesum(p_ref[rel, width:])
        gs = sigm(pre_ref[k, :, 3 * ch : 5 * ch].astype(F32))
        h = h_ref[k]
        gated = h * gs
        u_ref[rel, :] = (gated * gm).astype(BF)
        ggm_ref[...] += jnp.sum(back * gated, axis=0, keepdims=True)
        d = (back * gm - gated * kappa) * gs
        dir_ref[k] = d
        g_ref[rel, 3 * ch : 5 * ch] = (d * h * (1.0 - gs)).astype(BF)

    wait_all(need2)
    gph_ref[...] = jnp.zeros_like(gph_ref)
    cos = cos_ref[...][None]
    sin = sin_ref[...][None]
    zero = jnp.zeros((4, 8, ch), F32)

    def load(i):
        rows = rows_of(i, 8)
        return dk_ref[:, rows, :], dir_ref[:, rows, 0:ch], dir_ref[:, rows, ch : 2 * ch]

    def first_pass(j, st):
        fa, fb, prod = st
        d, da, db = load(n - 1 - j)
        ga = da + fa
        gb = db + fb
        return d * (cos * ga + sin * gb), d * (cos * gb - sin * ga), prod * d

    fa, fb, prod = lax.fori_loop(0, n, first_pass, (zero, zero, zero + 1.0), unroll=4)
    end_ref[:, :, 0:ch] = fa
    end_ref[:, :, ch : 2 * ch] = fb
    prod_ref[...] = prod
    cn, sn = rot_power(cos_ref[...], sin_ref[...], n)
    combine_segments(s, (3, 2, 1, 0), end_ref, prod_ref, init_ref, ch, cn, -sn)

    def second_pass(j, st):
        fa, fb = st
        i = n - 1 - j
        d, da, db = load(i)
        rows = rows_of(i, 8)
        ga = da + fa
        gb = db + fb
        dir_ref[:, rows, 0:ch] = ga
        dir_ref[:, rows, ch : 2 * ch] = gb
        return d * (cos * ga + sin * gb), d * (cos * gb - sin * ga)

    lax.fori_loop(
        0, n, second_pass, (init_ref[:, :, 0:ch], init_ref[:, :, ch : 2 * ch]), unroll=4
    )
    lb = lb_ref[...]

    def grads(k, carry):
        rel = rows_of(k, blk)
        ga = dir_ref[k, :, 0:ch]
        gb = dir_ref[k, :, ch : 2 * ch]
        ra = kr_ref[k, :, 0:ch]
        rb = kr_ref[k, :, ch : 2 * ch]
        a = pre_ref[k, :, 0:ch].astype(F32)
        b = pre_ref[k, :, ch : 2 * ch].astype(F32)
        sf = sigm(pre_ref[k, :, 2 * ch : 3 * ch].astype(F32))
        sa = sigm(a)
        sb = sigm(b)
        om = (1.0 - lb) * (1.0 - sf)
        gdec = ga * ra + gb * rb - (ga * a * sa + gb * b * sb)
        gph_ref[...] += jnp.sum(dk_ref[k] * (gb * ra - ga * rb), axis=0, keepdims=True)
        g_ref[rel, 0:ch] = (ga * (sa * (1.0 + a * (1.0 - sa))) * om).astype(BF)
        g_ref[rel, ch : 2 * ch] = (gb * (sb * (1.0 + b * (1.0 - sb))) * om).astype(BF)
        g_ref[rel, 2 * ch : 3 * ch] = (gdec * om * sf).astype(BF)
        return carry

    lax.fori_loop(0, 4, grads, 0)
    wait_all(need3)

    def emit(k):
        return mm_bt(g_ref[rows_of(k, blk), :], w_ref[...])

    sout_ref[0] = emit(1).astype(BF)
    sout_ref[1] = emit(3).astype(BF)
    saved = dma.start([(sout_ref, s_out)])
    k1_ref[...] = emit(2).astype(BF)
    k0_ref[...] = emit(0).astype(BF)
    saved += dma.start([(k1_ref, k1_out), (k0_ref, k0_out)])

    g1 = g1_ref[...]

    def gain(k, carry):
        rel = rows_of(k, blk)
        x_ref[rel, :] = (x_ref[rel, :].astype(F32) * g1).astype(BF)
        return carry

    lax.fori_loop(0, 4, gain, 0)
    first = idx_ref[1] == 0
    outs = ((own_ref, s0_ref), (e1_ref, s1_ref), (e2_ref, s2_ref), (e3_ref, s3_ref))
    targets = ((own_out, s0_out), (e1_out, s1_out), (e2_out, s2_out), (e3_out, s3_out))
    half = own_ref.shape[0]
    for kk in (2, 1, 3, 0):
        zz = (idx_ref[3] + kk) & 3
        v = mm_at(x_ref[:, rows_of(zz, 2 * half)], g_ref[...])
        lo, hi = v[0:half, :], v[half:, :]
        put_parts(
            kk, jnp.where(first, lo, hi), jnp.where(first, hi, lo), outs,
            (slice(None), pl.ds(0, 5 * ch)),
        )
        u = u_ref[:, rows_of((zz >> 1) ^ idx_ref[2], ch)]
        lo = mm_at(u, p_ref[:, rows_of(zz & 1, ch)])
        hi = mm_at(u, p_ref[:, rows_of(2 + (zz & 1), ch)])
        keep, send = jnp.where(first, lo, hi), jnp.where(first, hi, lo)
        for j in range(2):
            rows = slice(j * half, (j + 1) * half)
            put_parts(
                kk, keep[rows], send[rows], outs, (slice(None), pl.ds((5 + j) * ch, ch)),
            )
        saved += dma.start(list(zip(outs[kk], targets[kk])))
    wait_all(saved)


def gin_body(own_ref, got_ref, ry_ref, x_ref, gres_ref, g1_ref, out_ref, gg1_ref):
    gn = own_ref[...].astype(F32) + got_ref[0].astype(F32) + ry_ref[...].astype(F32)
    x = x_ref[...].astype(F32)
    sc = lax.rsqrt(jnp.mean(x * x, axis=1, keepdims=True) + EPS)
    first = x * sc
    gg1_ref[...] = jnp.sum(gn * first, axis=0, keepdims=True)
    nn = gn * g1_ref[...]
    res = gres_ref[...] + sc * (nn - first * jnp.mean(nn * first, axis=1, keepdims=True))
    out_ref[...] = mm(interleave(x.shape[0], True), res.astype(BF)).astype(BF)


def finish_body(idx_ref, m_ref, far_ref, o_in, f_in, gi_ref, go_ref, o_ref, f_ref):
    rows = m_ref.shape[0]
    ch = far_ref.shape[1] // 2
    nat, far = rows_of(idx_ref[2], ch), rows_of(1 - idx_ref[2], ch)
    gi_ref[:, nat] = m_ref[:, 0:ch]
    gi_ref[:, far] = far_ref[:, 0:ch].astype(F32)
    go_ref[:, nat] = m_ref[:, 3 * ch : 4 * ch]
    go_ref[:, far] = far_ref[:, ch:].astype(F32)
    o_ref[0:rows, :] = o_in[:, 0:ch].astype(F32)
    o_ref[rows:, :] = o_in[:, ch:].astype(F32)
    f_ref[...] = f_in[...].astype(F32)


def far_body(k_ref, g_ref, o_ref):
    o_ref[...] = (k_ref[...].astype(F32) + g_ref[0].astype(F32)).astype(BF)


def blockout_body(resid_ref, own_ref, got_ref, ry_ref, out_ref):
    res = resid_ref[...] + own_ref[...].astype(F32) + got_ref[0].astype(F32) + ry_ref[...].astype(F32)
    out_ref[...] = mm(interleave(res.shape[0], True), res.astype(BF)).astype(BF)


def after(value, *deps):
    return lax.optimization_barrier((value, deps))[0]


def seq_gather(v):
    yv = lax.ppermute(v, "seq", YSWAP)
    cv = lax.ppermute(v, "seq", CORE)
    ycv = lax.ppermute(yv, "seq", CORE)
    return [v, cv, yv, ycv]


def seq_scatter(k1, got):
    far = plus(k1, got[1])
    return got, lax.ppermute(far, "seq", YSWAP)


def batch_pieces():
    b = lax.axis_index("batch")
    z, x = b // 2, b % 2
    at = [2 * ((z + 4 - k) % 4) + x for k in range(4)]
    return at + [a ^ 1 for a in at]


def xsend(pack):
    return lax.ppermute(pack, "batch", XSWAP)


def plus(a, b):
    return (a.astype(F32) + b.astype(F32)).astype(BF)


class Scatter:
    def __init__(self, own, kept1, kept3, kept2, s2, s1, s3, s0):
        self.kept = [own, kept1, kept2, kept3]
        self.send = [s0, s1, s2, s3]
        self.got, self.part, self.z = {}, {}, {}

    def along_x(self, kk, *deps):
        self.got[kk] = xsend(after(self.send[kk], *deps) if deps else self.send[kk])

    def add(self, kk, *deps):
        kept = after(self.kept[kk], *deps) if deps else self.kept[kk]
        self.part[kk] = plus(kept, self.got[kk])

    def along_z(self, kk, *deps):
        part = after(self.part[kk], *deps) if deps else self.part[kk]
        self.z[kk] = lax.ppermute(part, "batch", zshift(kk))

    def total(self, *deps):
        out = after(self.kept[0], *deps) + self.got[0].astype(F32)
        for v in self.z.values():
            out = out + v.astype(F32)
        return out


def small_sum(v, *deps):
    v = v + lax.ppermute(v, "seq", CORE)
    v = v + lax.ppermute(v, "seq", YSWAP)
    v = v + lax.ppermute(v, "batch", XSWAP)
    v = after(v, *deps)
    return v + sum(lax.ppermute(v, "batch", zshift(k)) for k in (1, 2, 3))


def per_device(
    block_input, segment_ids, out_cotangent, lower_bound, gain_first, w_input, w_forget,
    w_outgate, phase_angle, gain_mixer, w_output, gain_second, w_gate, w_up, w_down,
):
    s = lax.axis_index("seq")
    b = lax.axis_index("batch")
    y, c = s // 2, s % 2
    z, x = b // 2, b % 2
    nb = lax.axis_size("batch")
    blk, width = block_input.shape[1:]
    tok = 4 * blk
    ch = width // 4
    hu = w_gate.shape[1]
    start = 2 * ch * c + ch * y
    wide = nb == 8
    dma = pltpu.SemaphoreType.DMA
    tail = width + 128
    row8 = width // 8

    far_cols = (1 - y) * ch
    far_src = jnp.concatenate(
        [
            lax.dynamic_slice(w_input, (0, far_cols), (w_input.shape[0], ch)),
            lax.dynamic_slice(w_outgate, (0, far_cols), (w_input.shape[0], ch)),
        ],
        axis=1,
    )
    far = lax.ppermute(far_src, "seq", YSWAP)
    fg = lax.ppermute(w_forget, "seq", FORGET_PERM)
    x_own, xp, cp = call(
        norm1_body, [sds((blk, width), BF)] * 3, [block_input[0], out_cotangent[0]],
        name="norm1",
    )
    pack_f = jnp.concatenate([w_gate.T, w_up.T, w_down], axis=0)
    zero = jnp.zeros((), jnp.int32)
    smem1 = [SMEM] + [VMEM] * 11
    if wide:
        at = batch_pieces()
        brow = [(a // 4) ^ y for a in at]
        bcol = [2 * (a % 2) + (a // 2) % 2 for a in at]
        idx = jnp.stack([s, x, y, z] + at + brow + bcol).astype(jnp.int32)
        moved = lax.ppermute(w_output, ("seq", "batch"), OUT_PERM)
        line = call(
            line_body, [sds((16, 512), BF)],
            [gain_first, gain_second, phase_angle, gain_mixer, segment_ids], room=None,
            name="line",
        )[0]
        line_x = xsend(line)
        pack_m, both = call(
            pack_body, [sds((row8, 7 * ch), BF), sds((16, 512), BF)],
            [idx, w_input, w_outgate, far, fg, moved, line, line_x],
            smem1[:8], room=None, name="pack",
        )
        mz1 = lax.ppermute(pack_m, "batch", zshift(1))
        mx0 = xsend(pack_m)
        mz3 = lax.ppermute(after(pack_m, mz1), "batch", zshift(3))
        mx1 = xsend(after(mz1, mx0))
        mz2 = lax.ppermute(after(pack_m, mz3, mx1), "batch", zshift(2))
        mx3 = xsend(after(mz3, mx1))
        xs = seq_gather(after(x_own, far))
        xs[3] = lax.ppermute(after(xs[2], mx3), "seq", CORE)
        mx2 = xsend(after(mz2, mx1, mx3))
        fz1 = lax.ppermute(after(pack_f, mz2), "batch", zshift(1))
        fz3 = lax.ppermute(after(pack_f, fz1), "batch", zshift(3))
        fx0 = xsend(after(pack_f, mx2))
        half = 3 * hu // 2
        fz2a = lax.ppermute(after(pack_f[0:half], fz3), "batch", zshift(2))
        fz2b = lax.ppermute(after(pack_f[half:], fz2a), "batch", zshift(2))
        fx1 = xsend(after(fz1, fx0))
        fx3 = xsend(after(fz3, fx1))
        fx2a = xsend(after(fz2a, fx3))
        fx2b = xsend(after(fz2b, fx3))
        mixes = [pack_m, mz1, mz2, mz3, mx0, mx1, mx2, mx3]
        ffns = [pack_f, fz1, fz2a, fz3, fx0, fx1, fx2a, fx3, fz2b, fx2b]
        lines = jnp.concatenate(
            [both] + [lax.ppermute(after(both, xs[2]), "batch", zshift(k)) for k in (1, 2, 3)], axis=0
        )
        lines = seq_gather(after(lines, mx3))
        cots = seq_gather(after(cp, lines[2]))
        gain1, gain2, cos, sin, gm, lb, keep = call(
            smalls_body,
            [sds((1, width), F32)] * 2 + [sds((1, ch), F32)] * 2
            + [sds((1, 2 * ch), F32), sds((1, ch), F32), sds((4, blk, 1), F32)],
            [idx, *lines, lower_bound[None]], smem1[:6],
            scratch=[
                pltpu.VMEM((1, width), F32), pltpu.VMEM((1, width), F32),
                pltpu.VMEM((2, 1, width), F32),
            ],
            room=None, name="smalls",
        )
        outs_w = []
    else:
        idx = jnp.stack([s, zero, y, zero] + [zero] * 24).astype(jnp.int32)
        xs = seq_gather(x_own)
        cots = seq_gather(cp)
        nat = lambda w: lax.dynamic_slice(w, (0, y * ch), (w.shape[0], ch))
        mix = [nat(w_input), far[:, 0:ch], fg, nat(w_outgate), far[:, ch:]]
        mixes = [lax.all_gather(jnp.concatenate(mix, axis=1), "batch", axis=0, tiled=True)]
        ffns = [lax.all_gather(pack_f, "batch", axis=1, tiled=True)]
        full = lax.all_gather(w_output, "batch", axis=0, tiled=True)
        full = lax.all_gather(full, "seq", axis=1, tiled=True)
        outs_w = [
            jnp.concatenate(
                [
                    lax.dynamic_slice(full, (y * width + start, 0), (ch, width)),
                    lax.dynamic_slice(full, ((1 - y) * width + start, 0), (ch, width)),
                ],
                axis=0,
            )
        ]
        small = jnp.concatenate(
            [gain_first, gain_second, phase_angle, gain_mixer, segment_ids[0].astype(BF)]
        )
        g1n, gmn = gain_first.shape[0], gain_mixer.shape[0]
        every = lax.all_gather(small, ("seq", "batch"), axis=0).reshape(4, nb, -1)
        gain1 = every[:, :, 0:g1n].reshape(1, width).astype(F32)
        gain2 = every[:, :, g1n : 2 * g1n].reshape(1, width).astype(F32)
        phase = every[:, :, 2 * g1n : 3 * g1n].reshape(1, width).astype(F32)
        gainm = every[:, :, 3 * g1n : 3 * g1n + gmn].reshape(2, width).astype(F32)
        ids = lax.dynamic_index_in_dim(every[:, :, 3 * g1n + gmn :], b, 1, False).reshape(tok)
        keep = jnp.concatenate([jnp.zeros((1,), F32), (ids[1:] == ids[:-1]).astype(F32)])
        keep = jnp.swapaxes(keep.reshape(4, 8, blk // 8), 1, 2).reshape(4, blk)
        keep = jnp.where(c == 1, keep[jnp.array([1, 0, 3, 2])], keep)
        keep = jnp.where(y == 1, keep[jnp.array([2, 3, 0, 1])], keep)[:, :, None]
        phase = lax.dynamic_slice(phase, (0, start), (1, ch))
        cos = jnp.cos(phase)
        sin = jnp.sin(phase) * jnp.where(y == 0, 1.0, -1.0).astype(F32)
        lb = lax.dynamic_slice(lower_bound[None, :], (0, start), (1, ch))
        gm = jnp.concatenate(
            [
                lax.dynamic_slice(gainm, (y, start), (1, ch)),
                lax.dynamic_slice(gainm, (1 - y, start), (1, ch)),
            ],
            axis=1,
        )
    early = []
    pieces = len(mixes)
    fpieces = len(ffns)
    sign = jnp.where(y == 0, 1.0, -1.0).astype(F32)

    scan_scratch = [
        pltpu.VMEM((4, 8, 2 * ch), F32), pltpu.VMEM((4, 8, ch), F32),
        pltpu.VMEM((4, 8, 2 * ch), F32),
    ]
    full_tok = pltpu.VMEM((tok, width), BF)
    big = pltpu.VMEM((4, blk, 2 * ch), F32)
    mix_all = mixes + outs_w
    pre, dk, h, kr, k0, k1, sout = call(
        functools.partial(mixer_fwd_body, pieces=pieces),
        [
            sds((4, blk, 5 * ch), BF), sds((4, blk, ch), F32), sds((4, blk, 2 * ch), F32),
            sds((4, blk, 2 * ch), F32), sds((blk, tail), BF), sds((blk, tail), BF),
            sds((2, blk, tail), BF),
        ],
        [idx, *xs, *mix_all, after(gain1, *early), keep, lb, cos, sin, gm],
        [SMEM] + [HBM] * (4 + len(mix_all)) + [VMEM] * 6,
        [HBM] * 7,
        scratch=[
            full_tok, pltpu.VMEM((width, 5 * ch), BF), pltpu.VMEM((2 * ch, width), BF),
            pltpu.VMEM((4, blk, 5 * ch), BF), pltpu.VMEM((4, blk, ch), F32), big, big,
            pltpu.VMEM((blk, tail), BF), pltpu.VMEM((blk, tail), BF),
            pltpu.VMEM((2, blk, tail), BF), big, big, *scan_scratch, dma((48,)),
        ],
        room=None, flops=2 * tok * width * 7 * ch, name="mixer_fwd",
    )
    if wide:
        sout = after(sout, fz3, fx0, *cots[1:3])
    got, near = seq_scatter(k1, lax.ppermute(sout, "seq", CORE))
    if wide:
        near = after(near, fz2a, fx1, cots[3])
    resid, fin, sc = call(
        functools.partial(resid_body, chans=2.0 * width),
        [sds((blk, width), F32), sds((blk, width), BF), sds((blk, 128), F32)],
        [xp, k0, got, near, gain2], name="resid",
    )
    fins = seq_gather(fin)
    if wide:
        fins[3] = lax.ppermute(after(fins[2], fx2a, fz2b), "seq", CORE)
    scat = [sds((blk, width), BF), sds((blk, width), BF), sds((2, blk, width), BF)]
    scat_v = [pltpu.VMEM(v.shape, v.dtype) for v in scat]
    part_f = sds((3 * hu, row8), BF)
    hid, ggu, k02, k12, sout2, kept2, s2 = call(
        functools.partial(ffn_body, pieces=fpieces),
        [sds((tok, hu), BF), sds((tok, 2 * hu), BF)] + scat + [part_f, part_f],
        [idx, *fins, *cots, *ffns], [SMEM] + [HBM] * (8 + fpieces),
        [HBM] * 7,
        scratch=[
            full_tok, full_tok, pltpu.VMEM((3 * hu, width), BF),
            pltpu.VMEM((tok, hu), BF), pltpu.VMEM((tok, 2 * hu), BF), *scat_v,
            pltpu.VMEM(part_f.shape, BF), pltpu.VMEM(part_f.shape, BF), dma((40,)),
        ],
        room=None, flops=10 * tok * width * hu, name="ffn",
    )

    got2 = lax.ppermute(sout2, "seq", CORE)
    far2 = pl.pallas_call(
        far_body,
        grid=(2,),
        out_shape=sds((blk, width), BF),
        in_specs=[
            pl.BlockSpec((blk // 2, width), lambda i: (i, 0)),
            pl.BlockSpec((1, blk // 2, width), lambda i: (1, i, 0)),
        ],
        out_specs=pl.BlockSpec((blk // 2, width), lambda i: (i, 0)),
        compiler_params=pltpu.CompilerParams(vmem_limit_bytes=63 * MB),
        cost_estimate=pl.CostEstimate(flops=10**8, bytes_accessed=2 * 10**6, transcendentals=0),
        name="far",
    )(k12, got2)
    near2 = lax.ppermute(far2, "seq", YSWAP)
    own_f, kept1, kept3, s1, s3, s0 = call(
        ffn_grad_body,
        [sds((3 * hu, row8), F32)] + [part_f] * 5,
        [idx, after(hid, far2), ggu, *fins, *cots],
        [SMEM, VMEM, VMEM] + [HBM] * 8, scratch=[full_tok, full_tok, dma((8,))],
        room=None, flops=6 * tok * width * hu, name="ffn_grad",
    )
    fsc = Scatter(own_f, kept1, kept3, kept2, s2, s1, s3, s0)
    first_sum = [s1]
    if wide:
        fsc.along_x(2)
        fsc.add(2, s1)
        fsc.along_z(2)
        fsc.along_x(1, fsc.got[2])
        fsc.along_x(3, fsc.got[1])
        first_sum.append(fsc.part[2])
    rows4 = blk // 4
    row = lambda w: pl.BlockSpec((rows4, w), lambda i: (i, 0))
    one = pl.BlockSpec((1, width), lambda i: (0, 0))
    gres, pay, gg2 = pl.pallas_call(
        functools.partial(gresid_body, chans=2.0 * width),
        grid=(4,),
        out_shape=[sds((blk, width), F32), sds((blk, tail), BF), sds((1, width), F32)],
        in_specs=[
            row(width), pl.BlockSpec((1, rows4, width), lambda i: (0, i, 0)), row(width),
            row(width), row(width), row(width), row(128), one,
        ],
        out_specs=[row(width), row(tail), one],
        compiler_params=pltpu.CompilerParams(vmem_limit_bytes=63 * MB),
        cost_estimate=pl.CostEstimate(
            flops=3 * 10**9, bytes_accessed=6 * 10**6, transcendentals=0
        ),
        name="gresid",
    )(k02, got2, near2, after(cp, *first_sum), resid, xp, sc, gain2)
    pays = seq_gather(pay)
    if wide:
        fsc.add(1, pay)
        fsc.along_z(1)
        pays[2] = after(pays[2], fsc.part[1])
        pays[3] = lax.ppermute(pays[2], "seq", CORE)
        fsc.add(3, pays[2])
        fsc.along_x(0, fsc.got[3])
        pays[1] = after(pays[1], fsc.part[3])
    part_m = [sds((row8, 7 * ch), F32)] + [sds((row8, 7 * ch), BF)] * 7
    ggm, gph, *msc, k04, k14, sout4 = call(
        functools.partial(bwd_body, pieces=pieces),
        [sds((1, 2 * ch), F32), sds((1, ch), F32)] + part_m + scat,
        [idx, *pays, *xs, *mix_all, pre, dk, h, kr, lb, cos, sin, gain1, gm],
        [SMEM] + [HBM] * (12 + len(mix_all)) + [VMEM] * 5, [VMEM] * 2 + [HBM] * 11,
        scratch=[
            *[pltpu.VMEM(v.shape, v.dtype) for v in part_m + scat],
            pltpu.VMEM((tok, tail), BF), full_tok, pltpu.VMEM((width, 5 * ch), BF),
            pltpu.VMEM((2 * ch, width), BF), pltpu.VMEM((4, blk, 5 * ch), BF),
            pltpu.VMEM((4, blk, ch), F32), big, big, pltpu.VMEM((tok, 2 * ch), BF),
            pltpu.VMEM((tok, 5 * ch), BF), big, *scan_scratch, dma((64,)),
        ],
        room=None, flops=6 * tok * width * 5 * ch, name="bwd",
    )
    msc = Scatter(*msc)
    if wide:
        msc.along_x(2)
        fsc.along_z(3, ggm)
        sout4 = after(sout4, fsc.z[2], fsc.z[1], fsc.got[0])
    got4, near4 = seq_scatter(k14, lax.ppermute(sout4, "seq", CORE))
    if wide:
        msc.add(2)
        msc.along_z(2)
        msc.along_x(1, msc.part[2])
        k04 = after(k04, msc.part[2])
    grad_input, gg1 = call(
        gin_body, [sds((blk, width), BF), sds((1, width), F32)],
        [k04, got4, near4, xp, gres, gain1], room=None, name="gin",
    )
    k03, k13, sout3 = call(
        functools.partial(down_body, pieces=fpieces), scat,
        [idx, after(hid, gg1, *([fsc.z[3]] if wide else [])), *ffns], [SMEM, VMEM] + [HBM] * fpieces,
        scratch=[pltpu.VMEM((hu, width), BF), dma((8,))],
        room=None, flops=2 * tok * width * hu, name="down",
    )
    got3, near3 = seq_scatter(k13, lax.ppermute(sout3, "seq", CORE))
    if wide:
        msc.add(1, gg1)
        msc.along_z(1)
        msc.along_x(3, msc.part[1])
        msc.add(3, sout3, msc.z[2])
        msc.along_z(3)
        msc.along_x(0, msc.part[3])
    block_output = call(
        blockout_body, [sds((blk, width), BF)], [resid, k03, got3, near3], name="blockout",
    )[0]

    if wide:
        g_f3 = fsc.total(msc.part[3])
        g_m = msc.total(block_output)
        o_back = lax.ppermute(g_m[:, 5 * ch :].astype(BF), ("seq", "batch"), OUT_BACK)
    else:
        def whole(parts):
            lo = jnp.stack([v.astype(F32) for v in parts.kept])
            hi = jnp.stack([v.astype(F32) for v in parts.send])
            return jnp.stack([lo, hi], axis=1).reshape((8,) + parts.send[0].shape)

        f8 = whole(fsc)
        g_f3 = lax.psum_scatter(
            jnp.swapaxes(f8, 0, 1).reshape(3 * hu, width), "batch", scatter_dimension=1,
            tiled=True,
        )
        m8 = whole(msc)
        g_m = lax.psum_scatter(
            m8[:, :, 0 : 5 * ch].reshape(width, 5 * ch), "batch", scatter_dimension=0, tiled=True
        )
        o8 = m8[:, :, 5 * ch :].reshape(2, 2, 2, row8, 2, ch)
        o_full = jnp.transpose(o8, (0, 4, 3, 2, 1, 5)).reshape(2, ch, width)
        spread = jnp.zeros((2, width, width), F32)
        spread = lax.dynamic_update_slice(spread, o_full, (0, start, 0)).reshape(
            2 * width, width
        )
        g_o = lax.psum_scatter(spread, "batch", scatter_dimension=0, tiled=True)
        g_o = lax.psum_scatter(g_o, "seq", scatter_dimension=1, tiled=True)

    far_back = lax.ppermute(
        jnp.concatenate([g_m[:, ch : 2 * ch], g_m[:, 4 * ch : 5 * ch]], axis=1).astype(BF),
        "seq", YSWAP,
    )
    g_f = lax.ppermute(
        g_m[:, 2 * ch : 3 * ch].astype(BF), "seq", [(d, q2) for q2, d in FORGET_PERM]
    )

    if wide:
        g_in, g_og, g_o, g_f = call(
            finish_body,
            [
                sds((row8, 2 * ch), F32), sds((row8, 2 * ch), F32), sds((2 * row8, ch), F32),
                sds((row8, ch), F32),
            ],
            [idx, g_m, far_back, o_back, g_f], [SMEM] + [VMEM] * 4, name="finish",
        )
    else:
        g_f = g_f.astype(F32)
        far_back = far_back.astype(F32)

        def rejoin(nat, farp):
            return jnp.where(
                y == 0,
                jnp.concatenate([nat, farp], axis=1),
                jnp.concatenate([farp, nat], axis=1),
            )

        g_in = rejoin(g_m[:, 0:ch], far_back[:, 0:ch])
        g_og = rejoin(g_m[:, 3 * ch : 4 * ch], far_back[:, ch:])

    ggm2 = jnp.where(
        y == 0,
        ggm.reshape(2, ch),
        jnp.concatenate([ggm[:, ch:], ggm[:, 0:ch]], axis=0),
    )
    spread_gm = lax.dynamic_update_slice(jnp.zeros((2, width), F32), ggm2, (0, start))
    spread_ph = lax.dynamic_update_slice(jnp.zeros((1, width), F32), gph * sign, (0, start))
    nd = 4 * nb
    vec = jnp.concatenate(
        [
            gg1.reshape(nd, -1), gg2.reshape(nd, -1), spread_ph.reshape(nd, -1),
            spread_gm.reshape(nd, -1),
        ],
        axis=1,
    )
    mine = small_sum(after(vec, sout3), msc.got[0], near3) if wide else lax.psum(vec, ("seq", "batch"))
    mine = lax.dynamic_index_in_dim(mine, s * nb + b, 0, False)
    g1n = gain_first.shape[0]
    gg1o = mine[0:g1n]
    gg2o = mine[g1n : 2 * g1n]
    gpho = mine[2 * g1n : 3 * g1n]
    ggmo = mine[3 * g1n :]
    return (
        block_output[None], grad_input[None], gg1o, g_in, g_f, g_og, gpho, ggmo, g_o, gg2o,
        g_f3[0:hu].T, g_f3[hu : 2 * hu].T, g_f3[2 * hu :],
    )


def solution(mesh):
    both = P(("seq", "batch"))
    mat = P("batch", "seq")
    in_specs = (
        P("batch", "seq", None), P("batch", "seq"), P("batch", "seq", None), P(), both, mat,
        mat, mat, both, both, mat, both, mat, mat, P("seq", "batch"),
    )
    out_specs = (
        P("batch", "seq", None), P("batch", "seq", None), both, mat, mat, mat, both, both, mat,
        both, mat, mat, P("seq", "batch"),
    )
    return jax.shard_map(
        per_device, mesh=mesh, in_specs=in_specs, out_specs=out_specs, check_vma=False
    )
```
